32 devices in a mesh: band: 4 (over y, core), tile: 8 (over z, x).
Axes of the slice: x: 2, y: 2, z: 4, core: 2. Of those that a mesh axis runs over, the one named last changes fastest.
Arguments:
- sketch: float32 [8, 4, 48, 128, 128], P(None, 'band', 'tile'), may hold values from -6 to 6
- diag_coef: float32 [4, 48, 128], P('band', 'tile'), may hold values from 1 to 2
- couple: float32 [4, 48, 128], P('band', 'tile'), may hold values from 0.3 to 0.8
- kernel: bfloat16 [8, 512, 4, 48, 128], P(None, None, 'band', 'tile'), may hold values from -0.013671875 to 0.013671875
- noise_prec: float32 [8, 512], replicated, may hold values from 0.5 to 4
Outputs:
- hessian_sketch: float32 [8, 4, 48, 128, 128], P(None, 'band', 'tile')
The draws below stay inside these ranges and needn't reach their ends.
All inputs are finite; a program needn't handle non-finite values.
Results may differ from the reference program's by a relative error of at most 0.0041.
Values may be sent and summed in bfloat16 or wider, within the bound.
No kernel may reach another device: no remote copies, remote signals or barrier semaphores. Data moves between devices by JAX's collectives and lax.ppermute only.
A program may use at most 128 MiB of HBM per device.

```python
import math
import jax
import jax.numpy as jnp

NT = 8
S = 512
K = 128
COLS = 128
BANDS = 4
ROWS = 48
POINTS = 24576


def shard_levels(own_key, shape, cuts, low, top_value):
    def one(position, blocks):
        steps = jax.random.uniform(jax.random.fold_in(jax.random.fold_in(own_key, 6), position), (blocks,), jnp.float32, low / len(cuts), top_value / len(cuts))
        return jnp.repeat(jnp.exp(steps), shape[position] // blocks).reshape((-1,) + (1,) * (len(shape) - position - 1))

    loudness = one(*cuts[0])
    for cut in cuts[1:]:
        loudness = loudness * one(*cut)
    return loudness


def bell_draw(own_key, extent, scale, reach, pieces=(), held_as=jnp.bfloat16):
    entries = scale * jax.random.normal(own_key, extent, jnp.float32)
    if pieces:
        entries = entries * shard_levels(own_key, extent, pieces, -0.22, 0.18)
    return jnp.clip(entries, -reach, reach).astype(held_as)


def setup_inputs(seed: int = 0) -> dict:
    seeds = jax.random.split(jax.random.key(seed), 6)
    sketch = bell_draw(seeds[0], (NT, BANDS, ROWS, COLS, K), 1.0, 6.0, ((1, 4), (2, 8)), jnp.float32)
    diag_coef = jnp.clip(1.0 + 1.0 * jax.random.uniform(seeds[1], (BANDS, ROWS, COLS), jnp.float32) ** shard_levels(seeds[1], (BANDS, ROWS, COLS), ((0, 4), (1, 8)), -0.2, 0.2), 1.0, 2.0)
    couple = jnp.clip(0.3 + 0.5 * jax.random.uniform(seeds[2], (BANDS, ROWS, COLS), jnp.float32) ** shard_levels(seeds[2], (BANDS, ROWS, COLS), ((0, 4), (1, 8)), -0.2, 0.2), 0.3, 0.8)
    kernel = bell_draw(seeds[3], (NT, S, BANDS, ROWS, COLS), (NT * POINTS) ** -0.5, 0.013671875, ((2, 4), (3, 8)))
    noise_prec = jnp.clip(jnp.exp(jax.random.uniform(seeds[4], (NT, S), jnp.float32, math.log(0.5), math.log(4.0))), 0.5, 4.0)
    return {"sketch": sketch, "diag_coef": diag_coef, "couple": couple, "kernel": kernel, "noise_prec": noise_prec}


def sweep(field, diag_coef, couple):
    dcf = diag_coef[None, :, :, :, None]
    cpl = couple[None, :, :, :, None]
    coupled = cpl * field
    padded = jnp.pad(coupled, ((0, 0), (0, 0), (1, 1), (1, 1), (0, 0)))
    beside = padded[:, :, 2:, 1:-1] + padded[:, :, :-2, 1:-1] + padded[:, :, 1:-1, 2:] + padded[:, :, 1:-1, :-2]
    return dcf * field - cpl * beside


def reference(sketch, diag_coef, couple, kernel, noise_prec):
    smoothed = sweep(sweep(sketch, diag_coef, couple), diag_coef, couple).astype(jnp.bfloat16)
    flat = smoothed.reshape(NT, POINTS, K)
    kflat = kernel.reshape(NT, S, POINTS)
    rows = []
    for step in range(NT):
        acc = jnp.zeros((S, K), jnp.float32)
        for lag in range(step + 1):
            acc = acc + jnp.dot(kflat[lag], flat[step - lag], preferred_element_type=jnp.float32)
        rows.append(acc)
    data = jnp.stack(rows)
    weighted = (data * noise_prec[:, :, None]).astype(jnp.bfloat16)
    grads = []
    for step in range(NT):
        acc = jnp.zeros((POINTS, K), jnp.float32)
        for lag in range(NT - step):
            acc = acc + jnp.dot(kflat[lag].T, weighted[step + lag], preferred_element_type=jnp.float32)
        grads.append(acc)
    adjoint = jnp.stack(grads).reshape(sketch.shape)
    return sweep(sweep(adjoint, diag_coef, couple), diag_coef, couple)
```

```python
import jax
import jax.numpy as jnp
from jax import lax
from jax.experimental import pallas as pl
from jax.experimental.pallas import tpu as pltpu
from jax.sharding import PartitionSpec as P

MIB = 1 << 20
HALO = 2


def beside(w):
    cols = w.shape[0]
    at = lax.broadcasted_iota(jnp.int32, w.shape, 0)
    before = jnp.where(at == 0, 0.0, pltpu.roll(w, 1, 0))
    after = jnp.where(at == cols - 1, 0.0, pltpu.roll(w, cols - 1, 0))
    return before + after


def spread_coefs(own, top, bottom, line, wide):
    rows, cols, width = own.shape[1], own.shape[2], wide.shape[3]
    for which in range(2):
        line[...] = jnp.zeros(line.shape, line.dtype)
        line[0:HALO, :] = top[which]
        line[HALO : HALO + rows, :] = own[which]
        line[HALO + rows : 2 * HALO + rows, :] = bottom[which]
        turned = line[...].T
        for row in range(rows + 2 * HALO):
            wide[which, row] = jnp.broadcast_to(turned[:, row : row + 1], (cols, width))


def two_sweeps(load, wide, rows, store):
    total = rows + 2 * HALO
    weighted = [None] * total
    first = [None] * total
    second = [None] * total

    def scaled(row):
        return wide[1, row] * load(row)

    def sweep_one(row):
        around = weighted[row - 1] + weighted[row + 1] + beside(weighted[row])
        return wide[0, row] * load(row) - wide[1, row] * around

    weighted[0] = scaled(0)
    weighted[1] = scaled(1)
    for row in range(1, total - 1):
        weighted[row + 1] = scaled(row + 1)
        first[row] = sweep_one(row)
        second[row] = wide[1, row] * first[row]
        if row >= 3:
            mid = row - 1
            around = second[mid - 1] + second[mid + 1] + beside(second[mid])
            store(mid - HALO, wide[0, mid] * first[mid] - wide[1, mid] * around)


def row_loader(field, top, bottom, step, rows):
    def load(row):
        if row < HALO:
            return top[step, row].astype(jnp.float32)
        if row < HALO + rows:
            return field[step, row - HALO]
        return bottom[step, row - HALO - rows].astype(jnp.float32)

    return load


def forward_kernel(field, top, bottom, own, ctop, cbottom, kern, data, line, wide, pairs):
    steps, rows, cols, width = field.shape
    points = rows * cols
    spread_coefs(own, ctop, cbottom, line, wide)
    pairs[0, :, 0:width] = jnp.zeros((points, width), pairs.dtype)

    @pl.loop(0, steps)
    def _(step):
        def store(row, value):
            rounded = value.astype(pairs.dtype)
            pairs[step, row * cols : (row + 1) * cols, width : 2 * width] = rounded
            pairs[step + 1, row * cols : (row + 1) * cols, 0:width] = rounded

        two_sweeps(row_loader(field, top, bottom, step, rows), wide, rows, store)

    for step in range(0, steps, 2):
        acc = None
        for lag in range(step + 2):
            left = jnp.concatenate([kern[lag, row] for row in range(rows)], axis=1)
            term = jnp.dot(left, pairs[step + 1 - lag], preferred_element_type=jnp.float32)
            acc = term if acc is None else acc + term
        data[step] = acc[:, 0:width].astype(data.dtype)
        data[step + 1] = acc[:, width : 2 * width].astype(data.dtype)


def forward(field, top, bottom, coefs, ctop, cbottom, kern):
    steps, rows, cols, width = field.shape
    sensors = kern.shape[2]
    points = rows * cols
    vmem = pl.BlockSpec(memory_space=pltpu.VMEM)
    return pl.pallas_call(
        forward_kernel,
        out_shape=jax.ShapeDtypeStruct((steps, sensors, width), jnp.bfloat16),
        in_specs=[vmem] * 7,
        out_specs=vmem,
        scratch_shapes=[
            pltpu.VMEM((cols, cols), jnp.float32),
            pltpu.VMEM((2, rows + 2 * HALO, cols, width), jnp.float32),
            pltpu.VMEM((steps + 1, points, 2 * width), jnp.bfloat16),
        ],
        compiler_params=pltpu.CompilerParams(vmem_limit_bytes=30 * MIB),
        cost_estimate=pl.CostEstimate(
            flops=steps * (steps + 1) * sensors * points * width, bytes_accessed=12 * MIB, transcendentals=0
        ),
        name="forward",
    )(field, top, bottom, coefs, ctop, cbottom, kern)


def adjoint_kernel(turned, weighted, field, head, tail, pairs):
    steps, rows, cols, width = field.shape
    sensors = weighted.shape[1]
    for step in range(steps):
        pairs[step, :, 0:width] = weighted[step]
        if step:
            pairs[step - 1, :, width : 2 * width] = weighted[step]
    pairs[steps - 1, :, width : 2 * width] = jnp.zeros((sensors, width), pairs.dtype)
    for step in range(0, steps, 2):
        acc = None
        for lag in range(steps - step):
            left = turned[lag].reshape(rows * cols, sensors)
            term = jnp.dot(left, pairs[step + lag], preferred_element_type=jnp.float32)
            acc = term if acc is None else acc + term
        for half in range(2):
            part = acc[:, half * width : (half + 1) * width].reshape(rows, cols, width)
            field[step + half] = part
            head[step + half] = part[0:HALO].astype(head.dtype)
            tail[step + half] = part[rows - HALO : rows].astype(tail.dtype)


def adjoint(turned, weighted):
    steps, rows, cols, sensors = turned.shape
    width = weighted.shape[2]
    vmem = pl.BlockSpec(memory_space=pltpu.VMEM)
    edge = jax.ShapeDtypeStruct((steps, HALO, cols, width), jnp.bfloat16)
    return pl.pallas_call(
        adjoint_kernel,
        out_shape=(jax.ShapeDtypeStruct((steps, rows, cols, width), jnp.float32), edge, edge),
        in_specs=[vmem] * 2,
        out_specs=(vmem, vmem, vmem),
        scratch_shapes=[pltpu.VMEM((steps, sensors, 2 * width), jnp.bfloat16)],
        compiler_params=pltpu.CompilerParams(vmem_limit_bytes=30 * MIB),
        cost_estimate=pl.CostEstimate(
            flops=steps * (steps + 1) * sensors * rows * cols * width, bytes_accessed=11 * MIB, transcendentals=0
        ),
        name="adjoint",
    )(turned, weighted)


def last_kernel(field, top, bottom, own, ctop, cbottom, out, line, wide):
    rows = field.shape[1]

    @pl.when(pl.program_id(0) == 0)
    def _():
        spread_coefs(own, ctop, cbottom, line, wide)

    def store(row, value):
        out[0, row] = value

    two_sweeps(row_loader(field, top, bottom, 0, rows), wide, rows, store)


def last_prior(field, top, bottom, coefs, ctop, cbottom):
    steps, rows, cols, width = field.shape
    vmem = pl.BlockSpec(memory_space=pltpu.VMEM)

    def block(count):
        return pl.BlockSpec((1, count, cols, width), lambda step: (step, 0, 0, 0))

    return pl.pallas_call(
        last_kernel,
        grid=(steps,),
        out_shape=jax.ShapeDtypeStruct(field.shape, jnp.float32),
        in_specs=[block(rows), block(HALO), block(HALO), vmem, vmem, vmem],
        out_specs=block(rows),
        scratch_shapes=[
            pltpu.VMEM((cols, cols), jnp.float32),
            pltpu.VMEM((2, rows + 2 * HALO, cols, width), jnp.float32),
        ],
        compiler_params=pltpu.CompilerParams(vmem_limit_bytes=16 * MIB),
        cost_estimate=pl.CostEstimate(flops=steps * points_ops(rows, cols, width), bytes_accessed=7 * MIB, transcendentals=0),
        name="last_prior",
    )(field, top, bottom, coefs, ctop, cbottom)


def points_ops(rows, cols, width):
    return 20 * rows * cols * width


def from_neighbours(head, tail):
    count = lax.axis_size("tile")
    down = [(i, i + 1) for i in range(count - 1)]
    up = [(i + 1, i) for i in range(count - 1)]
    return lax.ppermute(tail, "tile", down), lax.ppermute(head, "tile", up)


def body(sketch, diag_coef, couple, kernel, noise_prec):
    steps, _, rows, cols, width = sketch.shape
    sensors = kernel.shape[1]
    every = ("band", "tile")
    devices = lax.axis_size(every)
    field = sketch.reshape(steps, rows, cols, width)
    top, bottom = from_neighbours(
        field[:, :HALO].astype(jnp.bfloat16), field[:, rows - HALO :].astype(jnp.bfloat16)
    )
    coefs = jnp.concatenate([diag_coef, couple])
    ctop, cbottom = from_neighbours(coefs[:, :HALO], coefs[:, rows - HALO :])
    kern = kernel.reshape(steps, sensors, rows, cols)
    turned = jnp.transpose(kern, (0, 2, 3, 1))
    data = forward(field, top, bottom, coefs, ctop, cbottom, jnp.transpose(kern, (0, 2, 1, 3)))
    share = steps * sensors // devices
    pieces = lax.all_to_all(data.reshape(devices, share, width), every, 0, 0, tiled=True)
    mine = jnp.sum(pieces.astype(jnp.float32), axis=0)
    prec = lax.dynamic_slice(noise_prec.reshape(-1), (lax.axis_index(every) * share,), (share,))
    weighted = (mine * prec[:, None]).astype(jnp.bfloat16)
    weighted = lax.all_gather(weighted, every, axis=0, tiled=True).reshape(steps, sensors, width)
    back, head, tail = adjoint(turned, weighted)
    top, bottom = from_neighbours(head, tail)
    out = last_prior(back, top, bottom, coefs, ctop, cbottom)
    return out.reshape(sketch.shape)


def solution(mesh):
    placed = (
        P(None, "band", "tile", None, None),
        P("band", "tile", None),
        P("band", "tile", None),
        P(None, None, "band", "tile", None),
        P(),
    )
    return jax.shard_map(
        body,
        mesh=mesh,
        in_specs=placed,
        out_specs=P(None, "band", "tile", None, None),
        check_vma=False,
    )
```

```python
import jax
import jax.numpy as jnp
from jax import lax
from jax.experimental import pallas as pl
from jax.experimental.pallas import tpu as pltpu
from jax.sharding import Mesh
from jax.sharding import PartitionSpec as P

MIB = 1 << 20
HALO = 2


def beside(w):
    cols = w.shape[0]
    at = lax.broadcasted_iota(jnp.int32, w.shape, 0)
    before = jnp.where(at == 0, 0.0, pltpu.roll(w, 1, 0))
    after = jnp.where(at == cols - 1, 0.0, pltpu.roll(w, cols - 1, 0))
    return before + after


def spread_coefs(own, top, bottom, line, wide):
    rows, cols, width = own.shape[1], own.shape[2], wide.shape[3]
    for which in range(2):
        line[...] = jnp.zeros(line.shape, line.dtype)
        line[0:HALO, :] = top[which]
        line[HALO : HALO + rows, :] = own[which]
        line[HALO + rows : 2 * HALO + rows, :] = bottom[which]
        turned = line[...].T
        for row in range(rows + 2 * HALO):
            wide[which, row] = jnp.broadcast_to(turned[:, row : row + 1], (cols, width))


def two_sweeps(load, wide, rows, store):
    total = rows + 2 * HALO
    weighted = [None] * total
    first = [None] * total
    second = [None] * total

    def scaled(row):
        return wide[1, row] * load(row)

    def sweep_one(row):
        around = weighted[row - 1] + weighted[row + 1] + beside(weighted[row])
        return wide[0, row] * load(row) - wide[1, row] * around

    weighted[0] = scaled(0)
    weighted[1] = scaled(1)
    for row in range(1, total - 1):
        weighted[row + 1] = scaled(row + 1)
        first[row] = sweep_one(row)
        second[row] = wide[1, row] * first[row]
        if row >= 3:
            mid = row - 1
            around = second[mid - 1] + second[mid + 1] + beside(second[mid])
            store(mid - HALO, wide[0, mid] * first[mid] - wide[1, mid] * around)


def row_loader(field, top, bottom, step, rows):
    def load(row):
        if row < HALO:
            return top[step, row].astype(jnp.float32)
        if row < HALO + rows:
            return field[step, row - HALO]
        return bottom[step, row - HALO - rows].astype(jnp.float32)

    return load


def forward_kernel(twin, field, top, bottom, own, ctop, cbottom, kern, mine, other, line, wide, pairs):
    steps, rows, cols, width = field.shape
    points = rows * cols
    spread_coefs(own, ctop, cbottom, line, wide)
    pairs[0, :, 0:width] = jnp.zeros((points, width), pairs.dtype)

    @pl.loop(0, steps)
    def _(step):
        def store(row, value):
            rounded = value.astype(pairs.dtype)
            pairs[step, row * cols : (row + 1) * cols, width : 2 * width] = rounded
            pairs[step + 1, row * cols : (row + 1) * cols, 0:width] = rounded

        two_sweeps(row_loader(field, top, bottom, step, rows), wide, rows, store)

    for step in range(0, steps, 2):
        acc = None
        for lag in range(step + 2):
            left = jnp.concatenate([kern[lag, row] for row in range(rows)], axis=1)
            term = jnp.dot(left, pairs[step + 1 - lag], preferred_element_type=jnp.float32)
            acc = term if acc is None else acc + term
        half, at = divmod(step, steps // 2)

        @pl.when(twin[0] == half)
        def _():
            mine[at] = acc[:, 0:width]
            mine[at + 1] = acc[:, width : 2 * width]

        @pl.when(twin[0] != half)
        def _():
            other[at] = acc[:, 0:width].astype(other.dtype)
            other[at + 1] = acc[:, width : 2 * width].astype(other.dtype)


def forward(twin, field, top, bottom, coefs, ctop, cbottom, kern):
    steps, rows, cols, width = field.shape
    sensors = kern.shape[2]
    points = rows * cols
    vmem = pl.BlockSpec(memory_space=pltpu.VMEM)
    return pl.pallas_call(
        forward_kernel,
        out_shape=(
            jax.ShapeDtypeStruct((steps // 2, sensors, width), jnp.float32),
            jax.ShapeDtypeStruct((steps // 2, sensors, width), jnp.bfloat16),
        ),
        in_specs=[pl.BlockSpec(memory_space=pltpu.SMEM)] + [vmem] * 7,
        out_specs=(vmem, vmem),
        scratch_shapes=[
            pltpu.VMEM((cols, cols), jnp.float32),
            pltpu.VMEM((2, rows + 2 * HALO, cols, width), jnp.float32),
            pltpu.VMEM((steps + 1, points, 2 * width), jnp.bfloat16),
        ],
        compiler_params=pltpu.CompilerParams(vmem_limit_bytes=30 * MIB),
        cost_estimate=pl.CostEstimate(
            flops=steps * (steps + 1) * sensors * points * width, bytes_accessed=12 * MIB, transcendentals=0
        ),
        name="forward",
    )(twin, field, top, bottom, coefs, ctop, cbottom, kern)


def adjoint_kernel(twin, mine, other, turned, field, head, tail, pairs, held, arrived):
    steps, rows, cols, width = field.shape
    sensors = mine.shape[1]
    copies = [pltpu.make_async_copy(turned.at[lag], held.at[lag], arrived.at[lag]) for lag in range(steps)]
    for copy in copies:
        copy.start()
    pairs[steps, :, width : 2 * width] = jnp.zeros((sensors, width), pairs.dtype)
    for source, half in ((mine, twin[0]), (other, 1 - twin[0])):
        for at in range(steps // 2):
            step = half * (steps // 2) + at
            pairs[step + 1, :, 0:width] = source[at]
            pairs[step, :, width : 2 * width] = source[at]
    ready = 0
    for step in range(steps - 2, -1, -2):
        acc = None
        for lag in range(steps - step):
            while ready <= lag:
                copies[ready].wait()
                ready += 1
            left = held[lag].reshape(rows * cols, sensors)
            term = jnp.dot(left, pairs[step + lag + 1], preferred_element_type=jnp.float32)
            acc = term if acc is None else acc + term
        for half in range(2):
            part = acc[:, half * width : (half + 1) * width].reshape(rows, cols, width)
            field[step + half] = part
            head[step + half] = part[0:HALO].astype(head.dtype)
            tail[step + half] = part[rows - HALO : rows].astype(tail.dtype)


def adjoint(twin, mine, other, turned):
    steps, rows, cols, sensors = turned.shape
    width = mine.shape[2]
    vmem = pl.BlockSpec(memory_space=pltpu.VMEM)
    edge = jax.ShapeDtypeStruct((steps, HALO, cols, width), jnp.bfloat16)
    return pl.pallas_call(
        adjoint_kernel,
        out_shape=(jax.ShapeDtypeStruct((steps, rows, cols, width), jnp.float32), edge, edge),
        in_specs=[pl.BlockSpec(memory_space=pltpu.SMEM), vmem, vmem, pl.BlockSpec(memory_space=pl.ANY)],
        out_specs=(vmem, vmem, vmem),
        scratch_shapes=[
            pltpu.VMEM((steps + 1, sensors, 2 * width), jnp.bfloat16),
            pltpu.VMEM(turned.shape, turned.dtype),
            pltpu.SemaphoreType.DMA((steps,)),
        ],
        compiler_params=pltpu.CompilerParams(vmem_limit_bytes=30 * MIB),
        cost_estimate=pl.CostEstimate(
            flops=steps * (steps + 1) * sensors * rows * cols * width, bytes_accessed=11 * MIB, transcendentals=0
        ),
        name="adjoint",
    )(twin, mine, other, turned)


def last_kernel(field, top, bottom, own, ctop, cbottom, out, line, wide):
    rows = field.shape[1]

    @pl.when(pl.program_id(0) == 0)
    def _():
        spread_coefs(own, ctop, cbottom, line, wide)

    def store(row, value):
        out[0, row] = value

    two_sweeps(row_loader(field, top, bottom, 0, rows), wide, rows, store)


def last_prior(field, top, bottom, coefs, ctop, cbottom):
    steps, rows, cols, width = field.shape
    vmem = pl.BlockSpec(memory_space=pltpu.VMEM)

    def block(count):
        return pl.BlockSpec((1, count, cols, width), lambda step: (step, 0, 0, 0))

    return pl.pallas_call(
        last_kernel,
        grid=(steps,),
        out_shape=jax.ShapeDtypeStruct(field.shape, jnp.float32),
        in_specs=[block(rows), block(HALO), block(HALO), vmem, vmem, vmem],
        out_specs=block(rows),
        scratch_shapes=[
            pltpu.VMEM((cols, cols), jnp.float32),
            pltpu.VMEM((2, rows + 2 * HALO, cols, width), jnp.float32),
        ],
        compiler_params=pltpu.CompilerParams(vmem_limit_bytes=16 * MIB),
        cost_estimate=pl.CostEstimate(flops=steps * points_ops(rows, cols, width), bytes_accessed=7 * MIB, transcendentals=0),
        name="last_prior",
    )(field, top, bottom, coefs, ctop, cbottom)


def points_ops(rows, cols, width):
    return 20 * rows * cols * width


def from_neighbours(head, tail):
    count = lax.axis_size("tile")
    down = [(i, i + 1) for i in range(count - 1)]
    up = [(i + 1, i) for i in range(count - 1)]
    return lax.ppermute(tail, "tile", down), lax.ppermute(head, "tile", up)


def swap_twins(value):
    return lax.ppermute(value, "twin", [(0, 1), (1, 0)])


def body(sketch, diag_coef, couple, kernel, noise_prec):
    steps, _, rows, cols, width = sketch.shape
    sensors = kernel.shape[1]
    others = ("pair", "tile")
    groups = lax.axis_size(others)
    twin = lax.axis_index("twin")
    field = sketch.reshape(steps, rows, cols, width)
    top, bottom = from_neighbours(
        field[:, :HALO].astype(jnp.bfloat16), field[:, rows - HALO :].astype(jnp.bfloat16)
    )
    coefs = jnp.concatenate([diag_coef, couple])
    ctop, cbottom = from_neighbours(coefs[:, :HALO], coefs[:, rows - HALO :])
    kern = kernel.reshape(steps, sensors, rows, cols)
    turned = jnp.transpose(kern, (0, 2, 3, 1))
    which = twin.reshape(1)
    mine, other = forward(which, field, top, bottom, coefs, ctop, cbottom, jnp.transpose(kern, (0, 2, 1, 3)))
    both = (mine + swap_twins(other).astype(jnp.float32)).astype(jnp.bfloat16)
    share = steps * sensors // (2 * groups)
    pieces = lax.all_to_all(both.reshape(groups, share, width), others, 0, 0, tiled=True)
    total = jnp.sum(pieces.astype(jnp.float32), axis=0)
    start = (twin * groups + lax.axis_index(others)) * share
    prec = lax.dynamic_slice(noise_prec.reshape(-1), (start,), (share,))
    weighted = (total * prec[:, None]).astype(jnp.bfloat16)
    weighted = lax.all_gather(weighted, "tile", axis=0, tiled=True)
    weighted = lax.all_gather(weighted, "pair", axis=0, tiled=True).reshape(steps // 2, sensors, width)
    back, head, tail = adjoint(which, weighted, swap_twins(weighted), turned)
    top, bottom = from_neighbours(head, tail)
    out = last_prior(back, top, bottom, coefs, ctop, cbottom)
    return out.reshape(sketch.shape)


def solution(mesh):
    bands, tiles = mesh.shape["band"], mesh.shape["tile"]
    fine = Mesh(mesh.devices.reshape(bands // 2, 2, tiles), ("pair", "twin", "tile"))
    band = ("pair", "twin")
    placed = (
        P(None, band, "tile", None, None),
        P(band, "tile", None),
        P(band, "tile", None),
        P(None, None, band, "tile", None),
        P(),
    )
    return jax.shard_map(
        body,
        mesh=fine,
        in_specs=placed,
        out_specs=P(None, band, "tile", None, None),
        check_vma=False,
    )
```

```python
import jax
import jax.numpy as jnp
from jax import lax
from jax.experimental import pallas as pl
from jax.experimental.pallas import tpu as pltpu
from jax.sharding import Mesh
from jax.sharding import PartitionSpec as P

MIB = 1 << 20
HALO = 2


def beside(w):
    cols = w.shape[0]
    at = lax.broadcasted_iota(jnp.int32, w.shape, 0)
    before = jnp.where(at == 0, 0.0, pltpu.roll(w, 1, 0))
    after = jnp.where(at == cols - 1, 0.0, pltpu.roll(w, cols - 1, 0))
    return before + after


def spread_coefs(own, top, bottom, line, wide):
    rows, cols, width = own.shape[1], own.shape[2], wide.shape[3]
    for which in range(2):
        line[...] = jnp.zeros(line.shape, line.dtype)
        line[0:HALO, :] = top[which]
        line[HALO : HALO + rows, :] = own[which]
        line[HALO + rows : 2 * HALO + rows, :] = bottom[which]
        turned = line[...].T
        for row in range(rows + 2 * HALO):
            wide[which, row] = jnp.broadcast_to(turned[:, row : row + 1], (cols, width))


def two_sweeps(load, wide, rows, store):
    total = rows + 2 * HALO
    weighted = [None] * total
    first = [None] * total
    second = [None] * total

    def scaled(row):
        return wide[1, row] * load(row)

    def sweep_one(row):
        around = weighted[row - 1] + weighted[row + 1] + beside(weighted[row])
        return wide[0, row] * load(row) - wide[1, row] * around

    weighted[0] = scaled(0)
    weighted[1] = scaled(1)
    for row in range(1, total - 1):
        weighted[row + 1] = scaled(row + 1)
        first[row] = sweep_one(row)
        second[row] = wide[1, row] * first[row]
        if row >= 3:
            mid = row - 1
            around = second[mid - 1] + second[mid + 1] + beside(second[mid])
            store(mid - HALO, wide[0, mid] * first[mid] - wide[1, mid] * around)


def row_loader(field, top, bottom, step, rows):
    def load(row):
        if row < HALO:
            return top[step, row].astype(jnp.float32)
        if row < HALO + rows:
            return field[step, row - HALO]
        return bottom[step, row - HALO - rows].astype(jnp.float32)

    return load


def forward_kernel(twin, field, top, bottom, own, ctop, cbottom, kern, mine, other, line, wide, pairs, data):
    steps, rows, cols, width = field.shape
    points = rows * cols
    spread_coefs(own, ctop, cbottom, line, wide)
    pairs[0, :, 0:width] = jnp.zeros((points, width), pairs.dtype)

    @pl.loop(0, steps)
    def _(step):
        def store(row, value):
            rounded = value.astype(pairs.dtype)
            pairs[step, row * cols : (row + 1) * cols, width : 2 * width] = rounded
            pairs[step + 1, row * cols : (row + 1) * cols, 0:width] = rounded

        two_sweeps(row_loader(field, top, bottom, step, rows), wide, rows, store)

    for step in range(0, steps, 2):
        acc = None
        for lag in range(step + 2):
            left = jnp.concatenate([kern[lag, row] for row in range(rows)], axis=1)
            term = jnp.dot(left, pairs[step + 1 - lag], preferred_element_type=jnp.float32)
            acc = term if acc is None else acc + term
        data[step] = acc[:, 0:width]
        data[step + 1] = acc[:, width : 2 * width]
    kept = steps // 2
    mine[...] = data[pl.ds(twin[0] * kept, kept)]
    other[...] = data[pl.ds((1 - twin[0]) * kept, kept)].astype(other.dtype)


def forward(twin, field, top, bottom, coefs, ctop, cbottom, kern):
    steps, rows, cols, width = field.shape
    sensors = kern.shape[2]
    points = rows * cols
    vmem = pl.BlockSpec(memory_space=pltpu.VMEM)
    return pl.pallas_call(
        forward_kernel,
        out_shape=(
            jax.ShapeDtypeStruct((steps // 2, sensors, width), jnp.float32),
            jax.ShapeDtypeStruct((steps // 2, sensors, width), jnp.bfloat16),
        ),
        in_specs=[pl.BlockSpec(memory_space=pltpu.SMEM)] + [vmem] * 7,
        out_specs=(vmem, vmem),
        scratch_shapes=[
            pltpu.VMEM((cols, cols), jnp.float32),
            pltpu.VMEM((2, rows + 2 * HALO, cols, width), jnp.float32),
            pltpu.VMEM((steps + 1, points, 2 * width), jnp.bfloat16),
            pltpu.VMEM((steps, sensors, width), jnp.float32),
        ],
        compiler_params=pltpu.CompilerParams(vmem_limit_bytes=30 * MIB),
        cost_estimate=pl.CostEstimate(
            flops=steps * (steps + 1) * sensors * points * width, bytes_accessed=12 * MIB, transcendentals=0
        ),
        name="forward",
    )(twin, field, top, bottom, coefs, ctop, cbottom, kern)


def adjoint_kernel(twin, mine, other, turned, field, head, tail, pairs):
    steps, rows, cols, width = field.shape
    sensors = mine.shape[1]
    pairs[steps, :, width : 2 * width] = jnp.zeros((sensors, width), pairs.dtype)
    for source, half in ((mine, twin[0]), (other, 1 - twin[0])):
        for at in range(steps // 2):
            step = half * (steps // 2) + at
            pairs[step + 1, :, 0:width] = source[at]
            pairs[step, :, width : 2 * width] = source[at]
    for step in range(steps - 2, -1, -2):
        acc = None
        for lag in range(steps - step):
            left = turned[lag].reshape(rows * cols, sensors)
            term = jnp.dot(left, pairs[step + lag + 1], preferred_element_type=jnp.float32)
            acc = term if acc is None else acc + term
        for half in range(2):
            part = acc[:, half * width : (half + 1) * width].reshape(rows, cols, width)
            field[step + half] = part
            head[step + half] = part[0:HALO].astype(head.dtype)
            tail[step + half] = part[rows - HALO : rows].astype(tail.dtype)


def adjoint(twin, mine, other, turned):
    steps, rows, cols, sensors = turned.shape
    width = mine.shape[2]
    vmem = pl.BlockSpec(memory_space=pltpu.VMEM)
    edge = jax.ShapeDtypeStruct((steps, HALO, cols, width), jnp.bfloat16)
    return pl.pallas_call(
        adjoint_kernel,
        out_shape=(jax.ShapeDtypeStruct((steps, rows, cols, width), jnp.float32), edge, edge),
        in_specs=[pl.BlockSpec(memory_space=pltpu.SMEM), vmem, vmem, vmem],
        out_specs=(vmem, vmem, vmem),
        scratch_shapes=[
            pltpu.VMEM((steps + 1, sensors, 2 * width), jnp.bfloat16),
        ],
        compiler_params=pltpu.CompilerParams(vmem_limit_bytes=30 * MIB),
        cost_estimate=pl.CostEstimate(
            flops=steps * (steps + 1) * sensors * rows * cols * width, bytes_accessed=11 * MIB, transcendentals=0
        ),
        name="adjoint",
    )(twin, mine, other, turned)


def last_kernel(field, top, bottom, own, ctop, cbottom, out, line, wide):
    rows = field.shape[1]

    @pl.when(pl.program_id(0) == 0)
    def _():
        spread_coefs(own, ctop, cbottom, line, wide)

    def store(row, value):
        out[0, row] = value

    two_sweeps(row_loader(field, top, bottom, 0, rows), wide, rows, store)


def last_prior(field, top, bottom, coefs, ctop, cbottom):
    steps, rows, cols, width = field.shape
    vmem = pl.BlockSpec(memory_space=pltpu.VMEM)

    def block(count):
        return pl.BlockSpec((1, count, cols, width), lambda step: (step, 0, 0, 0))

    return pl.pallas_call(
        last_kernel,
        grid=(steps,),
        out_shape=jax.ShapeDtypeStruct(field.shape, jnp.float32),
        in_specs=[block(rows), block(HALO), block(HALO), vmem, vmem, vmem],
        out_specs=block(rows),
        scratch_shapes=[
            pltpu.VMEM((cols, cols), jnp.float32),
            pltpu.VMEM((2, rows + 2 * HALO, cols, width), jnp.float32),
        ],
        compiler_params=pltpu.CompilerParams(vmem_limit_bytes=16 * MIB),
        cost_estimate=pl.CostEstimate(flops=steps * points_ops(rows, cols, width), bytes_accessed=7 * MIB, transcendentals=0),
        name="last_prior",
    )(field, top, bottom, coefs, ctop, cbottom)


def points_ops(rows, cols, width):
    return 20 * rows * cols * width


def from_neighbours(head, tail):
    count = lax.axis_size("tile")
    down = [(i, i + 1) for i in range(count - 1)]
    up = [(i + 1, i) for i in range(count - 1)]
    return lax.ppermute(tail, "tile", down), lax.ppermute(head, "tile", up)


def swap_twins(value):
    return lax.ppermute(value, "twin", [(0, 1), (1, 0)])


def body(sketch, diag_coef, couple, kernel, noise_prec):
    steps, _, rows, cols, width = sketch.shape
    sensors = kernel.shape[1]
    others = ("pair", "tile")
    groups = lax.axis_size(others)
    twin = lax.axis_index("twin")
    field = sketch.reshape(steps, rows, cols, width)
    top, bottom = from_neighbours(
        field[:, :HALO].astype(jnp.bfloat16), field[:, rows - HALO :].astype(jnp.bfloat16)
    )
    coefs = jnp.concatenate([diag_coef, couple])
    ctop, cbottom = from_neighbours(coefs[:, :HALO], coefs[:, rows - HALO :])
    kern = kernel.reshape(steps, sensors, rows, cols)
    turned = jnp.transpose(kern, (0, 2, 3, 1))
    top, bottom, turned = lax.optimization_barrier((top, bottom, turned))
    which = twin.reshape(1)
    mine, other = forward(which, field, top, bottom, coefs, ctop, cbottom, jnp.transpose(kern, (0, 2, 1, 3)))
    both = (mine + swap_twins(other).astype(jnp.float32)).astype(jnp.bfloat16)
    share = steps * sensors // (2 * groups)
    pieces = lax.all_to_all(both.reshape(groups, share, width), others, 0, 0, tiled=True)
    total = jnp.sum(pieces.astype(jnp.float32), axis=0)
    start = (twin * groups + lax.axis_index(others)) * share
    prec = lax.dynamic_slice(noise_prec.reshape(-1), (start,), (share,))
    weighted = (total * prec[:, None]).astype(jnp.bfloat16)
    copies = jnp.broadcast_to(weighted[None], (groups, share, width))
    weighted = lax.all_to_all(copies, others, 0, 0, tiled=True).reshape(steps // 2, sensors, width)
    back, head, tail = adjoint(which, weighted, swap_twins(weighted), turned)
    top, bottom = from_neighbours(head, tail)
    out = last_prior(back, top, bottom, coefs, ctop, cbottom)
    return out.reshape(sketch.shape)


def solution(mesh):
    bands, tiles = mesh.shape["band"], mesh.shape["tile"]
    fine = Mesh(mesh.devices.reshape(bands // 2, 2, tiles), ("pair", "twin", "tile"))
    band = ("pair", "twin")
    placed = (
        P(None, band, "tile", None, None),
        P(band, "tile", None),
        P(band, "tile", None),
        P(None, None, band, "tile", None),
        P(),
    )
    return jax.shard_map(
        body,
        mesh=fine,
        in_specs=placed,
        out_specs=P(None, band, "tile", None, None),
        check_vma=False,
    )
```

```python
import functools

import jax
import jax.numpy as jnp
from jax import lax
from jax.experimental import pallas as pl
from jax.experimental.pallas import tpu as pltpu
from jax.sharding import Mesh
from jax.sharding import PartitionSpec as P

MIB = 1 << 20
HALO = 2
NOTE = 16
VMEM = pl.BlockSpec(memory_space=pltpu.VMEM)
SMEM = pl.BlockSpec(memory_space=pltpu.SMEM)
HBM = pl.BlockSpec(memory_space=pltpu.HBM)
ANY = pl.BlockSpec(memory_space=pl.ANY)


def call(kernel, name, out_shape, in_specs, out_specs, scratch, limit, flops, moved, grid=()):
    return pl.pallas_call(
        kernel,
        grid=grid,
        out_shape=out_shape,
        in_specs=in_specs,
        out_specs=out_specs,
        scratch_shapes=scratch,
        compiler_params=pltpu.CompilerParams(vmem_limit_bytes=limit * MIB),
        cost_estimate=pl.CostEstimate(flops=flops, bytes_accessed=moved, transcendentals=0),
        name=name,
    )


def first_lanes(value):
    lane = lax.broadcasted_iota(jnp.int32, value.shape, value.ndim - 1)
    return lane < value.shape[-1] // 2


def swap_lanes(value):
    return pltpu.roll(value, value.shape[-1] // 2, value.ndim - 1)


def side_by_side(early, late, chunk):
    if chunk == 0:
        return jnp.where(first_lanes(early), early, swap_lanes(late))
    return jnp.where(first_lanes(early), swap_lanes(early), late)


def beside(w):
    cols = w.shape[0]
    at = lax.broadcasted_iota(jnp.int32, w.shape, 0)
    before = jnp.where(at == 0, 0.0, pltpu.roll(w, 1, 0))
    after = jnp.where(at == cols - 1, 0.0, pltpu.roll(w, cols - 1, 0))
    return before + after


def message_row(which, row):
    return (which * HALO + row) * 2


def spread_coefs(own, ctop, cbottom, line, wide):
    rows, cols, width = own.shape[1], own.shape[2], wide.shape[3]
    body_rows = ctop.shape[0] - NOTE
    above = ctop[body_rows : body_rows + NOTE, :].astype(jnp.float32)
    below = cbottom[body_rows : body_rows + NOTE, :].astype(jnp.float32)
    for which in range(2):
        line[...] = jnp.zeros(line.shape, line.dtype)
        for row in range(HALO):
            at = message_row(which, row)
            line[row : row + 1, :] = (above[at : at + 1] + above[at + 1 : at + 2])[:, 0:cols]
            far = HALO + rows + row
            line[far : far + 1, :] = (below[at : at + 1] + below[at + 1 : at + 2])[:, 0:cols]
        line[HALO : HALO + rows, :] = own[which]
        turned = line[...].T
        for row in range(rows + 2 * HALO):
            wide[which, row] = jnp.broadcast_to(turned[:, row : row + 1], (cols, width))


def two_sweeps(load, wide, rows, store):
    total = rows + 2 * HALO
    value = [None] * total
    scaled = [None] * total
    first = [None] * total
    second = [None] * total

    def take(row):
        value[row] = load(row)
        scaled[row] = wide[1, row] * value[row]

    take(0)
    take(1)
    for row in range(1, total - 1):
        take(row + 1)
        around = scaled[row - 1] + scaled[row + 1] + beside(scaled[row])
        first[row] = wide[0, row] * value[row] - wide[1, row] * around
        second[row] = wide[1, row] * first[row]
        if row >= 3:
            mid = row - 1
            around = second[mid - 1] + second[mid + 1] + beside(second[mid])
            store(mid - HALO, wide[0, mid] * first[mid] - wide[1, mid] * around)


def message_loader(own_row, top, bottom, step, rows, cols):
    def edge(message, row):
        at = pl.multiple_of((step * HALO + row) * cols, cols)
        return message[pl.ds(at, cols), :].astype(jnp.float32)

    def load(row):
        if row < HALO:
            return edge(top, row)
        if row < HALO + rows:
            return own_row(row - HALO)
        return edge(bottom, row - HALO - rows)

    return load


def pack_kernel(field, coefs, head_a, tail_a, head_b, tail_b, note, edges, arrived):
    steps, rows, cols, width = field.shape
    half = steps // 2
    copies = []
    for side, first in enumerate((0, rows - HALO)):
        copies.append(pltpu.make_async_copy(field.at[:, pl.ds(first, HALO)], edges.at[side], arrived.at[side]))
        copies[side].start()
    for side, first, out_a, out_b in ((0, 0, head_a, head_b), (1, rows - HALO, tail_a, tail_b)):
        copies[side].wait()
        source = edges.at[side]
        for step in range(half):
            for row in range(HALO):
                at = (step * HALO + row) * cols
                early, late = source[step, row], source[step + half, row]
                out_a[at : at + cols, :] = side_by_side(early, late, 0).astype(out_a.dtype)
                out_b[at : at + cols, :] = side_by_side(early, late, 1).astype(out_b.dtype)
        note[...] = jnp.zeros(note.shape, note.dtype)
        for which in range(2):
            for row in range(HALO):
                at = message_row(which, row)
                whole = coefs[which, first + row : first + row + 1, :]
                high = whole.astype(jnp.bfloat16).astype(jnp.float32)
                note[at : at + 1, 0:cols] = high
                note[at + 1 : at + 2, 0:cols] = whole - high
        out_a[half * HALO * cols :, :] = note[...].astype(out_a.dtype)


def pack(field, coefs):
    steps, rows, cols, width = field.shape
    size = steps // 2 * HALO * cols
    with_note = jax.ShapeDtypeStruct((size + NOTE, width), jnp.bfloat16)
    plain = jax.ShapeDtypeStruct((size, width), jnp.bfloat16)
    return call(
        pack_kernel,
        "pack",
        (with_note, with_note, plain, plain),
        [HBM, VMEM],
        (VMEM,) * 4,
        [
            pltpu.VMEM((NOTE, width), jnp.float32),
            pltpu.VMEM((2, steps, HALO, cols, width), jnp.float32),
            pltpu.SemaphoreType.DMA((2,)),
        ],
        16,
        4 * size * width,
        12 * size * width,
    )(field, coefs)


def forward_kernel(chunk, twin, field, top, bottom, own, ctop, cbottom, kern, _, mine, other, line, wide, pairs, data):
    steps, rows, cols, width = field.shape
    half = steps // 2
    points = rows * cols
    spread_coefs(own, ctop, cbottom, line, wide)
    pairs[0, :, 0:width] = jnp.zeros((points, width), pairs.dtype)

    @pl.loop(0, half)
    def _(step):
        def own_row(row):
            return side_by_side(field[step, row], field[step + half, row], chunk)

        def store(row, value):
            span = slice(row * cols, (row + 1) * cols)
            now = value.astype(pairs.dtype)
            late = jnp.where(first_lanes(value), 0.0, swap_lanes(value)).astype(pairs.dtype)
            pairs[step + half, span, width : 2 * width] = now
            pairs[step + half + 1, span, 0:width] = now
            pairs[step, span, width : 2 * width] = late
            pairs[step + 1, span, 0:width] = late

        two_sweeps(message_loader(own_row, top, bottom, step, rows, cols), wide, rows, store)

    for step in range(0, half, 2):
        acc = None
        for lag in range(min(steps, step + half + 2)):
            left = jnp.concatenate([kern[lag, row] for row in range(rows)], axis=1)
            term = jnp.dot(left, pairs[step + 1 - lag + half], preferred_element_type=jnp.float32)
            acc = term if acc is None else acc + term
        data[step] = acc[:, 0:width]
        data[step + 1] = acc[:, width : 2 * width]
    kept = half // 2
    mine[...] = data[pl.ds(twin[0] * kept, kept)]
    other[...] = data[pl.ds((1 - twin[0]) * kept, kept)].astype(other.dtype)


def forward(chunk, twin, field, top, bottom, coefs, ctop, cbottom, kern, after):
    steps, rows, cols, width = field.shape
    sensors = kern.shape[2]
    points = rows * cols
    half = steps // 2
    return call(
        functools.partial(forward_kernel, chunk),
        "forward",
        (
            jax.ShapeDtypeStruct((half // 2, sensors, width), jnp.float32),
            jax.ShapeDtypeStruct((half // 2, sensors, width), jnp.bfloat16),
        ),
        [SMEM] + [VMEM] * 7 + [ANY],
        (VMEM, VMEM),
        [
            pltpu.VMEM((cols, cols), jnp.float32),
            pltpu.VMEM((2, rows + 2 * HALO, cols, width), jnp.float32),
            pltpu.VMEM((steps + 1, points, 2 * width), jnp.bfloat16),
            pltpu.VMEM((half, sensors, width), jnp.float32),
        ],
        30,
        steps * (steps + 1) * sensors * points * width // 2,
        10 * MIB,
    )(twin, field, top, bottom, coefs, ctop, cbottom, kern, after)


def join_kernel(mine, got, both):
    both[...] = (mine[...] + got[...].astype(jnp.float32)).astype(both.dtype)


def join(mine, got):
    out = jax.ShapeDtypeStruct(got.shape, got.dtype)
    return call(join_kernel, "join", out, [VMEM] * 2, VMEM, [], 16, mine.size, 8 * mine.size)(mine, got)


def scale_kernel(pieces, prec, _, copies):
    total = pieces[0].astype(jnp.float32)
    for piece in range(1, pieces.shape[0]):
        total = total + pieces[piece].astype(jnp.float32)
    weighted = (total * prec[...]).astype(copies.dtype)
    for piece in range(pieces.shape[0]):
        copies[piece] = weighted


def scale(pieces, prec, after):
    out = jax.ShapeDtypeStruct(pieces.shape, pieces.dtype)
    moved = 4 * pieces.size
    return call(scale_kernel, "scale", out, [VMEM, VMEM, ANY], VMEM, [], 16, pieces.size, moved)(pieces, prec, after)


def turn_kernel(kern, _, turned):
    for row in range(kern.shape[1]):
        turned[0, row] = kern[0, row].T


def turn(kern, after):
    steps, rows, sensors, cols = kern.shape
    return call(
        turn_kernel,
        "turn",
        jax.ShapeDtypeStruct((steps, rows, cols, sensors), kern.dtype),
        [pl.BlockSpec((1, rows, sensors, cols), lambda lag: (lag, 0, 0, 0)), ANY],
        pl.BlockSpec((1, rows, cols, sensors), lambda lag: (lag, 0, 0, 0)),
        [],
        16,
        0,
        4 * kern.size,
        (steps,),
    )(kern, after)


def adjoint_kernel(twin, mine, other, turned, _, field, head, tail, pairs):
    half, rows, cols, width = field.shape
    steps = 2 * half
    sensors = mine.shape[1]
    kept = half // 2
    pairs[steps, :, width : 2 * width] = jnp.zeros((sensors, width), pairs.dtype)
    for source, part in ((mine, twin[0]), (other, 1 - twin[0])):
        for at in range(kept):
            step = part * kept + at
            now = source[at]
            wide = now.astype(jnp.float32)
            late = jnp.where(first_lanes(wide), swap_lanes(wide), 0.0).astype(pairs.dtype)
            pairs[step + 1, :, 0:width] = now
            pairs[step, :, width : 2 * width] = now
            pairs[step + half + 1, :, 0:width] = late
            pairs[step + half, :, width : 2 * width] = late
    for step in range(0, half, 2):
        acc = None
        for lag in range(steps - step):
            left = turned[lag].reshape(rows * cols, sensors)
            term = jnp.dot(left, pairs[step + lag + 1], preferred_element_type=jnp.float32)
            acc = term if acc is None else acc + term
        for side in range(2):
            part = acc[:, side * width : (side + 1) * width]
            field[step + side] = part.reshape(rows, cols, width)
            at = (step + side) * HALO * cols
            head[at : at + HALO * cols, :] = part[0 : HALO * cols].astype(head.dtype)
            tail[at : at + HALO * cols, :] = part[(rows - HALO) * cols :].astype(tail.dtype)


def adjoint(twin, mine, other, turned, after):
    steps, rows, cols, sensors = turned.shape
    width = mine.shape[2]
    half = steps // 2
    edge = jax.ShapeDtypeStruct((half * HALO * cols, width), jnp.bfloat16)
    return call(
        adjoint_kernel,
        "adjoint",
        (jax.ShapeDtypeStruct((half, rows, cols, width), jnp.float32), edge, edge),
        [SMEM] + [VMEM] * 3 + [ANY],
        (VMEM,) * 3,
        [pltpu.VMEM((steps + 1, sensors, 2 * width), jnp.bfloat16)],
        30,
        steps * (steps + 1) * sensors * rows * cols * width // 2,
        10 * MIB,
    )(twin, mine, other, turned, after)


def smooth_kernel(field, top, bottom, own, ctop, cbottom, _, out, line, wide):
    half, rows, cols, _ = field.shape
    spread_coefs(own, ctop, cbottom, line, wide)

    @pl.loop(0, half)
    def _(step):
        def own_row(row):
            return field[step, row]

        def store(row, value):
            out[step, row] = value

        two_sweeps(message_loader(own_row, top, bottom, step, rows, cols), wide, rows, store)


def coef_scratch(rows, cols, width):
    return [
        pltpu.VMEM((cols, cols), jnp.float32),
        pltpu.VMEM((2, rows + 2 * HALO, cols, width), jnp.float32),
    ]


def smooth(field, top, bottom, coefs, ctop, cbottom, after):
    half, rows, cols, width = field.shape
    return call(
        smooth_kernel,
        "smooth",
        jax.ShapeDtypeStruct(field.shape, jnp.float32),
        [VMEM] * 6 + [ANY],
        VMEM,
        coef_scratch(rows, cols, width),
        16,
        20 * field.size,
        4 * MIB,
    )(field, top, bottom, coefs, ctop, cbottom, after)


def finish_kernel(field, top, bottom, done, own, ctop, cbottom, out, line, wide):
    rows, cols = field.shape[1], field.shape[2]

    @pl.when(pl.program_id(0) == 0)
    def _():
        spread_coefs(own, ctop, cbottom, line, wide)

    def own_row(row):
        return field[0, row]

    def store(row, value):
        before = done[0, row]
        out[0, 0, row] = jnp.where(first_lanes(value), before, swap_lanes(value))
        out[1, 0, row] = jnp.where(first_lanes(value), swap_lanes(before), value)

    two_sweeps(message_loader(own_row, top, bottom, 0, rows, cols), wide, rows, store)


def finish(field, top, bottom, done, coefs, ctop, cbottom):
    half, rows, cols, width = field.shape
    whole = pl.BlockSpec((1, rows, cols, width), lambda step: (step, 0, 0, 0))
    edge = pl.BlockSpec((HALO * cols, width), lambda step: (step, 0))
    return call(
        finish_kernel,
        "finish",
        jax.ShapeDtypeStruct((2,) + field.shape, jnp.float32),
        [whole, edge, edge, whole, VMEM, VMEM, VMEM],
        pl.BlockSpec((2, 1, rows, cols, width), lambda step: (0, step, 0, 0, 0)),
        coef_scratch(rows, cols, width),
        16,
        20 * field.size,
        7 * MIB,
        (half,),
    )(field, top, bottom, done, coefs, ctop, cbottom)


def from_neighbours(head, tail):
    count = lax.axis_size("tile")
    down = [(i, i + 1) for i in range(count - 1)]
    up = [(i + 1, i) for i in range(count - 1)]
    return lax.ppermute(tail, "tile", down), lax.ppermute(head, "tile", up)


def swap_twins(value):
    return lax.ppermute(value, "twin", [(0, 1), (1, 0)])


def body(sketch, diag_coef, couple, kernel, noise_prec):
    steps, _, rows, cols, width = sketch.shape
    sensors = kernel.shape[1]
    others = ("pair", "tile")
    groups = lax.axis_size(others)
    twin = lax.axis_index("twin")
    which = twin.reshape(1)
    field = sketch.reshape(steps, rows, cols, width)
    coefs = jnp.concatenate([diag_coef, couple])
    kern = jnp.transpose(kernel.reshape(steps, sensors, rows, cols), (0, 2, 1, 3))

    quarter = steps // 4 * sensors
    share = quarter // groups
    start = twin * quarter + lax.axis_index(others) * share
    flat = noise_prec.reshape(-1)
    early = lax.dynamic_slice(flat, (start,), (share,))
    late = lax.dynamic_slice(flat, (start + 2 * quarter,), (share,))
    prec = jnp.where(first_lanes(jnp.zeros((share, width))), early[:, None], late[:, None])

    head_a, tail_a, head_b, tail_b = pack(field, coefs)
    edges = [from_neighbours(head_a, tail_a), from_neighbours(head_b, tail_b)]
    note = edges[0]

    def summed(chunk, after):
        mine, other = forward(chunk, which, field, *edges[chunk], coefs, *note, kern, after)
        both = join(mine, swap_twins(other))
        return both, lax.all_to_all(both.reshape(groups, share, width), others, 0, 0, tiled=True)

    def spread(copies):
        return lax.all_to_all(copies, others, 0, 0, tiled=True).reshape(steps // 4, sensors, width)

    def returned(weighted, turned, after):
        back, head, tail = adjoint(which, weighted, swap_twins(weighted), turned, after)
        return back, *from_neighbours(head, tail)

    both_a, pieces_a = summed(0, coefs)
    both_b, pieces_b = summed(1, both_a)
    copies_a = scale(pieces_a, prec, both_b)
    weighted_a = spread(copies_a)
    turned = turn(kern, copies_a)
    copies_b = scale(pieces_b, prec, turned)
    weighted_b = spread(copies_b)
    field_a = returned(weighted_a, turned, copies_b)
    field_b = returned(weighted_b, turned, field_a[0])
    done = smooth(*field_a, coefs, *note, field_b[0])
    return finish(*field_b, done, coefs, *note).reshape(sketch.shape)


def solution(mesh):
    bands, tiles = mesh.shape["band"], mesh.shape["tile"]
    fine = Mesh(mesh.devices.reshape(bands // 2, 2, tiles), ("pair", "twin", "tile"))
    band = ("pair", "twin")
    placed = (
        P(None, band, "tile", None, None),
        P(band, "tile", None),
        P(band, "tile", None),
        P(None, None, band, "tile", None),
        P(),
    )
    return jax.shard_map(
        body,
        mesh=fine,
        in_specs=placed,
        out_specs=P(None, band, "tile", None, None),
        check_vma=False,
    )
```

```python
import functools

import jax
import jax.numpy as jnp
from jax import lax
from jax.experimental import pallas as pl
from jax.experimental.pallas import tpu as pltpu
from jax.sharding import Mesh
from jax.sharding import PartitionSpec as P

MIB = 1 << 20
HALO = 2
NOTE = 16
PARTS = 1
VMEM = pl.BlockSpec(memory_space=pltpu.VMEM)
SMEM = pl.BlockSpec(memory_space=pltpu.SMEM)
HBM = pl.BlockSpec(memory_space=pltpu.HBM)


def call(kernel, name, out_shape, in_specs, out_specs, scratch, limit, moved, grid=(), aliases={}):
    return pl.pallas_call(
        kernel,
        grid=grid,
        out_shape=out_shape,
        in_specs=in_specs,
        out_specs=out_specs,
        scratch_shapes=scratch,
        input_output_aliases=aliases,
        compiler_params=pltpu.CompilerParams(vmem_limit_bytes=limit * MIB),
        cost_estimate=pl.CostEstimate(flops=0, bytes_accessed=moved * MIB, transcendentals=0),
        name=name,
    )


def f32(*shape):
    return jax.ShapeDtypeStruct(shape, jnp.float32)


def bf16(*shape):
    return jax.ShapeDtypeStruct(shape, jnp.bfloat16)


def edge_rows(rows):
    return [*range(HALO), *range(rows - HALO, rows)]


def beside(w):
    cols = w.shape[0]
    at = lax.broadcasted_iota(jnp.int32, w.shape, 0)
    before = jnp.where(at == 0, 0.0, pltpu.roll(w, 1, 0))
    after = jnp.where(at == cols - 1, 0.0, pltpu.roll(w, cols - 1, 0))
    return before + after


def note_row(which, row):
    return (which * HALO + row) * 2


def spread_line(line, wide, which, count):
    turned = line[...].T
    cols, width = wide.shape[2], wide.shape[3]
    for row in range(count):
        wide[which, row] = jnp.broadcast_to(turned[:, row : row + 1], (cols, width))


def spread_own(diag, couple, line, wide):
    rows = diag.shape[0]
    for which, own in enumerate((diag, couple)):
        line[...] = jnp.zeros(line.shape, line.dtype)
        line[0:rows, :] = own[...]
        spread_line(line, wide, which, rows)


def spread_all(diag, couple, ctop, cbottom, line, wide):
    rows, cols = diag.shape
    size = ctop.shape[0] - NOTE
    above = ctop[size : size + NOTE, :].astype(jnp.float32)
    below = cbottom[size : size + NOTE, :].astype(jnp.float32)
    for which, own in enumerate((diag, couple)):
        line[...] = jnp.zeros(line.shape, line.dtype)
        for row in range(HALO):
            at = note_row(which, row)
            line[row : row + 1, :] = (above[at : at + 1] + above[at + 1 : at + 2])[:, 0:cols]
            far = HALO + rows + row
            line[far : far + 1, :] = (below[at : at + 1] + below[at + 1 : at + 2])[:, 0:cols]
        line[HALO : HALO + rows, :] = own[...]
        spread_line(line, wide, which, rows + 2 * HALO)


def coef_scratch(rows, cols, width):
    return [pltpu.VMEM((cols, cols), jnp.float32), pltpu.VMEM((2, rows, cols, width), jnp.float32)]


def one_sweep(values, scaled, wide, row):
    around = beside(scaled[row])
    if row > 0:
        around = around + scaled[row - 1]
    if row + 1 < len(scaled):
        around = around + scaled[row + 1]
    return wide[0, row] * values[row] - wide[1, row] * around


def own_sweeps(load, wide, rows, store):
    values, scaled, first, second = ([None] * rows for _ in range(4))
    for row in range(rows + 2):
        if row < rows:
            values[row] = load(row)
            scaled[row] = wide[1, row] * values[row]
        if 0 < row <= rows:
            first[row - 1] = one_sweep(values, scaled, wide, row - 1)
            second[row - 1] = wide[1, row - 1] * first[row - 1]
        if row > 1:
            store(row - 2, one_sweep(first, second, wide, row - 2), scaled)


def halo_part(message, at, edge_scaled, wide, side, rows, cols):
    order = (0, 1, HALO, HALO + 1) if side == 0 else tuple(rows + 2 * HALO - 1 - i for i in range(4))
    far, near, edge, inner = order
    far_row, near_row = (0, 1) if side == 0 else (1, 0)

    def take(row):
        start = pl.multiple_of(at + row * cols, cols)
        return message[pl.ds(start, cols), :].astype(jnp.float32)

    near_value = take(near_row)
    near_scaled = wide[1, near] * near_value
    around = wide[1, far] * take(far_row) + edge_scaled + beside(near_scaled)
    near_second = wide[1, near] * (wide[0, near] * near_value - wide[1, near] * around)
    first = -wide[1, edge] * near_scaled
    second = wide[1, edge] * first
    on_edge = wide[0, edge] * first - wide[1, edge] * (near_second + beside(second))
    return on_edge, -wide[1, inner] * second


def pack_kernel(field, diag, couple, *refs):
    heads, tails = refs[:PARTS], refs[PARTS : 2 * PARTS]
    note, edges, arrived = refs[2 * PARTS :]
    steps, rows, cols, width = field.shape
    span = steps // PARTS
    copies = []
    for side, first in enumerate((0, rows - HALO)):
        copies.append(pltpu.make_async_copy(field.at[:, pl.ds(first, HALO)], edges.at[side], arrived.at[side]))
        copies[side].start()
    for side, first, outs in ((0, 0, heads), (1, rows - HALO, tails)):
        note[...] = jnp.zeros(note.shape, note.dtype)
        for which, own in enumerate((diag, couple)):
            for row in range(HALO):
                at = note_row(which, row)
                whole = own[first + row : first + row + 1, :]
                high = whole.astype(jnp.bfloat16).astype(jnp.float32)
                note[at : at + 1, 0:cols] = high
                note[at + 1 : at + 2, 0:cols] = whole - high
        outs[0][span * HALO * cols :, :] = note[...].astype(jnp.bfloat16)
        copies[side].wait()
        for step in range(steps):
            for row in range(HALO):
                at = (step % span * HALO + row) * cols
                outs[step // span][at : at + cols, :] = edges[side, step, row].astype(jnp.bfloat16)


def pack(field, diag, couple):
    steps, rows, cols, width = field.shape
    size = steps // PARTS * HALO * cols
    shapes = [bf16(size + (NOTE if part == 0 else 0), width) for part in range(PARTS)]
    out = call(
        pack_kernel,
        "pack",
        shapes * 2,
        [HBM, VMEM, VMEM],
        [VMEM] * (2 * PARTS),
        [
            pltpu.VMEM((NOTE, width), jnp.float32),
            pltpu.VMEM((2, steps, HALO, cols, width), jnp.float32),
            pltpu.SemaphoreType.DMA((2,)),
        ],
        60,
        3,
    )(field, diag, couple)
    return out[:PARTS], out[PARTS:]


def before_kernel(field, diag, couple, kern, edges, scaled, data, line, wide, pairs):
    steps, rows, cols, width = field.shape
    inner = rows - 2 * HALO
    listed = edge_rows(rows)
    spread_own(diag, couple, line, wide)
    pairs[0, :, 0:width] = jnp.zeros((inner * cols, width), pairs.dtype)

    @pl.loop(0, steps)
    def _(step):
        def store(row, value, weighted):
            if row in listed:
                edges[step, listed.index(row)] = value
            else:
                at = (row - HALO) * cols
                rounded = value.astype(pairs.dtype)
                pairs[step, at : at + cols, width : 2 * width] = rounded
                pairs[step + 1, at : at + cols, 0:width] = rounded
            if row == 0:
                scaled[step, 0] = weighted[0]
            if row == rows - 1:
                scaled[step, 1] = weighted[rows - 1]

        own_sweeps(lambda row: field[step, row], wide, rows, store)

    for step in range(0, steps, 2):
        acc = None
        for lag in range(step + 2):
            left = jnp.concatenate([kern[lag, row] for row in range(HALO, rows - HALO)], axis=1)
            term = jnp.dot(left, pairs[step + 1 - lag], preferred_element_type=jnp.float32)
            acc = term if acc is None else acc + term
        data[step] = acc[:, 0:width]
        data[step + 1] = acc[:, width : 2 * width]


def before(field, diag, couple, kern):
    steps, rows, cols, width = field.shape
    sensors = kern.shape[2]
    inner = (rows - 2 * HALO) * cols
    return call(
        before_kernel,
        "before",
        (f32(steps, 2 * HALO, cols, width), f32(steps, 2, cols, width), f32(steps, sensors, width)),
        [VMEM] * 4,
        [VMEM] * 3,
        coef_scratch(rows, cols, width) + [pltpu.VMEM((steps + 1, inner, 2 * width), jnp.bfloat16)],
        24,
        12,
    )(field, diag, couple, kern)


def forward_kernel(part, twin, top, bottom, diag, couple, ctop, cbottom, edges, scaled, kern, start, *refs):
    past = refs[0] if part else None
    mine, other, pairs, line, wide, data = refs[1 if part else 0 :]
    steps, rows = kern.shape[0], kern.shape[1]
    cols, width = edges.shape[2], edges.shape[3]
    span = steps // PARTS
    first = part * span
    listed = edge_rows(rows)
    spread_all(diag, couple, ctop, cbottom, line, wide)
    if part:
        pairs[0, :, 0:width] = past[span, :, 0:width]
    else:
        pairs[0, :, 0:width] = jnp.zeros((2 * HALO * cols, width), pairs.dtype)

    @pl.loop(0, span)
    def _(step):
        for side, message in enumerate((top, bottom)):
            at = step * (HALO * cols)
            on_edge, inner = halo_part(message, at, scaled[step + first, side], wide, side, rows, cols)
            spots = (0, 1) if side == 0 else (2 * HALO - 1, 2 * HALO - 2)
            for spot, extra in zip(spots, (on_edge, inner)):
                rounded = (edges[step + first, spot] + extra).astype(pairs.dtype)
                at = spot * cols
                pairs[step, at : at + cols, width : 2 * width] = rounded
                pairs[step + 1, at : at + cols, 0:width] = rounded

    for step in range(first, first + span, 2):
        acc = jnp.concatenate([start[step], start[step + 1]], axis=1)
        for lag in range(step + 2):
            left = jnp.concatenate([kern[lag, row] for row in listed], axis=1)
            block = step + 1 - lag
            right = pairs[block - first] if block >= first else past[block]
            acc = acc + jnp.dot(left, right, preferred_element_type=jnp.float32)
        data[step - first] = acc[:, 0:width]
        data[step - first + 1] = acc[:, width : 2 * width]
    kept = data.shape[1] // 2
    mine[...] = data[:, pl.ds(pl.multiple_of(twin[0] * kept, kept), kept), :]
    other[...] = data[:, pl.ds(pl.multiple_of((1 - twin[0]) * kept, kept), kept), :].astype(other.dtype)


def forward(part, twin, top, bottom, diag, couple, ctop, cbottom, edges, scaled, kern, start, past):
    steps, rows, sensors, cols = kern.shape
    width = edges.shape[3]
    span = steps // PARTS
    extra = [past] if part else []
    return call(
        functools.partial(forward_kernel, part),
        "forward",
        (f32(span, sensors // 2, width), bf16(span, sensors // 2, width), bf16(span + 1, 2 * HALO * cols, 2 * width)),
        [SMEM] + [VMEM] * (10 + len(extra)),
        [VMEM] * 3,
        coef_scratch(rows + 2 * HALO, cols, width) + [pltpu.VMEM((span, sensors, width), jnp.float32)],
        24,
        4,
    )(twin, top, bottom, diag, couple, ctop, cbottom, edges, scaled, kern, start, *extra)


def join_kernel(mine, got, both):
    both[...] = (mine[...] + got[...].astype(jnp.float32)).astype(both.dtype)


def join(mine, got):
    return call(join_kernel, "join", bf16(*got.shape), [VMEM] * 2, VMEM, [], 16, 1)(mine, got)


def scale_kernel(pieces, prec, out):
    total = pieces[0].astype(jnp.float32)
    for piece in range(1, pieces.shape[0]):
        total = total + pieces[piece].astype(jnp.float32)
    weighted = (total * prec[...]).astype(out.dtype)
    for piece in range(pieces.shape[0]):
        out[piece] = weighted


def scale(pieces, prec):
    return call(scale_kernel, "scale", bf16(*pieces.shape), [VMEM] * 2, VMEM, [], 16, 1)(pieces, prec)


def turn_kernel(kern, turned):
    for row in range(kern.shape[1]):
        turned[0, row] = kern[0, row].T


def turn(kern):
    steps, rows, sensors, cols = kern.shape
    return call(
        turn_kernel,
        "turn",
        bf16(steps, rows, cols, sensors),
        [pl.BlockSpec((1, rows, sensors, cols), lambda lag: (lag, 0, 0, 0))],
        pl.BlockSpec((1, rows, cols, sensors), lambda lag: (lag, 0, 0, 0)),
        [],
        16,
        6,
        (steps,),
    )(kern)


def fill_pairs(twin, mine, other, pairs):
    steps, kept, width = mine.shape
    pairs[steps, :, width : 2 * width] = jnp.zeros((2 * kept, width), pairs.dtype)
    for source, half in ((mine, twin[0]), (other, 1 - twin[0])):
        at = pl.ds(pl.multiple_of(half * kept, kept), kept)
        for step in range(steps):
            pairs[step + 1, at, 0:width] = source[step]
            pairs[step, at, width : 2 * width] = source[step]


def outer_kernel(twin, mine, other, turned, field, head, tail, pairs):
    steps, rows, cols, sensors = turned.shape
    width = mine.shape[2]
    fill_pairs(twin, mine, other, pairs)
    strip = HALO * cols
    for step in range(0, steps, 2):
        acc = None
        for lag in range(steps - step):
            left = jnp.concatenate([turned[lag, 0:HALO], turned[lag, rows - HALO : rows]], axis=0)
            left = left.reshape(2 * strip, sensors)
            term = jnp.dot(left, pairs[step + lag + 1], preferred_element_type=jnp.float32)
            acc = term if acc is None else acc + term
        for side in range(2):
            part = acc[:, side * width : (side + 1) * width]
            field[step + side] = part.reshape(2 * HALO, cols, width)
            at = (step + side) * strip
            head[at : at + strip, :] = part[0:strip].astype(head.dtype)
            tail[at : at + strip, :] = part[strip:].astype(tail.dtype)


def outer(twin, mine, other, turned):
    steps, rows, cols, sensors = turned.shape
    width = mine.shape[2]
    edge = bf16(steps * HALO * cols, width)
    return call(
        outer_kernel,
        "outer",
        (f32(steps, 2 * HALO, cols, width), edge, edge),
        [SMEM] + [VMEM] * 3,
        [VMEM] * 3,
        [pltpu.VMEM((steps + 1, sensors, 2 * width), jnp.bfloat16)],
        24,
        4,
    )(twin, mine, other, turned)


def inner_kernel(twin, mine, other, turned, field, diag, couple, edges, scaled, out, pairs, core, line, wide):
    steps, rows, cols, sensors = turned.shape
    width = mine.shape[2]
    inner = rows - 2 * HALO
    pack_at = pl.program_id(0)

    @pl.when(pack_at == 0)
    def _():
        fill_pairs(twin, mine, other, pairs)
        spread_own(diag, couple, line, wide)
        for step in range(0, steps, 2):
            acc = None
            for lag in range(steps - step):
                left = turned[lag, HALO : rows - HALO].reshape(inner * cols, sensors)
                term = jnp.dot(left, pairs[step + lag + 1], preferred_element_type=jnp.float32)
                acc = term if acc is None else acc + term
            for side in range(2):
                core[step + side] = acc[:, side * width : (side + 1) * width].reshape(inner, cols, width)

    listed = edge_rows(rows)
    span = out.shape[0]

    @pl.loop(0, span)
    def _(at):
        step = pack_at * span + at

        def load(row):
            return field[step, listed.index(row)] if row in listed else core[step, row - HALO]

        def store(row, value, weighted):
            if row in listed:
                edges[step, listed.index(row)] = value
            else:
                out[at, row - HALO] = value
            if row == 0:
                scaled[step, 0] = weighted[0]
            if row == rows - 1:
                scaled[step, 1] = weighted[rows - 1]

        own_sweeps(load, wide, rows, store)


def inner(twin, mine, other, turned, field, diag, couple):
    steps, rows, cols, sensors = turned.shape
    width = mine.shape[2]
    core = rows - 2 * HALO
    assert core == HALO
    span = steps // 2
    return call(
        inner_kernel,
        "inner",
        (f32(steps, 2 * HALO, cols, width), f32(steps, 2, cols, width), f32(steps, rows, cols, width)),
        [SMEM] + [VMEM] * 6,
        [VMEM, VMEM, pl.BlockSpec((span, core, cols, width), lambda step: (step, 1, 0, 0))],
        [
            pltpu.VMEM((steps + 1, sensors, 2 * width), jnp.bfloat16),
            pltpu.VMEM((steps, core, cols, width), jnp.float32),
        ]
        + coef_scratch(rows, cols, width),
        30,
        10,
        (steps // span,),
    )(twin, mine, other, turned, field, diag, couple)


def finish_kernel(top, bottom, diag, couple, ctop, cbottom, edges, scaled, _, out, line, wide):
    rows, cols = diag.shape
    span = out.shape[0]
    strip = HALO * cols

    @pl.when((pl.program_id(0) == 0) & (pl.program_id(1) == 0))
    def _():
        spread_all(diag, couple, ctop, cbottom, line, wide)

    for side, message in enumerate((top, bottom)):

        @pl.when(pl.program_id(1) == side)
        def _():
            @pl.loop(0, span)
            def _(at):
                step = pl.program_id(0) * span + at
                on_edge, inner = halo_part(message, step * strip, scaled[step, side], wide, side, rows, cols)
                spots = (0, 1) if side == 0 else (2 * HALO - 1, 2 * HALO - 2)
                for spot, extra in zip(spots, (on_edge, inner)):
                    out[at, spot % HALO] = edges[step, spot] + extra


def finish(top, bottom, diag, couple, ctop, cbottom, edges, scaled, out):
    steps, rows, cols, width = out.shape
    span = steps // 2
    return call(
        finish_kernel,
        "finish",
        f32(*out.shape),
        [VMEM] * 8 + [HBM],
        pl.BlockSpec((span, HALO, cols, width), lambda step, side: (step, side * (rows // HALO - 1), 0, 0)),
        coef_scratch(rows + 2 * HALO, cols, width),
        24,
        5,
        (steps // span, 2),
        {8: 0},
    )(top, bottom, diag, couple, ctop, cbottom, edges, scaled, out)


def from_neighbours(head, tail):
    count = lax.axis_size("tile")
    down = [(i, i + 1) for i in range(count - 1)]
    up = [(i + 1, i) for i in range(count - 1)]
    return lax.ppermute(tail, "tile", down), lax.ppermute(head, "tile", up)


def swap_twins(value):
    return lax.ppermute(value, "twin", [(0, 1), (1, 0)])


def body(sketch, diag_coef, couple, kernel, noise_prec):
    steps, _, rows, cols, width = sketch.shape
    sensors = kernel.shape[1]
    others = ("pair", "tile")
    groups = lax.axis_size(others)
    twin = lax.axis_index("twin")
    which = twin.reshape(1)
    field = sketch.reshape(steps, rows, cols, width)
    diag, couple = diag_coef.reshape(rows, cols), couple.reshape(rows, cols)
    kern = jnp.transpose(kernel.reshape(steps, sensors, rows, cols), (0, 2, 1, 3))
    kept = sensors // 2
    span = steps // PARTS
    share = span * kept // groups

    heads, tails = pack(field, diag, couple)
    halos = [from_neighbours(head, tail) for head, tail in zip(heads, tails)]
    note = halos[0]
    edges, scaled, data = before(field, diag, couple, kern)
    turned = turn(kern)

    noise = lax.dynamic_slice(noise_prec, (0, twin * kept), (steps, kept)).reshape(PARTS, span * kept)
    start = lax.axis_index(others) * share
    prec = [
        jnp.broadcast_to(lax.dynamic_slice(noise[part], (start,), (share,))[:, None], (share, width))
        for part in range(PARTS)
    ]

    past, copies = None, []
    for part in range(PARTS):
        mine, other, past = forward(part, which, *halos[part], diag, couple, *note, edges, scaled, kern, data, past)
        both = join(mine, swap_twins(other)).reshape(groups, share, width)
        pieces = lax.all_to_all(both, others, 0, 0, tiled=True)
        copies.append(scale(pieces, prec[part]))

    sent = copies[0] if PARTS == 1 else jnp.concatenate(copies, axis=1)
    weighted = lax.all_to_all(sent, others, 0, 0, tiled=True)
    if PARTS > 1:
        weighted = jnp.swapaxes(weighted.reshape(groups, PARTS, share, width), 0, 1)
    weighted = weighted.reshape(steps, kept, width)
    other = swap_twins(weighted)
    field, head, tail = outer(which, weighted, other, turned)
    top, bottom = from_neighbours(head, tail)
    edges, scaled, out = inner(which, weighted, other, turned, field, diag, couple)
    return finish(top, bottom, diag, couple, *note, edges, scaled, out).reshape(sketch.shape)


def solution(mesh):
    bands, tiles = mesh.shape["band"], mesh.shape["tile"]
    fine = Mesh(mesh.devices.reshape(bands // 2, 2, tiles), ("pair", "twin", "tile"))
    band = ("pair", "twin")
    placed = (
        P(None, band, "tile", None, None),
        P(band, "tile", None),
        P(band, "tile", None),
        P(None, None, band, "tile", None),
        P(),
    )
    return jax.shard_map(
        body,
        mesh=fine,
        in_specs=placed,
        out_specs=P(None, band, "tile", None, None),
        check_vma=False,
    )
```

```python
import functools

import jax
import jax.numpy as jnp
from jax import lax
from jax.experimental import pallas as pl
from jax.experimental.pallas import tpu as pltpu
from jax.sharding import Mesh
from jax.sharding import PartitionSpec as P

MIB = 1 << 20
HALO = 2
PARTS = 1
VMEM = pl.BlockSpec(memory_space=pltpu.VMEM)
SMEM = pl.BlockSpec(memory_space=pltpu.SMEM)
HBM = pl.BlockSpec(memory_space=pltpu.HBM)


def call(kernel, name, out_shape, in_specs, out_specs, scratch, limit, moved, grid=(), aliases={}):
    return pl.pallas_call(
        kernel,
        grid=grid,
        out_shape=out_shape,
        in_specs=in_specs,
        out_specs=out_specs,
        scratch_shapes=scratch,
        input_output_aliases=aliases,
        compiler_params=pltpu.CompilerParams(vmem_limit_bytes=limit * MIB),
        cost_estimate=pl.CostEstimate(flops=0, bytes_accessed=moved * MIB, transcendentals=0),
        name=name,
    )


def f32(*shape):
    return jax.ShapeDtypeStruct(shape, jnp.float32)


def bf16(*shape):
    return jax.ShapeDtypeStruct(shape, jnp.bfloat16)


def edge_rows(rows):
    return [*range(HALO), *range(rows - HALO, rows)]


def beside(w):
    cols = w.shape[0]
    at = lax.broadcasted_iota(jnp.int32, w.shape, 0)
    before = jnp.where(at == 0, 0.0, pltpu.roll(w, 1, 0))
    after = jnp.where(at == cols - 1, 0.0, pltpu.roll(w, cols - 1, 0))
    return before + after


def spread(own, halos, line, wide):
    rows, cols = own[0].shape
    for which in range(2):
        line[...] = jnp.zeros(line.shape, line.dtype)
        for side, halo in enumerate(halos):
            at = side * (HALO + rows)
            line[at : at + HALO, :] = halo[which]
        line[HALO : HALO + rows, :] = own[which][...]
        turned = line[...].T
        for row in range(rows + 2 * HALO):
            wide[which, row] = jnp.broadcast_to(turned[:, row : row + 1], wide.shape[2:])


def mix_coefs(wide, mix):
    total = wide.shape[1]
    for side in range(2):
        far, near, edge, inner = (row if side == 0 else total - 1 - row for row in range(4))
        square = wide[1, edge] * wide[1, edge]
        mix[side, 0] = wide[1, near]
        mix[side, 1] = wide[1, far]
        mix[side, 2] = wide[1, near] * wide[0, near]
        mix[side, 3] = wide[1, near] * wide[1, near]
        mix[side, 4] = -square
        mix[side, 5] = -wide[0, edge] * wide[1, edge]
        mix[side, 6] = wide[1, edge]
        mix[side, 7] = wide[1, inner] * square


def coef_scratch(rows, cols, width):
    return [pltpu.VMEM((cols, cols), jnp.float32), pltpu.VMEM((2, rows, cols, width), jnp.float32)]


def one_sweep(values, scaled, wide, row):
    around = beside(scaled[row])
    if row > 0:
        around = around + scaled[row - 1]
    if row + 1 < len(scaled):
        around = around + scaled[row + 1]
    return wide[0, row + HALO] * values[row] - wide[1, row + HALO] * around


def own_sweeps(load, wide, rows, store):
    values, scaled, first, second = ([None] * rows for _ in range(4))
    for row in range(rows + 2):
        if row < rows:
            values[row] = load(row)
            scaled[row] = wide[1, row + HALO] * values[row]
        if 0 < row <= rows:
            first[row - 1] = one_sweep(values, scaled, wide, row - 1)
            second[row - 1] = wide[1, row - 1 + HALO] * first[row - 1]
        if row > 1:
            store(row - 2, one_sweep(first, second, wide, row - 2), scaled)


def halo_part(message, at, edge_scaled, mix, side):
    cols = edge_scaled.shape[0]
    far_row, near_row = (0, 1) if side == 0 else (1, 0)

    def take(row):
        start = pl.multiple_of(at + row * cols, cols)
        return message[pl.ds(start, cols), :].astype(jnp.float32)

    near = take(near_row)
    scaled = mix[side, 0] * near
    around = mix[side, 1] * take(far_row) + edge_scaled + beside(scaled)
    near_second = mix[side, 2] * near - mix[side, 3] * around
    second = mix[side, 4] * scaled
    on_edge = mix[side, 5] * scaled - mix[side, 6] * (near_second + beside(second))
    return on_edge, mix[side, 7] * scaled


def spots_of(side):
    return (0, 1) if side == 0 else (2 * HALO - 1, 2 * HALO - 2)


def pack_kernel(field, *refs):
    heads, tails = refs[:PARTS], refs[PARTS : 2 * PARTS]
    edges, arrived = refs[2 * PARTS :]
    steps, rows, cols, width = field.shape
    span = steps // PARTS
    copies = []
    for side, first in enumerate((0, rows - HALO)):
        for part in range(PARTS):
            at = pl.ds(part * span, span)
            source = field.at[at, pl.ds(first, HALO)]
            copies.append(pltpu.make_async_copy(source, edges.at[side, at], arrived.at[side, part]))
            copies[-1].start()
    for side, outs in enumerate((heads, tails)):
        for part in range(PARTS):
            copies[side * PARTS + part].wait()
            for step in range(span):
                for row in range(HALO):
                    at = (step * HALO + row) * cols
                    outs[part][at : at + cols, :] = edges[side, part * span + step, row].astype(jnp.bfloat16)


def pack(field):
    steps, rows, cols, width = field.shape
    size = steps // PARTS * HALO * cols
    out = call(
        pack_kernel,
        "pack",
        [bf16(size, width)] * (2 * PARTS),
        [HBM],
        [VMEM] * (2 * PARTS),
        [pltpu.VMEM((2, steps, HALO, cols, width), jnp.float32), pltpu.SemaphoreType.DMA((2, PARTS))],
        62,
        3,
    )(field)
    return out[:PARTS], out[PARTS:]


def before_kernel(field, diag, couple, kern, edges, scaled, data, line, wide, pairs):
    steps, rows, cols, width = field.shape
    inner = rows - 2 * HALO
    listed = edge_rows(rows)
    spread((diag, couple), (), line, wide)
    pairs[0, :, 0:width] = jnp.zeros((inner * cols, width), pairs.dtype)

    @pl.loop(0, steps)
    def _(step):
        def store(row, value, weighted):
            if row in listed:
                edges[step, listed.index(row)] = value
            else:
                at = (row - HALO) * cols
                rounded = value.astype(pairs.dtype)
                pairs[step, at : at + cols, width : 2 * width] = rounded
                pairs[step + 1, at : at + cols, 0:width] = rounded
            if row == 0:
                scaled[step, 0] = weighted[0]
            if row == rows - 1:
                scaled[step, 1] = weighted[rows - 1]

        own_sweeps(lambda row: field[step, row], wide, rows, store)

    for step in range(0, steps, 2):
        acc = None
        for lag in range(step + 2):
            left = jnp.concatenate([kern[lag, row] for row in range(HALO, rows - HALO)], axis=1)
            term = jnp.dot(left, pairs[step + 1 - lag], preferred_element_type=jnp.float32)
            acc = term if acc is None else acc + term
        data[step] = acc[:, 0:width]
        data[step + 1] = acc[:, width : 2 * width]


def before(field, diag, couple, kern):
    steps, rows, cols, width = field.shape
    sensors = kern.shape[2]
    inner = (rows - 2 * HALO) * cols
    return call(
        before_kernel,
        "before",
        (f32(steps, 2 * HALO, cols, width), f32(steps, 2, cols, width), f32(steps, sensors, width)),
        [VMEM] * 4,
        [VMEM] * 3,
        coef_scratch(rows + 2 * HALO, cols, width) + [pltpu.VMEM((steps + 1, inner, 2 * width), jnp.bfloat16)],
        24,
        12,
    )(field, diag, couple, kern)


def forward_kernel(part, twin, top, bottom, diag, couple, ctop, cbottom, edges, scaled, kern, start, *refs):
    if PARTS == 1:
        _, mine, other, line, wide, mix, data, pairs = refs
        past = None
    elif part == 0:
        _, mine, other, pairs, line, wide, mix, data = refs
        past = None
    else:
        past, mine, other, line, wide, mix, data, pairs = refs
    steps, rows = kern.shape[0], kern.shape[1]
    cols, width = edges.shape[2], edges.shape[3]
    span = steps // PARTS
    first = part * span
    listed = edge_rows(rows)
    spread((diag, couple), (ctop, cbottom), line, wide)
    mix_coefs(wide, mix)
    if part:
        pairs[0, :, 0:width] = past[span, :, 0:width]
    else:
        pairs[0, :, 0:width] = jnp.zeros((2 * HALO * cols, width), pairs.dtype)

    @pl.loop(0, span)
    def _(step):
        for side, message in enumerate((top, bottom)):
            added = halo_part(message, step * (HALO * cols), scaled[step + first, side], mix, side)
            for spot, extra in zip(spots_of(side), added):
                rounded = (edges[step + first, spot] + extra).astype(pairs.dtype)
                at = spot * cols
                pairs[step, at : at + cols, width : 2 * width] = rounded
                pairs[step + 1, at : at + cols, 0:width] = rounded

    for step in range(first, first + span, 2):
        acc = jnp.concatenate([start[step], start[step + 1]], axis=1)
        for lag in range(step + 2):
            left = jnp.concatenate([kern[lag, row] for row in listed], axis=1)
            block = step + 1 - lag
            right = pairs[block - first] if block >= first else past[block]
            acc = acc + jnp.dot(left, right, preferred_element_type=jnp.float32)
        data[step - first] = acc[:, 0:width]
        data[step - first + 1] = acc[:, width : 2 * width]
    kept = data.shape[1] // 2
    mine[...] = data[:, pl.ds(pl.multiple_of(twin[0] * kept, kept), kept), :]
    other[...] = data[:, pl.ds(pl.multiple_of((1 - twin[0]) * kept, kept), kept), :].astype(other.dtype)


def forward(part, twin, top, bottom, diag, couple, ctop, cbottom, edges, scaled, kern, start, past):
    steps, rows, sensors, cols = kern.shape
    width = edges.shape[3]
    span = steps // PARTS
    blocks = (span + 1, 2 * HALO * cols, 2 * width)
    passed = PARTS > 1 and part == 0
    out = call(
        functools.partial(forward_kernel, part),
        "forward",
        [f32(span, sensors // 2, width), bf16(span, sensors // 2, width)] + [bf16(*blocks)] * passed,
        [SMEM] + [VMEM] * 10 + [VMEM if part else HBM],
        [VMEM] * (2 + passed),
        coef_scratch(rows + 2 * HALO, cols, width)
        + [pltpu.VMEM((2, 8, cols, width), jnp.float32), pltpu.VMEM((span, sensors, width), jnp.float32)]
        + [pltpu.VMEM(blocks, jnp.bfloat16)] * (not passed),
        24,
        1,
    )(twin, top, bottom, diag, couple, ctop, cbottom, edges, scaled, kern, start, past)
    return out if passed else (*out, None)


def join_kernel(mine, got, both):
    both[...] = (mine[...] + got[...].astype(jnp.float32)).astype(both.dtype)


def join(mine, got):
    return call(join_kernel, "join", bf16(*got.shape), [VMEM] * 2, VMEM, [], 16, 1)(mine, got)


def scale_kernel(pieces, prec, out):
    total = pieces[0].astype(jnp.float32)
    for piece in range(1, pieces.shape[0]):
        total = total + pieces[piece].astype(jnp.float32)
    weighted = (total * prec[...]).astype(out.dtype)
    for piece in range(pieces.shape[0]):
        out[piece] = weighted


def scale(pieces, prec):
    return call(scale_kernel, "scale", bf16(*pieces.shape), [VMEM] * 2, VMEM, [], 16, 1)(pieces, prec)


def turn_kernel(kern, turned):
    for row in range(kern.shape[1]):
        turned[0, row] = kern[0, row].T


def turn(kern):
    steps, rows, sensors, cols = kern.shape
    return call(
        turn_kernel,
        "turn",
        bf16(steps, rows, cols, sensors),
        [pl.BlockSpec((1, rows, sensors, cols), lambda lag: (lag, 0, 0, 0))],
        pl.BlockSpec((1, rows, cols, sensors), lambda lag: (lag, 0, 0, 0)),
        [],
        16,
        6,
        (steps,),
    )(kern)


def fill_pairs(twin, mine, other, pairs):
    steps, kept, width = mine.shape
    pairs[steps, :, width : 2 * width] = jnp.zeros((2 * kept, width), pairs.dtype)
    for source, half in ((mine, twin[0]), (other, 1 - twin[0])):
        at = pl.ds(pl.multiple_of(half * kept, kept), kept)
        for step in range(steps):
            pairs[step + 1, at, 0:width] = source[step]
            pairs[step, at, width : 2 * width] = source[step]


def outer_kernel(twin, mine, other, turned, field, head, tail, pairs):
    steps, rows, cols, sensors = turned.shape
    width = mine.shape[2]
    fill_pairs(twin, mine, other, pairs)
    strip = HALO * cols
    for step in range(0, steps, 2):
        acc = None
        for lag in range(steps - step):
            left = jnp.concatenate([turned[lag, 0:HALO], turned[lag, rows - HALO : rows]], axis=0)
            left = left.reshape(2 * strip, sensors)
            term = jnp.dot(left, pairs[step + lag + 1], preferred_element_type=jnp.float32)
            acc = term if acc is None else acc + term
        for side in range(2):
            part = acc[:, side * width : (side + 1) * width]
            field[step + side] = part.reshape(2 * HALO, cols, width)
            at = (step + side) * strip
            head[at : at + strip, :] = part[0:strip].astype(head.dtype)
            tail[at : at + strip, :] = part[strip:].astype(tail.dtype)


def outer(twin, mine, other, turned):
    steps, rows, cols, sensors = turned.shape
    width = mine.shape[2]
    edge = bf16(steps * HALO * cols, width)
    return call(
        outer_kernel,
        "outer",
        (f32(steps, 2 * HALO, cols, width), edge, edge),
        [SMEM] + [VMEM] * 3,
        [VMEM] * 3,
        [pltpu.VMEM((steps + 1, sensors, 2 * width), jnp.bfloat16)],
        24,
        4,
    )(twin, mine, other, turned)


def inner_kernel(
    twin, mine, other, turned, field, diag, couple, ctop, cbottom, edges, scaled, out, mix, pairs, core, line, wide
):
    steps, rows, cols, sensors = turned.shape
    width = mine.shape[2]
    inner = rows - 2 * HALO
    pack_at = pl.program_id(0)

    @pl.when(pack_at == 0)
    def _():
        fill_pairs(twin, mine, other, pairs)
        spread((diag, couple), (ctop, cbottom), line, wide)
        mix_coefs(wide, mix)
        for step in range(0, steps, 2):
            acc = None
            for lag in range(steps - step):
                left = turned[lag, HALO : rows - HALO].reshape(inner * cols, sensors)
                term = jnp.dot(left, pairs[step + lag + 1], preferred_element_type=jnp.float32)
                acc = term if acc is None else acc + term
            for side in range(2):
                core[step + side] = acc[:, side * width : (side + 1) * width].reshape(inner, cols, width)

    listed = edge_rows(rows)
    span = out.shape[0]

    @pl.loop(0, span)
    def _(at):
        step = pack_at * span + at

        def load(row):
            return field[step, listed.index(row)] if row in listed else core[step, row - HALO]

        def store(row, value, weighted):
            if row in listed:
                edges[step, listed.index(row)] = value
            else:
                out[at, row - HALO] = value
            if row == 0:
                scaled[step, 0] = weighted[0]
            if row == rows - 1:
                scaled[step, 1] = weighted[rows - 1]

        own_sweeps(load, wide, rows, store)


def inner(twin, mine, other, turned, field, diag, couple, ctop, cbottom):
    steps, rows, cols, sensors = turned.shape
    width = mine.shape[2]
    core = rows - 2 * HALO
    assert core == HALO
    span = steps // 2
    return call(
        inner_kernel,
        "inner",
        (
            f32(steps, 2 * HALO, cols, width),
            f32(steps, 2, cols, width),
            f32(steps, rows, cols, width),
            f32(2, 8, cols, width),
        ),
        [SMEM] + [VMEM] * 8,
        [VMEM, VMEM, pl.BlockSpec((span, core, cols, width), lambda step: (step, 1, 0, 0)), VMEM],
        [
            pltpu.VMEM((steps + 1, sensors, 2 * width), jnp.bfloat16),
            pltpu.VMEM((steps, core, cols, width), jnp.float32),
        ]
        + coef_scratch(rows + 2 * HALO, cols, width),
        30,
        10,
        (steps // span,),
    )(twin, mine, other, turned, field, diag, couple, ctop, cbottom)


def finish_kernel(side, message, mix, edges, scaled, _, out):
    span, _, cols, _ = out.shape
    first = pl.program_id(0) * span

    @pl.loop(0, span)
    def _(at):
        step = first + at
        added = halo_part(message, step * (HALO * cols), scaled[step, side], mix, side)
        for spot, extra in zip(spots_of(side), added):
            out[at, spot % HALO] = edges[step, spot] + extra


def finish(side, message, mix, edges, scaled, out):
    steps, rows, cols, width = out.shape
    span = steps // 2
    place = side * (rows // HALO - 1)
    return call(
        functools.partial(finish_kernel, side),
        "finish",
        f32(*out.shape),
        [VMEM] * 4 + [HBM],
        pl.BlockSpec((span, HALO, cols, width), lambda step: (step, place, 0, 0)),
        [],
        16,
        2,
        (steps // span,),
        {4: 0},
    )(message, mix, edges, scaled, out)


def from_neighbours(head, tail):
    count = lax.axis_size("tile")
    down = [(i, i + 1) for i in range(count - 1)]
    up = [(i + 1, i) for i in range(count - 1)]
    return lax.ppermute(tail, "tile", down), lax.ppermute(head, "tile", up)


def swap_twins(value):
    return lax.ppermute(value, "twin", [(0, 1), (1, 0)])


def body(sketch, diag_coef, couple, kernel, noise_prec):
    steps, _, rows, cols, width = sketch.shape
    sensors = kernel.shape[1]
    others = ("pair", "tile")
    groups = lax.axis_size(others)
    twin = lax.axis_index("twin")
    which = twin.reshape(1)
    field = sketch.reshape(steps, rows, cols, width)
    diag, couple = diag_coef.reshape(rows, cols), couple.reshape(rows, cols)
    kern = jnp.transpose(kernel.reshape(steps, sensors, rows, cols), (0, 2, 1, 3))
    kept = sensors // 2
    span = steps // PARTS
    share = span * kept // groups

    heads, tails = pack(field)
    halos = [from_neighbours(head, tail) for head, tail in zip(heads, tails)]
    coefs = jnp.stack([diag, couple])
    note = from_neighbours(coefs[:, :HALO], coefs[:, rows - HALO :])
    edges, scaled, data = before(field, diag, couple, kern)
    turned = turn(kern)

    noise = lax.dynamic_slice(noise_prec, (0, twin * kept), (steps, kept)).reshape(PARTS, span * kept)
    start = lax.axis_index(others) * share
    prec = [
        jnp.broadcast_to(lax.dynamic_slice(noise[part], (start,), (share,))[:, None], (share, width))
        for part in range(PARTS)
    ]

    past, copies = turned, []
    for part in range(PARTS):
        mine, other, past = forward(part, which, *halos[part], diag, couple, *note, edges, scaled, kern, data, past)
        both = join(mine, swap_twins(other)).reshape(groups, share, width)
        pieces = lax.all_to_all(both, others, 0, 0, tiled=True)
        copies.append(scale(pieces, prec[part]))

    sent = copies[0] if PARTS == 1 else jnp.concatenate(copies, axis=1)
    weighted = lax.all_to_all(sent, others, 0, 0, tiled=True)
    if PARTS > 1:
        weighted = jnp.swapaxes(weighted.reshape(groups, PARTS, share, width), 0, 1)
    weighted = weighted.reshape(steps, kept, width)
    other = swap_twins(weighted)
    field, head, tail = outer(which, weighted, other, turned)
    top, bottom = from_neighbours(head, tail)
    edges, scaled, out, mix = inner(which, weighted, other, turned, field, diag, couple, *note)
    out = finish(0, top, mix, edges, scaled, out)
    out = finish(1, bottom, mix, edges, scaled, out)
    return out.reshape(sketch.shape)


def solution(mesh):
    bands, tiles = mesh.shape["band"], mesh.shape["tile"]
    fine = Mesh(mesh.devices.reshape(bands // 2, 2, tiles), ("pair", "twin", "tile"))
    band = ("pair", "twin")
    placed = (
        P(None, band, "tile", None, None),
        P(band, "tile", None),
        P(band, "tile", None),
        P(None, None, band, "tile", None),
        P(),
    )
    return jax.shard_map(
        body,
        mesh=fine,
        in_specs=placed,
        out_specs=P(None, band, "tile", None, None),
        check_vma=False,
    )
```

```python
import functools

import jax
import jax.numpy as jnp
from jax import lax
from jax.experimental import pallas as pl
from jax.experimental.pallas import tpu as pltpu
from jax.sharding import Mesh
from jax.sharding import PartitionSpec as P

MIB = 1 << 20
HALO = 2
VMEM = pl.BlockSpec(memory_space=pltpu.VMEM)
SMEM = pl.BlockSpec(memory_space=pltpu.SMEM)
HBM = pl.BlockSpec(memory_space=pltpu.HBM)


def call(kernel, name, out_shape, in_specs, out_specs, scratch, limit, moved, grid=(), aliases={}):
    return pl.pallas_call(
        kernel,
        grid=grid,
        out_shape=out_shape,
        in_specs=in_specs,
        out_specs=out_specs,
        scratch_shapes=scratch,
        input_output_aliases=aliases,
        compiler_params=pltpu.CompilerParams(vmem_limit_bytes=limit * MIB),
        cost_estimate=pl.CostEstimate(flops=0, bytes_accessed=moved * MIB, transcendentals=0),
        name=name,
    )


def f32(*shape):
    return jax.ShapeDtypeStruct(shape, jnp.float32)


def bf16(*shape):
    return jax.ShapeDtypeStruct(shape, jnp.bfloat16)


def edge_rows(rows):
    return [*range(HALO), *range(rows - HALO, rows)]


def beside(w):
    cols = w.shape[0]
    at = lax.broadcasted_iota(jnp.int32, w.shape, 0)
    before = jnp.where(at == 0, 0.0, pltpu.roll(w, 1, 0))
    after = jnp.where(at == cols - 1, 0.0, pltpu.roll(w, cols - 1, 0))
    return before + after


def spread(own, halos, line, wide):
    rows, cols = own[0].shape
    for which in range(2):
        line[...] = jnp.zeros(line.shape, line.dtype)
        for side, halo in enumerate(halos):
            at = side * (HALO + rows)
            line[at : at + HALO, :] = halo[which]
        line[HALO : HALO + rows, :] = own[which][...]
        turned = line[...].T
        for row in range(rows + 2 * HALO):
            wide[which, row] = jnp.broadcast_to(turned[:, row : row + 1], wide.shape[2:])


def mix_coefs(wide, mix):
    total = wide.shape[1]
    for side in range(2):
        far, near, edge, inner = (row if side == 0 else total - 1 - row for row in range(4))
        square = wide[1, edge] * wide[1, edge]
        mix[side, 0] = wide[1, near]
        mix[side, 1] = wide[1, far]
        mix[side, 2] = wide[1, near] * wide[0, near]
        mix[side, 3] = wide[1, near] * wide[1, near]
        mix[side, 4] = -square
        mix[side, 5] = -wide[0, edge] * wide[1, edge]
        mix[side, 6] = wide[1, edge]
        mix[side, 7] = wide[1, inner] * square


def coef_scratch(rows, cols, width):
    return [pltpu.VMEM((cols, cols), jnp.float32), pltpu.VMEM((2, rows, cols, width), jnp.float32)]


def one_sweep(values, scaled, wide, row):
    around = beside(scaled[row])
    if row > 0:
        around = around + scaled[row - 1]
    if row + 1 < len(scaled):
        around = around + scaled[row + 1]
    return wide[0, row + HALO] * values[row] - wide[1, row + HALO] * around


def own_sweeps(load, wide, rows, store):
    values, scaled, first, second = ([None] * rows for _ in range(4))
    for row in range(rows + 2):
        if row < rows:
            values[row] = load(row)
            scaled[row] = wide[1, row + HALO] * values[row]
        if 0 < row <= rows:
            first[row - 1] = one_sweep(values, scaled, wide, row - 1)
            second[row - 1] = wide[1, row - 1 + HALO] * first[row - 1]
        if row > 1:
            store(row - 2, one_sweep(first, second, wide, row - 2), scaled)


def halo_part(message, at, edge_scaled, mix, side):
    cols = edge_scaled.shape[0]
    far_row, near_row = (0, 1) if side == 0 else (1, 0)

    def take(row):
        start = pl.multiple_of(at + row * cols, cols)
        return message[pl.ds(start, cols), :].astype(jnp.float32)

    near = take(near_row)
    scaled = mix[side, 0] * near
    around = mix[side, 1] * take(far_row) + edge_scaled + beside(scaled)
    near_second = mix[side, 2] * near - mix[side, 3] * around
    second = mix[side, 4] * scaled
    on_edge = mix[side, 5] * scaled - mix[side, 6] * (near_second + beside(second))
    return on_edge, mix[side, 7] * scaled


def spots_of(side):
    return (0, 1) if side == 0 else (2 * HALO - 1, 2 * HALO - 2)


def pack_kernel(field, head, tail, edges, packed, arrived, left):
    steps, rows, cols, _ = field.shape
    strip = HALO * cols
    sides = ((0, head), (rows - HALO, tail))
    coming, going = [], []
    for step in range(steps):
        for side, (first, out) in enumerate(sides):
            source = field.at[step, pl.ds(first, HALO)]
            coming.append(pltpu.make_async_copy(source, edges.at[side, step], arrived.at[side, step]))
            target = out.at[pl.ds(step * strip, strip)]
            going.append(pltpu.make_async_copy(packed.at[side, step], target, left.at[side, step]))
    for copy in coming:
        copy.start()
    for at, (copy, out) in enumerate(zip(coming, going)):
        step, side = divmod(at, len(sides))
        copy.wait()
        for row in range(HALO):
            packed[side, step, row * cols : (row + 1) * cols, :] = edges[side, step, row].astype(packed.dtype)
        out.start()
    for copy in going:
        copy.wait()


def pack(field):
    steps, rows, cols, width = field.shape
    size = steps * HALO * cols
    return call(
        pack_kernel,
        "pack",
        [bf16(size, width)] * 2,
        [HBM],
        [HBM] * 2,
        [
            pltpu.VMEM((2, steps, HALO, cols, width), jnp.float32),
            pltpu.VMEM((2, steps, HALO * cols, width), jnp.bfloat16),
            pltpu.SemaphoreType.DMA((2, steps)),
            pltpu.SemaphoreType.DMA((2, steps)),
        ],
        62,
        3,
    )(field)


def before_kernel(field, diag, couple, kern, edges, scaled, data, line, wide, pairs):
    steps, rows, cols, width = field.shape
    inner = rows - 2 * HALO
    listed = edge_rows(rows)
    spread((diag, couple), (), line, wide)
    pairs[0, :, 0:width] = jnp.zeros((inner * cols, width), pairs.dtype)

    @pl.loop(0, steps)
    def _(step):
        def store(row, value, weighted):
            if row in listed:
                edges[step, listed.index(row)] = value
            else:
                at = (row - HALO) * cols
                rounded = value.astype(pairs.dtype)
                pairs[step, at : at + cols, width : 2 * width] = rounded
                pairs[step + 1, at : at + cols, 0:width] = rounded
            if row == 0:
                scaled[step, 0] = weighted[0]
            if row == rows - 1:
                scaled[step, 1] = weighted[rows - 1]

        own_sweeps(lambda row: field[step, row], wide, rows, store)

    for step in range(0, steps, 2):
        acc = None
        for lag in range(step + 2):
            left = jnp.concatenate([kern[lag, row] for row in range(HALO, rows - HALO)], axis=1)
            term = jnp.dot(left, pairs[step + 1 - lag], preferred_element_type=jnp.float32)
            acc = term if acc is None else acc + term
        data[step] = acc[:, 0:width]
        data[step + 1] = acc[:, width : 2 * width]


def before(field, diag, couple, kern):
    steps, rows, cols, width = field.shape
    sensors = kern.shape[2]
    inner = (rows - 2 * HALO) * cols
    return call(
        before_kernel,
        "before",
        (f32(steps, 2 * HALO, cols, width), f32(steps, 2, cols, width), f32(steps, sensors, width)),
        [VMEM] * 4,
        [VMEM] * 3,
        coef_scratch(rows + 2 * HALO, cols, width) + [pltpu.VMEM((steps + 1, inner, 2 * width), jnp.bfloat16)],
        8,
        12,
    )(field, diag, couple, kern)


def edge_product(half, pairs, kern, start, out):
    steps, rows, sensors, _ = kern.shape
    width = out.shape[2]
    kept = sensors // 2
    span = pl.ds(pl.multiple_of(half * kept, kept), kept)
    for step in range(0, steps, 2):
        acc = jnp.concatenate([start[step, span, :], start[step + 1, span, :]], axis=1)
        for lag in range(step + 2):
            left = jnp.concatenate([kern[lag, row, span, :] for row in edge_rows(rows)], axis=1)
            acc = acc + jnp.dot(left, pairs[step + 1 - lag], preferred_element_type=jnp.float32)
        out[step] = acc[:, 0:width].astype(out.dtype)
        out[step + 1] = acc[:, width : 2 * width].astype(out.dtype)


def leaving_kernel(
    twin, top, bottom, diag, couple, ctop, cbottom, edges, scaled, kern, start, _, __, out, pairs, line, wide, mix
):
    steps = kern.shape[0]
    cols, width = edges.shape[2], edges.shape[3]
    spread((diag, couple), (ctop, cbottom), line, wide)
    mix_coefs(wide, mix)
    pairs[0, :, 0:width] = jnp.zeros((2 * HALO * cols, width), pairs.dtype)

    @pl.loop(0, steps)
    def _(step):
        for side, message in enumerate((top, bottom)):
            added = halo_part(message, step * (HALO * cols), scaled[step, side], mix, side)
            for spot, extra in zip(spots_of(side), added):
                rounded = (edges[step, spot] + extra).astype(pairs.dtype)
                at = spot * cols
                pairs[step, at : at + cols, width : 2 * width] = rounded
                pairs[step + 1, at : at + cols, 0:width] = rounded

    edge_product(1 - twin[0], pairs, kern, start, out)


def leaving(twin, top, bottom, diag, couple, ctop, cbottom, edges, scaled, kern, start, *after):
    steps, rows, sensors, cols = kern.shape
    width = edges.shape[3]
    return call(
        leaving_kernel,
        "leaving",
        [bf16(steps, sensors // 2, width), bf16(steps + 1, 2 * HALO * cols, 2 * width)],
        [SMEM] + [VMEM] * 10 + [HBM] * 2,
        [VMEM] * 2,
        coef_scratch(rows + 2 * HALO, cols, width) + [pltpu.VMEM((2, 8, cols, width), jnp.float32)],
        12,
        1,
    )(twin, top, bottom, diag, couple, ctop, cbottom, edges, scaled, kern, start, *after)


def staying_kernel(twin, pairs, kern, start, out):
    edge_product(twin[0], pairs, kern, start, out)


def staying(twin, pairs, kern, start):
    steps, sensors, width = start.shape
    out = f32(steps, sensors // 2, width)
    return call(staying_kernel, "staying", out, [SMEM] + [VMEM] * 3, VMEM, [], 8, 1)(twin, pairs, kern, start)


def join_kernel(mine, got, both):
    both[...] = (mine[...] + got[...].astype(jnp.float32)).astype(both.dtype)


def join(mine, got):
    return call(join_kernel, "join", bf16(*got.shape), [VMEM] * 2, VMEM, [], 4, 1)(mine, got)


def scale_kernel(pieces, prec, out):
    total = pieces[0].astype(jnp.float32)
    for piece in range(1, pieces.shape[0]):
        total = total + pieces[piece].astype(jnp.float32)
    weighted = (total * prec[...]).astype(out.dtype)
    for piece in range(pieces.shape[0]):
        out[piece] = weighted


def scale(pieces, prec):
    return call(scale_kernel, "scale", bf16(*pieces.shape), [VMEM] * 2, VMEM, [], 4, 1)(pieces, prec)


def turn_kernel(kern, turned):
    for row in range(kern.shape[1]):
        turned[0, row] = kern[0, row].T


def turn(kern):
    steps, rows, sensors, cols = kern.shape
    return call(
        turn_kernel,
        "turn",
        bf16(steps, rows, cols, sensors),
        [pl.BlockSpec((1, rows, sensors, cols), lambda lag: (lag, 0, 0, 0))],
        pl.BlockSpec((1, rows, cols, sensors), lambda lag: (lag, 0, 0, 0)),
        [],
        8,
        6,
        (steps,),
    )(kern)


def fill_pairs(twin, mine, other, pairs):
    steps, kept, width = mine.shape
    pairs[steps, :, width : 2 * width] = jnp.zeros((2 * kept, width), pairs.dtype)
    for source, half in ((mine, twin[0]), (other, 1 - twin[0])):
        at = pl.ds(pl.multiple_of(half * kept, kept), kept)
        for step in range(steps):
            pairs[step + 1, at, 0:width] = source[step]
            pairs[step, at, width : 2 * width] = source[step]


def outer_kernel(twin, mine, other, turned, field, head, tail, pairs):
    steps, rows, cols, sensors = turned.shape
    width = mine.shape[2]
    fill_pairs(twin, mine, other, pairs)
    strip = HALO * cols
    for step in range(0, steps, 2):
        acc = None
        for lag in range(steps - step):
            left = jnp.concatenate([turned[lag, 0:HALO], turned[lag, rows - HALO : rows]], axis=0)
            left = left.reshape(2 * strip, sensors)
            term = jnp.dot(left, pairs[step + lag + 1], preferred_element_type=jnp.float32)
            acc = term if acc is None else acc + term
        for side in range(2):
            part = acc[:, side * width : (side + 1) * width]
            field[step + side] = part.reshape(2 * HALO, cols, width)
            at = (step + side) * strip
            head[at : at + strip, :] = part[0:strip].astype(head.dtype)
            tail[at : at + strip, :] = part[strip:].astype(tail.dtype)


def outer(twin, mine, other, turned):
    steps, rows, cols, sensors = turned.shape
    width = mine.shape[2]
    edge = bf16(steps * HALO * cols, width)
    return call(
        outer_kernel,
        "outer",
        (f32(steps, 2 * HALO, cols, width), edge, edge),
        [SMEM] + [VMEM] * 3,
        [VMEM] * 3,
        [pltpu.VMEM((steps + 1, sensors, 2 * width), jnp.bfloat16)],
        8,
        4,
    )(twin, mine, other, turned)


def inner_kernel(
    twin, mine, other, turned, field, diag, couple, ctop, cbottom, edges, scaled, out, mix, pairs, core, line, wide
):
    steps, rows, cols, sensors = turned.shape
    width = mine.shape[2]
    inner = rows - 2 * HALO
    pack_at = pl.program_id(0)

    @pl.when(pack_at == 0)
    def _():
        fill_pairs(twin, mine, other, pairs)
        spread((diag, couple), (ctop, cbottom), line, wide)
        mix_coefs(wide, mix)
        for step in range(0, steps, 2):
            acc = None
            for lag in range(steps - step):
                left = turned[lag, HALO : rows - HALO].reshape(inner * cols, sensors)
                term = jnp.dot(left, pairs[step + lag + 1], preferred_element_type=jnp.float32)
                acc = term if acc is None else acc + term
            for side in range(2):
                core[step + side] = acc[:, side * width : (side + 1) * width].reshape(inner, cols, width)

    listed = edge_rows(rows)
    span = out.shape[0]

    @pl.loop(0, span)
    def _(at):
        step = pack_at * span + at

        def load(row):
            return field[step, listed.index(row)] if row in listed else core[step, row - HALO]

        def store(row, value, weighted):
            if row in listed:
                edges[step, listed.index(row)] = value
            else:
                out[at, row - HALO] = value
            if row == 0:
                scaled[step, 0] = weighted[0]
            if row == rows - 1:
                scaled[step, 1] = weighted[rows - 1]

        own_sweeps(load, wide, rows, store)


def inner(twin, mine, other, turned, field, diag, couple, ctop, cbottom):
    steps, rows, cols, sensors = turned.shape
    width = mine.shape[2]
    core = rows - 2 * HALO
    assert core == HALO
    span = steps // 2
    return call(
        inner_kernel,
        "inner",
        (
            f32(steps, 2 * HALO, cols, width),
            f32(steps, 2, cols, width),
            f32(steps, rows, cols, width),
            f32(2, 8, cols, width),
        ),
        [SMEM] + [VMEM] * 8,
        [VMEM, VMEM, pl.BlockSpec((span, core, cols, width), lambda step: (step, 1, 0, 0)), VMEM],
        [
            pltpu.VMEM((steps + 1, sensors, 2 * width), jnp.bfloat16),
            pltpu.VMEM((steps, core, cols, width), jnp.float32),
        ]
        + coef_scratch(rows + 2 * HALO, cols, width),
        12,
        10,
        (steps // span,),
    )(twin, mine, other, turned, field, diag, couple, ctop, cbottom)


def finish_kernel(side, message, mix, edges, scaled, _, out):
    span, _, cols, _ = out.shape
    first = pl.program_id(0) * span

    @pl.loop(0, span)
    def _(at):
        step = first + at
        added = halo_part(message, step * (HALO * cols), scaled[step, side], mix, side)
        for spot, extra in zip(spots_of(side), added):
            out[at, spot % HALO] = edges[step, spot] + extra


def finish(side, message, mix, edges, scaled, out):
    steps, rows, cols, width = out.shape
    span = steps // 2
    place = side * (rows // HALO - 1)
    return call(
        functools.partial(finish_kernel, side),
        "finish",
        f32(*out.shape),
        [VMEM] * 4 + [HBM],
        pl.BlockSpec((span, HALO, cols, width), lambda step: (step, place, 0, 0)),
        [],
        4,
        2,
        (steps // span,),
        {4: 0},
    )(message, mix, edges, scaled, out)


def from_neighbours(head, tail):
    count = lax.axis_size("tile")
    down = [(i, i + 1) for i in range(count - 1)]
    up = [(i + 1, i) for i in range(count - 1)]
    return lax.ppermute(tail, "tile", down), lax.ppermute(head, "tile", up)


def swap_twins(value):
    return lax.ppermute(value, "twin", [(0, 1), (1, 0)])


def body(sketch, diag_coef, couple, kernel, noise_prec):
    steps, _, rows, cols, width = sketch.shape
    sensors = kernel.shape[1]
    others = ("pair", "tile")
    groups = lax.axis_size(others)
    twin = lax.axis_index("twin")
    which = twin.reshape(1)
    field = sketch.reshape(steps, rows, cols, width)
    diag, couple = diag_coef.reshape(rows, cols), couple.reshape(rows, cols)
    kern = jnp.transpose(kernel.reshape(steps, sensors, rows, cols), (0, 2, 1, 3))
    kept = sensors // 2
    share = steps * kept // groups

    halo = from_neighbours(*pack(field))
    coefs = jnp.stack([diag, couple])
    note = from_neighbours(coefs[:, :HALO], coefs[:, rows - HALO :])
    edges, scaled, data = before(field, diag, couple, kern)
    turned = turn(kern)

    noise = lax.dynamic_slice(noise_prec, (0, twin * kept), (steps, kept)).reshape(steps * kept)
    noise = lax.dynamic_slice(noise, (lax.axis_index(others) * share,), (share,))
    prec = jnp.broadcast_to(noise[:, None], (share, width))

    gone, pairs = leaving(which, *halo, diag, couple, *note, edges, scaled, kern, data, turned, prec)
    both = join(staying(which, pairs, kern, data), swap_twins(gone)).reshape(groups, share, width)
    pieces = lax.all_to_all(both, others, 0, 0, tiled=True)
    weighted = lax.all_to_all(scale(pieces, prec), others, 0, 0, tiled=True).reshape(steps, kept, width)
    other = swap_twins(weighted)
    field, head, tail = outer(which, weighted, other, turned)
    top, bottom = from_neighbours(head, tail)
    edges, scaled, out, mix = inner(which, weighted, other, turned, field, diag, couple, *note)
    out = finish(0, top, mix, edges, scaled, out)
    out = finish(1, bottom, mix, edges, scaled, out)
    return out.reshape(sketch.shape)


def solution(mesh):
    bands, tiles = mesh.shape["band"], mesh.shape["tile"]
    fine = Mesh(mesh.devices.reshape(bands // 2, 2, tiles), ("pair", "twin", "tile"))
    band = ("pair", "twin")
    placed = (
        P(None, band, "tile", None, None),
        P(band, "tile", None),
        P(band, "tile", None),
        P(None, None, band, "tile", None),
        P(),
    )
    return jax.shard_map(
        body,
        mesh=fine,
        in_specs=placed,
        out_specs=P(None, band, "tile", None, None),
        check_vma=False,
    )
```

```python
import functools

import jax
import jax.numpy as jnp
from jax import lax
from jax.experimental import pallas as pl
from jax.experimental.pallas import tpu as pltpu
from jax.sharding import Mesh
from jax.sharding import PartitionSpec as P

MIB = 1 << 20
HALO = 2
VMEM = pl.BlockSpec(memory_space=pltpu.VMEM)
SMEM = pl.BlockSpec(memory_space=pltpu.SMEM)
HBM = pl.BlockSpec(memory_space=pltpu.HBM)


def call(kernel, name, out_shape, in_specs, out_specs, scratch, moved, grid=(), aliases={}, limit=16):
    return pl.pallas_call(
        kernel,
        grid=grid,
        out_shape=out_shape,
        in_specs=in_specs,
        out_specs=out_specs,
        scratch_shapes=scratch,
        input_output_aliases=aliases,
        compiler_params=pltpu.CompilerParams(vmem_limit_bytes=limit * MIB),
        cost_estimate=pl.CostEstimate(flops=0, bytes_accessed=moved * MIB, transcendentals=0),
        name=name,
    )


def f32(*shape):
    return jax.ShapeDtypeStruct(shape, jnp.float32)


def bf16(*shape):
    return jax.ShapeDtypeStruct(shape, jnp.bfloat16)


def edge_rows(rows):
    return [*range(HALO), *range(rows - HALO, rows)]


def beside(w):
    cols = w.shape[0]
    at = lax.broadcasted_iota(jnp.int32, w.shape, 0)
    before = jnp.where(at == 0, 0.0, pltpu.roll(w, 1, 0))
    after = jnp.where(at == cols - 1, 0.0, pltpu.roll(w, cols - 1, 0))
    return before + after


def spread(own, halos, line, wide):
    rows, cols = own[0].shape
    for which in range(2):
        line[...] = jnp.zeros(line.shape, line.dtype)
        for side, halo in enumerate(halos):
            at = side * (HALO + rows)
            line[at : at + HALO, :] = halo[which]
        line[HALO : HALO + rows, :] = own[which][...]
        turned = line[...].T
        for row in range(rows + 2 * HALO):
            wide[which, row] = jnp.broadcast_to(turned[:, row : row + 1], wide.shape[2:])


def mix_coefs(wide, mix):
    total = wide.shape[1]
    for side in range(2):
        far, near, edge, inner = (row if side == 0 else total - 1 - row for row in range(4))
        square = wide[1, edge] * wide[1, edge]
        mix[side, 0] = wide[1, near]
        mix[side, 1] = wide[1, far]
        mix[side, 2] = wide[1, near] * wide[0, near]
        mix[side, 3] = wide[1, near] * wide[1, near]
        mix[side, 4] = -square
        mix[side, 5] = -wide[0, edge] * wide[1, edge]
        mix[side, 6] = wide[1, edge]
        mix[side, 7] = wide[1, inner] * square


def coef_scratch(rows, cols, width):
    return [pltpu.VMEM((cols, cols), jnp.float32), pltpu.VMEM((2, rows, cols, width), jnp.float32)]


def one_sweep(values, scaled, wide, row):
    around = beside(scaled[row])
    if row > 0:
        around = around + scaled[row - 1]
    if row + 1 < len(scaled):
        around = around + scaled[row + 1]
    return wide[0, row + HALO] * values[row] - wide[1, row + HALO] * around


def own_sweeps(load, wide, rows, store):
    values, scaled, first, second = ([None] * rows for _ in range(4))
    for row in range(rows + 2):
        if row < rows:
            values[row] = load(row)
            scaled[row] = wide[1, row + HALO] * values[row]
        if 0 < row <= rows:
            first[row - 1] = one_sweep(values, scaled, wide, row - 1)
            second[row - 1] = wide[1, row - 1 + HALO] * first[row - 1]
        if row > 1:
            store(row - 2, one_sweep(first, second, wide, row - 2), scaled)


def halo_part(message, at, edge_scaled, mix, side):
    cols = edge_scaled.shape[0]
    far_row, near_row = (0, 1) if side == 0 else (1, 0)

    def take(row):
        start = pl.multiple_of(at + row * cols, cols)
        return message[pl.ds(start, cols), :].astype(jnp.float32)

    near = take(near_row)
    scaled = mix[side, 0] * near
    around = mix[side, 1] * take(far_row) + edge_scaled + beside(scaled)
    near_second = mix[side, 2] * near - mix[side, 3] * around
    second = mix[side, 4] * scaled
    on_edge = mix[side, 5] * scaled - mix[side, 6] * (near_second + beside(second))
    return on_edge, mix[side, 7] * scaled


def spots_of(side):
    return (0, 1) if side == 0 else (2 * HALO - 1, 2 * HALO - 2)


def pack_kernel(first, field, _, out, edges, packed, arrived, left):
    steps, rows, cols, width = field.shape
    strip = HALO * cols
    coming, going = [], []
    for step in range(steps):
        source = field.at[step, pl.ds(first, HALO)]
        coming.append(pltpu.make_async_copy(source, edges.at[step], arrived.at[step]))
        coming[step].start()
        going.append(pltpu.make_async_copy(packed.at[step], out.at[pl.ds(step * strip, strip)], left.at[step]))
    for step in range(steps):
        coming[step].wait()
        packed[step] = edges[step].reshape(strip, width).astype(packed.dtype)
        going[step].start()
    for copy in going:
        copy.wait()


def pack(first, field, after):
    steps, rows, cols, width = field.shape
    strip = HALO * cols
    return call(
        functools.partial(pack_kernel, first),
        "pack",
        bf16(steps * strip, width),
        [HBM] * 2,
        HBM,
        [
            pltpu.VMEM((steps, HALO, cols, width), jnp.float32),
            pltpu.VMEM((steps, strip, width), jnp.bfloat16),
            pltpu.SemaphoreType.DMA((steps,)),
            pltpu.SemaphoreType.DMA((steps,)),
        ],
        3,
        limit=62,
    )(field, after)


def before_kernel(field, diag, couple, kern, _, edges, scaled, data, turned, outward, line, wide, pairs):
    steps, rows, cols, width = field.shape
    inner = rows - 2 * HALO
    listed = edge_rows(rows)
    spread((diag, couple), (), line, wide)
    pairs[0, :, 0:width] = jnp.zeros((inner * cols, width), pairs.dtype)

    @pl.loop(0, steps)
    def _(step):
        def store(row, value, weighted):
            if row in listed:
                edges[step, listed.index(row)] = value
            else:
                at = (row - HALO) * cols
                rounded = value.astype(pairs.dtype)
                pairs[step, at : at + cols, width : 2 * width] = rounded
                pairs[step + 1, at : at + cols, 0:width] = rounded
            if row == 0:
                scaled[step, 0] = weighted[0]
            if row == rows - 1:
                scaled[step, 1] = weighted[rows - 1]

        own_sweeps(lambda row: field[step, row], wide, rows, store)

    @pl.loop(0, steps)
    def _(lag):
        for row in range(rows):
            turned[lag, row] = kern[lag, row].T
        for spot, row in enumerate(listed):
            outward[lag, :, spot * cols : (spot + 1) * cols] = kern[lag, row]

    for step in range(0, steps, 2):
        acc = None
        for lag in range(step + 2):
            left = jnp.concatenate([kern[lag, row] for row in range(HALO, rows - HALO)], axis=1)
            term = jnp.dot(left, pairs[step + 1 - lag], preferred_element_type=jnp.float32)
            acc = term if acc is None else acc + term
        data[step] = acc[:, 0:width]
        data[step + 1] = acc[:, width : 2 * width]


def before(field, diag, couple, kern, after):
    steps, rows, cols, width = field.shape
    sensors = kern.shape[2]
    inner = (rows - 2 * HALO) * cols
    return call(
        before_kernel,
        "before",
        (
            f32(steps, 2 * HALO, cols, width),
            f32(steps, 2, cols, width),
            f32(steps, sensors, width),
            bf16(steps, rows, cols, sensors),
            bf16(steps, sensors, 2 * HALO * cols),
        ),
        [VMEM] * 4 + [HBM],
        [VMEM] * 5,
        coef_scratch(rows + 2 * HALO, cols, width) + [pltpu.VMEM((steps + 1, inner, 2 * width), jnp.bfloat16)],
        12,
    )(field, diag, couple, kern, after)


def edge_product(half, pairs, outward, start, out):
    steps, sensors, _ = outward.shape
    width = out.shape[2]
    kept = sensors // 2
    span = pl.ds(pl.multiple_of(half * kept, kept), kept)
    for step in range(0, steps, 2):
        acc = jnp.concatenate([start[step, span, :], start[step + 1, span, :]], axis=1)
        for lag in range(step + 2):
            left = outward[lag, span, :]
            acc = acc + jnp.dot(left, pairs[step + 1 - lag], preferred_element_type=jnp.float32)
        out[step] = acc[:, 0:width].astype(out.dtype)
        out[step + 1] = acc[:, width : 2 * width].astype(out.dtype)


def leaving_kernel(
    twin, top, bottom, diag, couple, ctop, cbottom, edges, scaled, outward, start, out, pairs, line, wide, mix
):
    steps = outward.shape[0]
    cols, width = edges.shape[2], edges.shape[3]
    spread((diag, couple), (ctop, cbottom), line, wide)
    mix_coefs(wide, mix)
    pairs[0, :, 0:width] = jnp.zeros((2 * HALO * cols, width), pairs.dtype)

    @pl.loop(0, steps)
    def _(step):
        for side, message in enumerate((top, bottom)):
            added = halo_part(message, step * (HALO * cols), scaled[step, side], mix, side)
            for spot, extra in zip(spots_of(side), added):
                rounded = (edges[step, spot] + extra).astype(pairs.dtype)
                at = spot * cols
                pairs[step, at : at + cols, width : 2 * width] = rounded
                pairs[step + 1, at : at + cols, 0:width] = rounded

    edge_product(1 - twin[0], pairs, outward, start, out)


def leaving(twin, top, bottom, diag, couple, ctop, cbottom, edges, scaled, outward, start):
    steps, sensors, _ = outward.shape
    rows, cols = diag.shape
    width = edges.shape[3]
    return call(
        leaving_kernel,
        "leaving",
        [bf16(steps, sensors // 2, width), bf16(steps + 1, 2 * HALO * cols, 2 * width)],
        [SMEM] + [VMEM] * 10,
        [VMEM] * 2,
        coef_scratch(rows + 2 * HALO, cols, width) + [pltpu.VMEM((2, 8, cols, width), jnp.float32)],
        1,
    )(twin, top, bottom, diag, couple, ctop, cbottom, edges, scaled, outward, start)


def staying_kernel(twin, pairs, outward, start, out):
    edge_product(twin[0], pairs, outward, start, out)


def staying(twin, pairs, outward, start):
    steps, sensors, width = start.shape
    out = f32(steps, sensors // 2, width)
    return call(staying_kernel, "staying", out, [SMEM] + [VMEM] * 3, VMEM, [], 1)(twin, pairs, outward, start)


def join_kernel(mine, got, both):
    both[...] = (mine[...] + got[...].astype(jnp.float32)).astype(both.dtype)


def join(mine, got):
    return call(join_kernel, "join", bf16(*got.shape), [VMEM] * 2, VMEM, [], 1)(mine, got)


def scale_kernel(pieces, prec, out):
    total = pieces[0].astype(jnp.float32)
    for piece in range(1, pieces.shape[0]):
        total = total + pieces[piece].astype(jnp.float32)
    weighted = (total * prec[...]).astype(out.dtype)
    for piece in range(pieces.shape[0]):
        out[piece] = weighted


def scale(pieces, prec):
    return call(scale_kernel, "scale", bf16(*pieces.shape), [VMEM] * 2, VMEM, [], 1)(pieces, prec)


def fill_pairs(twin, mine, other, pairs):
    steps, kept, width = mine.shape
    pairs[steps, :, width : 2 * width] = jnp.zeros((2 * kept, width), pairs.dtype)
    for source, half in ((mine, twin[0]), (other, 1 - twin[0])):
        at = pl.ds(pl.multiple_of(half * kept, kept), kept)
        for step in range(steps):
            pairs[step + 1, at, 0:width] = source[step]
            pairs[step, at, width : 2 * width] = source[step]


def strip_product(rows, turned, pairs, field, message):
    steps, _, cols, sensors = turned.shape
    strip = HALO * cols
    width = message.shape[1]
    for step in range(0, steps, 2):
        acc = None
        for lag in range(steps - step):
            left = turned[lag, rows].reshape(strip, sensors)
            term = jnp.dot(left, pairs[step + lag + 1], preferred_element_type=jnp.float32)
            acc = term if acc is None else acc + term
        for side in range(2):
            part = acc[:, side * width : (side + 1) * width]
            field[step + side] = part.reshape(HALO, cols, width)
            at = (step + side) * strip
            message[at : at + strip, :] = part.astype(message.dtype)


def tail_kernel(twin, mine, other, turned, field, message, pairs):
    rows = turned.shape[1]
    fill_pairs(twin, mine, other, pairs)
    strip_product(slice(rows - HALO, rows), turned, pairs, field, message)


def head_kernel(pairs, turned, _, field, message):
    strip_product(slice(0, HALO), turned, pairs, field, message)


def adjoint_tail(twin, mine, other, turned):
    steps, _, cols, sensors = turned.shape
    width = mine.shape[2]
    return call(
        tail_kernel,
        "adjoint_tail",
        (
            f32(steps, HALO, cols, width),
            bf16(steps * HALO * cols, width),
            bf16(steps + 1, sensors, 2 * width),
        ),
        [SMEM] + [VMEM] * 3,
        [VMEM] * 3,
        [],
        4,
    )(twin, mine, other, turned)


def adjoint_head(pairs, turned, after):
    steps, _, cols, _ = turned.shape
    width = pairs.shape[2] // 2
    return call(
        head_kernel,
        "adjoint_head",
        (f32(steps, HALO, cols, width), bf16(steps * HALO * cols, width)),
        [VMEM, VMEM, HBM],
        [VMEM] * 2,
        [],
        4,
    )(pairs, turned, after)


def inner_kernel(
    pairs, turned, upper, lower, diag, couple, ctop, cbottom, edges, scaled, out, mix, core, line, wide
):
    steps, rows, cols, sensors = turned.shape
    width = core.shape[3]
    inner = rows - 2 * HALO
    pack_at = pl.program_id(0)

    @pl.when(pack_at == 0)
    def _():
        spread((diag, couple), (ctop, cbottom), line, wide)
        mix_coefs(wide, mix)
        for step in range(0, steps, 2):
            acc = None
            for lag in range(steps - step):
                left = turned[lag, HALO : rows - HALO].reshape(inner * cols, sensors)
                term = jnp.dot(left, pairs[step + lag + 1], preferred_element_type=jnp.float32)
                acc = term if acc is None else acc + term
            for side in range(2):
                core[step + side] = acc[:, side * width : (side + 1) * width].reshape(inner, cols, width)

    listed = edge_rows(rows)
    span = out.shape[0]

    @pl.loop(0, span)
    def _(at):
        step = pack_at * span + at

        def load(row):
            if row < HALO:
                return upper[step, row]
            return core[step, row - HALO] if row < rows - HALO else lower[step, row - rows + HALO]

        def store(row, value, weighted):
            if row in listed:
                edges[step, listed.index(row)] = value
            else:
                out[at, row - HALO] = value
            if row == 0:
                scaled[step, 0] = weighted[0]
            if row == rows - 1:
                scaled[step, 1] = weighted[rows - 1]

        own_sweeps(load, wide, rows, store)


def inner(pairs, turned, upper, lower, diag, couple, ctop, cbottom):
    steps, rows, cols, _ = turned.shape
    width = upper.shape[3]
    core = rows - 2 * HALO
    assert core == HALO
    span = steps // 2
    return call(
        inner_kernel,
        "inner",
        (
            f32(steps, 2 * HALO, cols, width),
            f32(steps, 2, cols, width),
            f32(steps, rows, cols, width),
            f32(2, 8, cols, width),
        ),
        [VMEM] * 8,
        [VMEM, VMEM, pl.BlockSpec((span, core, cols, width), lambda step: (step, 1, 0, 0)), VMEM],
        [pltpu.VMEM((steps, core, cols, width), jnp.float32)] + coef_scratch(rows + 2 * HALO, cols, width),
        10,
        (steps // span,),
    )(pairs, turned, upper, lower, diag, couple, ctop, cbottom)


def finish_kernel(side, message, mix, edges, scaled, _, out):
    span, _, cols, _ = out.shape
    first = pl.program_id(0) * span

    @pl.loop(0, span)
    def _(at):
        step = first + at
        added = halo_part(message, step * (HALO * cols), scaled[step, side], mix, side)
        for spot, extra in zip(spots_of(side), added):
            out[at, spot % HALO] = edges[step, spot] + extra


def finish(side, message, mix, edges, scaled, out):
    steps, rows, cols, width = out.shape
    span = steps // 2
    place = side * (rows // HALO - 1)
    return call(
        functools.partial(finish_kernel, side),
        "finish",
        f32(*out.shape),
        [VMEM] * 4 + [HBM],
        pl.BlockSpec((span, HALO, cols, width), lambda step: (step, place, 0, 0)),
        [],
        2,
        (steps // span,),
        {4: 0},
    )(message, mix, edges, scaled, out)


def send_down(tail):
    return lax.ppermute(tail, "tile", [(i, i + 1) for i in range(lax.axis_size("tile") - 1)])


def send_up(head):
    return lax.ppermute(head, "tile", [(i + 1, i) for i in range(lax.axis_size("tile") - 1)])


def swap_twins(value):
    return lax.ppermute(value, "twin", [(0, 1), (1, 0)])


def body(sketch, diag_coef, couple, kernel, noise_prec):
    steps, _, rows, cols, width = sketch.shape
    sensors = kernel.shape[1]
    others = ("pair", "tile")
    groups = lax.axis_size(others)
    twin = lax.axis_index("twin")
    which = twin.reshape(1)
    field = sketch.reshape(steps, rows, cols, width)
    diag, couple = diag_coef.reshape(rows, cols), couple.reshape(rows, cols)
    kern = jnp.transpose(kernel.reshape(steps, sensors, rows, cols), (0, 2, 1, 3))
    kept = sensors // 2
    share = steps * kept // groups

    tail = pack(rows - HALO, field, sketch)
    top = send_down(tail)
    bottom = send_up(pack(0, field, tail))
    coefs = jnp.stack([diag, couple])
    note = send_down(coefs[:, rows - HALO :]), send_up(coefs[:, :HALO])
    noise = lax.dynamic_slice(noise_prec, (0, twin * kept), (steps, kept)).reshape(steps * kept)
    noise = lax.dynamic_slice(noise, (lax.axis_index(others) * share,), (share,))
    prec = jnp.broadcast_to(noise[:, None], (share, width))
    edges, scaled, data, turned, outward = before(field, diag, couple, kern, prec)

    gone, pairs = leaving(which, top, bottom, diag, couple, *note, edges, scaled, outward, data)
    both = join(staying(which, pairs, outward, data), swap_twins(gone)).reshape(groups, share, width)
    pieces = lax.all_to_all(both, others, 0, 0, tiled=True)
    weighted = lax.all_to_all(scale(pieces, prec), others, 0, 0, tiled=True).reshape(steps, kept, width)
    lower, tail, pairs = adjoint_tail(which, weighted, swap_twins(weighted), turned)
    top = send_down(tail)
    upper, head = adjoint_head(pairs, turned, tail)
    bottom = send_up(head)
    edges, scaled, out, mix = inner(pairs, turned, upper, lower, diag, couple, *note)
    out = finish(0, top, mix, edges, scaled, out)
    out = finish(1, bottom, mix, edges, scaled, out)
    return out.reshape(sketch.shape)


def solution(mesh):
    bands, tiles = mesh.shape["band"], mesh.shape["tile"]
    fine = Mesh(mesh.devices.reshape(bands // 2, 2, tiles), ("pair", "twin", "tile"))
    band = ("pair", "twin")
    placed = (
        P(None, band, "tile", None, None),
        P(band, "tile", None),
        P(band, "tile", None),
        P(None, None, band, "tile", None),
        P(),
    )
    return jax.shard_map(
        body,
        mesh=fine,
        in_specs=placed,
        out_specs=P(None, band, "tile", None, None),
        check_vma=False,
    )
```

```python
import functools

import jax
import jax.numpy as jnp
from jax import lax
from jax.experimental import pallas as pl
from jax.experimental.pallas import tpu as pltpu
from jax.sharding import Mesh
from jax.sharding import PartitionSpec as P

MIB = 1 << 20
HALO = 2
VMEM = pl.BlockSpec(memory_space=pltpu.VMEM)
SMEM = pl.BlockSpec(memory_space=pltpu.SMEM)
HBM = pl.BlockSpec(memory_space=pltpu.HBM)


def call(kernel, name, out_shape, in_specs, out_specs, scratch, moved, grid=(), aliases={}, limit=16):
    return pl.pallas_call(
        kernel,
        grid=grid,
        out_shape=out_shape,
        in_specs=in_specs,
        out_specs=out_specs,
        scratch_shapes=scratch,
        input_output_aliases=aliases,
        compiler_params=pltpu.CompilerParams(vmem_limit_bytes=limit * MIB),
        cost_estimate=pl.CostEstimate(flops=0, bytes_accessed=moved * MIB, transcendentals=0),
        name=name,
    )


def f32(*shape):
    return jax.ShapeDtypeStruct(shape, jnp.float32)


def bf16(*shape):
    return jax.ShapeDtypeStruct(shape, jnp.bfloat16)


def edge_rows(rows):
    return [*range(HALO), *range(rows - HALO, rows)]


def beside(w):
    cols = w.shape[0]
    at = lax.broadcasted_iota(jnp.int32, w.shape, 0)
    before = jnp.where(at == 0, 0.0, pltpu.roll(w, 1, 0))
    after = jnp.where(at == cols - 1, 0.0, pltpu.roll(w, cols - 1, 0))
    return before + after


def spread(own, halos, line, wide):
    rows, cols = own[0].shape
    for which in range(2):
        line[...] = jnp.zeros(line.shape, line.dtype)
        for side, halo in enumerate(halos):
            at = side * (HALO + rows)
            line[at : at + HALO, :] = halo[which]
        line[HALO : HALO + rows, :] = own[which][...]
        turned = line[...].T
        for row in range(rows + 2 * HALO):
            wide[which, row] = jnp.broadcast_to(turned[:, row : row + 1], wide.shape[2:])


def mix_coefs(wide, mix):
    total = wide.shape[1]
    for side in range(2):
        far, near, edge, inner = (row if side == 0 else total - 1 - row for row in range(4))
        square = wide[1, edge] * wide[1, edge]
        mix[side, 0] = wide[1, near]
        mix[side, 1] = wide[1, far]
        mix[side, 2] = wide[1, near] * wide[0, near]
        mix[side, 3] = wide[1, near] * wide[1, near]
        mix[side, 4] = -square
        mix[side, 5] = -wide[0, edge] * wide[1, edge]
        mix[side, 6] = wide[1, edge]
        mix[side, 7] = wide[1, inner] * square


def coef_scratch(rows, cols, width):
    return [pltpu.VMEM((cols, cols), jnp.float32), pltpu.VMEM((2, rows, cols, width), jnp.float32)]


def one_sweep(values, scaled, wide, row):
    around = beside(scaled[row])
    if row > 0:
        around = around + scaled[row - 1]
    if row + 1 < len(scaled):
        around = around + scaled[row + 1]
    return wide[0, row + HALO] * values[row] - wide[1, row + HALO] * around


def own_sweeps(load, wide, rows, store):
    values, scaled, first, second = ([None] * rows for _ in range(4))
    for row in range(rows + 2):
        if row < rows:
            values[row] = load(row)
            scaled[row] = wide[1, row + HALO] * values[row]
        if 0 < row <= rows:
            first[row - 1] = one_sweep(values, scaled, wide, row - 1)
            second[row - 1] = wide[1, row - 1 + HALO] * first[row - 1]
        if row > 1:
            store(row - 2, one_sweep(first, second, wide, row - 2), scaled)


def halo_part(message, at, edge_scaled, mix, side):
    cols = edge_scaled.shape[0]
    far_row, near_row = (0, 1) if side == 0 else (1, 0)

    def take(row):
        start = pl.multiple_of(at + row * cols, cols)
        return message[pl.ds(start, cols), :].astype(jnp.float32)

    near = take(near_row)
    scaled = mix[side, 0] * near
    around = mix[side, 1] * take(far_row) + edge_scaled + beside(scaled)
    near_second = mix[side, 2] * near - mix[side, 3] * around
    second = mix[side, 4] * scaled
    on_edge = mix[side, 5] * scaled - mix[side, 6] * (near_second + beside(second))
    return on_edge, mix[side, 7] * scaled


def spots_of(side):
    return (0, 1) if side == 0 else (2 * HALO - 1, 2 * HALO - 2)


def pack_kernel(first, field, _, out, edges, packed, arrived, left):
    steps, rows, cols, width = field.shape
    strip = HALO * cols
    coming, going = [], []
    for step in range(steps):
        source = field.at[step, pl.ds(first, HALO)]
        coming.append(pltpu.make_async_copy(source, edges.at[step], arrived.at[step]))
        coming[step].start()
        going.append(pltpu.make_async_copy(packed.at[step], out.at[pl.ds(step * strip, strip)], left.at[step]))
    for step in range(steps):
        coming[step].wait()
        packed[step] = edges[step].reshape(strip, width).astype(packed.dtype)
        going[step].start()
    for copy in going:
        copy.wait()


def pack(first, field, after):
    steps, rows, cols, width = field.shape
    strip = HALO * cols
    return call(
        functools.partial(pack_kernel, first),
        "pack",
        bf16(steps * strip, width),
        [HBM] * 2,
        HBM,
        [
            pltpu.VMEM((steps, HALO, cols, width), jnp.float32),
            pltpu.VMEM((steps, strip, width), jnp.bfloat16),
            pltpu.SemaphoreType.DMA((steps,)),
            pltpu.SemaphoreType.DMA((steps,)),
        ],
        3,
        limit=62,
    )(field, after)


def before_kernel(field, diag, couple, kern, _, edges, scaled, data, turned, outward, line, wide, pairs):
    steps, rows, cols, width = field.shape
    inner = rows - 2 * HALO
    listed = edge_rows(rows)
    spread((diag, couple), (), line, wide)
    pairs[0, :, 0:width] = jnp.zeros((inner * cols, width), pairs.dtype)

    @pl.loop(0, steps)
    def _(step):
        def store(row, value, weighted):
            if row in listed:
                edges[step, listed.index(row)] = value
            else:
                at = (row - HALO) * cols
                rounded = value.astype(pairs.dtype)
                pairs[step, at : at + cols, width : 2 * width] = rounded
                pairs[step + 1, at : at + cols, 0:width] = rounded
            if row == 0:
                scaled[step, 0] = weighted[0]
            if row == rows - 1:
                scaled[step, 1] = weighted[rows - 1]

        own_sweeps(lambda row: field[step, row], wide, rows, store)

    @pl.loop(0, steps)
    def _(lag):
        for row in range(rows):
            turned[lag, row] = kern[lag, row].T
        for spot, row in enumerate(listed):
            outward[lag, :, spot * cols : (spot + 1) * cols] = kern[lag, row]

    for step in range(0, steps, 2):
        acc = None
        for lag in range(step + 2):
            left = jnp.concatenate([kern[lag, row] for row in range(HALO, rows - HALO)], axis=1)
            term = jnp.dot(left, pairs[step + 1 - lag], preferred_element_type=jnp.float32)
            acc = term if acc is None else acc + term
        data[step] = acc[:, 0:width]
        data[step + 1] = acc[:, width : 2 * width]


def before(field, diag, couple, kern, after):
    steps, rows, cols, width = field.shape
    sensors = kern.shape[2]
    inner = (rows - 2 * HALO) * cols
    return call(
        before_kernel,
        "before",
        (
            f32(steps, 2 * HALO, cols, width),
            f32(steps, 2, cols, width),
            f32(steps, sensors, width),
            bf16(steps, rows, cols, sensors),
            bf16(steps, sensors, 2 * HALO * cols),
        ),
        [VMEM] * 4 + [HBM],
        [VMEM] * 5,
        coef_scratch(rows + 2 * HALO, cols, width) + [pltpu.VMEM((steps + 1, inner, 2 * width), jnp.bfloat16)],
        12,
    )(field, diag, couple, kern, after)


def edge_product(half, pairs, outward, start, out):
    steps, sensors, _ = outward.shape
    width = out.shape[2]
    kept = sensors // 2
    span = pl.ds(pl.multiple_of(half * kept, kept), kept)
    for step in range(0, steps, 2):
        acc = jnp.concatenate([start[step, span, :], start[step + 1, span, :]], axis=1)
        for lag in range(step + 2):
            left = outward[lag, span, :]
            acc = acc + jnp.dot(left, pairs[step + 1 - lag], preferred_element_type=jnp.float32)
        out[step] = acc[:, 0:width].astype(out.dtype)
        out[step + 1] = acc[:, width : 2 * width].astype(out.dtype)


def leaving_kernel(
    twin, top, bottom, diag, couple, ctop, cbottom, edges, scaled, outward, start, out, pairs, line, wide, mix
):
    steps = outward.shape[0]
    cols, width = edges.shape[2], edges.shape[3]
    spread((diag, couple), (ctop, cbottom), line, wide)
    mix_coefs(wide, mix)
    pairs[0, :, 0:width] = jnp.zeros((2 * HALO * cols, width), pairs.dtype)

    @pl.loop(0, steps)
    def _(step):
        for side, message in enumerate((top, bottom)):
            added = halo_part(message, step * (HALO * cols), scaled[step, side], mix, side)
            for spot, extra in zip(spots_of(side), added):
                rounded = (edges[step, spot] + extra).astype(pairs.dtype)
                at = spot * cols
                pairs[step, at : at + cols, width : 2 * width] = rounded
                pairs[step + 1, at : at + cols, 0:width] = rounded

    edge_product(1 - twin[0], pairs, outward, start, out)


def leaving(twin, top, bottom, diag, couple, ctop, cbottom, edges, scaled, outward, start):
    steps, sensors, _ = outward.shape
    rows, cols = diag.shape
    width = edges.shape[3]
    return call(
        leaving_kernel,
        "leaving",
        [bf16(steps, sensors // 2, width), bf16(steps + 1, 2 * HALO * cols, 2 * width)],
        [SMEM] + [VMEM] * 10,
        [VMEM] * 2,
        coef_scratch(rows + 2 * HALO, cols, width) + [pltpu.VMEM((2, 8, cols, width), jnp.float32)],
        1,
    )(twin, top, bottom, diag, couple, ctop, cbottom, edges, scaled, outward, start)


def staying_kernel(twin, pairs, outward, start, out):
    edge_product(twin[0], pairs, outward, start, out)


def staying(twin, pairs, outward, start):
    steps, sensors, width = start.shape
    out = f32(steps, sensors // 2, width)
    return call(staying_kernel, "staying", out, [SMEM] + [VMEM] * 3, VMEM, [], 1)(twin, pairs, outward, start)


def join_kernel(parts, mine, got, both):
    steps, kept, width = mine.shape
    groups, share, _ = both.shape
    rows = share // parts
    span = steps // parts
    for step in range(steps):
        total = (mine[step] + got[step].astype(jnp.float32)).astype(both.dtype)
        part, at = divmod(step, span)
        owners = kept // rows
        place = slice(at * owners, (at + 1) * owners), slice(part * rows, (part + 1) * rows)
        both[place] = total.reshape(owners, rows, width)


def join(parts, groups, mine, got):
    steps, kept, width = mine.shape
    out = bf16(groups, steps * kept // groups, width)
    kernel = functools.partial(join_kernel, parts)
    return call(kernel, "join", out, [VMEM] * 2, VMEM, [], 1)(mine, got)


def scale_kernel(pieces, prec, *outs):
    total = pieces[0].astype(jnp.float32)
    for piece in range(1, pieces.shape[0]):
        total = total + pieces[piece].astype(jnp.float32)
    weighted = (total * prec[...]).astype(pieces.dtype)
    rows = outs[0].shape[1]
    for part, out in enumerate(outs):
        for piece in range(pieces.shape[0]):
            out[piece] = weighted[part * rows : (part + 1) * rows]


def scale(parts, pieces, prec):
    groups, share, width = pieces.shape
    shapes = [bf16(groups, share // parts, width)] * parts
    return call(scale_kernel, "scale", shapes, [VMEM] * 2, [VMEM] * parts, [], 1)(pieces, prec)


def fill_pairs(twin, mine, other, pairs, later):
    span, kept, width = mine.shape
    follows = later[0][0, :, 0:width] if later else jnp.zeros((2 * kept, width), pairs.dtype)
    pairs[span - 1, :, width : 2 * width] = follows
    for source, half in ((mine, twin[0]), (other, 1 - twin[0])):
        at = pl.ds(pl.multiple_of(half * kept, kept), kept)
        for step in range(span):
            pairs[step, at, 0:width] = source[step]
            if step:
                pairs[step - 1, at, width : 2 * width] = source[step]


def strip_product(rows, turned, blocks, store):
    steps, _, cols, sensors = turned.shape
    blocks = [block.at[at] for block in blocks for at in range(block.shape[0])]
    first = steps - len(blocks)
    for step in range(first, steps, 2):
        acc = None
        for lag in range(steps - step):
            left = turned[lag, rows].reshape((rows.stop - rows.start) * cols, sensors)
            right = blocks[step + lag - first][...]
            term = jnp.dot(left, right, preferred_element_type=jnp.float32)
            acc = term if acc is None else acc + term
        width = acc.shape[1] // 2
        if not store(step - first, acc[:, 0:width]):
            break
        store(step - first + 1, acc[:, width:])


def strip_store(field, message):
    span, _, cols, width = field.shape
    strip = HALO * cols

    def store(at, part):
        if at >= span:
            return False
        field[at] = part.reshape(HALO, cols, width)
        message[at * strip : (at + 1) * strip, :] = part.astype(message.dtype)
        return True

    return store


def tail_kernel(twin, mine, other, turned, *refs):
    *later, field, message, pairs = refs
    rows = turned.shape[1]
    fill_pairs(twin, mine, other, pairs, later)
    strip_product(slice(rows - HALO, rows), turned, [pairs, *later], strip_store(field, message))


def head_kernel(count, turned, _, *refs):
    field, message = refs[count:]
    strip_product(slice(0, HALO), turned, refs[:count], strip_store(field, message))


def strip_shapes(span, cols, width):
    return [f32(span, HALO, cols, width), bf16(span * HALO * cols, width)]


def adjoint_tail(twin, mine, other, turned, later):
    _, _, cols, sensors = turned.shape
    span, _, width = mine.shape
    return call(
        tail_kernel,
        "adjoint_tail",
        strip_shapes(span, cols, width) + [bf16(span, sensors, 2 * width)],
        [SMEM] + [VMEM] * (3 + len(later)),
        [VMEM] * 3,
        [],
        1,
    )(twin, mine, other, turned, *later)


def adjoint_head(blocks, turned, after):
    cols = turned.shape[2]
    span, _, width = blocks[0].shape
    return call(
        functools.partial(head_kernel, len(blocks)),
        "adjoint_head",
        strip_shapes(span, cols, width // 2),
        [VMEM, HBM] + [VMEM] * len(blocks),
        [VMEM] * 2,
        [],
        1,
    )(turned, after, *blocks)


def inner_kernel(parts, turned, diag, couple, ctop, cbottom, *refs):
    blocks, uppers, lowers = (refs[kind * parts : (kind + 1) * parts] for kind in range(3))
    edges, scaled, out, mix, core, line, wide = refs[3 * parts :]
    steps, rows, cols, _ = turned.shape
    width = core.shape[3]
    inner = rows - 2 * HALO
    listed = edge_rows(rows)
    span = steps // parts

    spread((diag, couple), (ctop, cbottom), line, wide)
    mix_coefs(wide, mix)

    def keep(at, part):
        core[at] = part.reshape(inner, cols, width)
        return True

    strip_product(slice(HALO, rows - HALO), turned, blocks, keep)

    for part in range(parts):

        @pl.loop(0, span)
        def _(at):
            step = part * span + at

            def load(row):
                if row < HALO:
                    return uppers[part][at, row]
                return core[step, row - HALO] if row < rows - HALO else lowers[part][at, row - rows + HALO]

            def store(row, value, weighted):
                if row in listed:
                    edges[step, listed.index(row)] = value
                else:
                    core[step, row - HALO] = value
                if row == 0:
                    scaled[step, 0] = weighted[0]
                if row == rows - 1:
                    scaled[step, 1] = weighted[rows - 1]

            own_sweeps(load, wide, rows, store)

    pltpu.sync_copy(core, out.at[:, pl.ds(HALO, inner)])


def inner(blocks, turned, uppers, lowers, diag, couple, ctop, cbottom):
    steps, rows, cols, _ = turned.shape
    width = uppers[0].shape[3]
    parts = len(blocks)
    return call(
        functools.partial(inner_kernel, parts),
        "inner",
        (
            f32(steps, 2 * HALO, cols, width),
            f32(steps, 2, cols, width),
            f32(steps, rows, cols, width),
            f32(2, 8, cols, width),
        ),
        [VMEM] * (5 + 3 * parts),
        [VMEM, VMEM, HBM, VMEM],
        [pltpu.VMEM((steps, rows - 2 * HALO, cols, width), jnp.float32)] + coef_scratch(rows + 2 * HALO, cols, width),
        8,
    )(turned, diag, couple, ctop, cbottom, *blocks, *uppers, *lowers)


def finish_kernel(side, first, message, mix, edges, scaled, _, out):
    span, _, cols, _ = out.shape
    begin = pl.program_id(0) * span

    @pl.loop(0, span)
    def _(at):
        step = begin + at
        added = halo_part(message, step * (HALO * cols), scaled[first + step, side], mix, side)
        for spot, extra in zip(spots_of(side), added):
            out[at, spot % HALO] = edges[first + step, spot] + extra


def finish(side, first, message, mix, edges, scaled, out):
    steps, rows, cols, width = out.shape
    count = message.shape[0] // (HALO * cols)
    span = count // 2
    place = side * (rows // HALO - 1)
    return call(
        functools.partial(finish_kernel, side, first),
        "finish",
        f32(*out.shape),
        [VMEM] * 4 + [HBM],
        pl.BlockSpec((span, HALO, cols, width), lambda step: (first // span + step, place, 0, 0)),
        [],
        1,
        (count // span,),
        {4: 0},
    )(message, mix, edges, scaled, out)


def send_down(tail):
    return lax.ppermute(tail, "tile", [(i, i + 1) for i in range(lax.axis_size("tile") - 1)])


def send_up(head):
    return lax.ppermute(head, "tile", [(i + 1, i) for i in range(lax.axis_size("tile") - 1)])


def swap_twins(value):
    return lax.ppermute(value, "twin", [(0, 1), (1, 0)])


def body(sketch, diag_coef, couple, kernel, noise_prec):
    steps, _, rows, cols, width = sketch.shape
    sensors = kernel.shape[1]
    others = ("pair", "tile")
    groups = lax.axis_size(others)
    twin = lax.axis_index("twin")
    which = twin.reshape(1)
    field = sketch.reshape(steps, rows, cols, width)
    diag, couple = diag_coef.reshape(rows, cols), couple.reshape(rows, cols)
    kern = jnp.transpose(kernel.reshape(steps, sensors, rows, cols), (0, 2, 1, 3))
    kept = sensors // 2
    share = steps * kept // groups

    tail = pack(rows - HALO, field, sketch)
    top = send_down(tail)
    bottom = send_up(pack(0, field, tail))
    coefs = jnp.stack([diag, couple])
    note = send_down(coefs[:, rows - HALO :]), send_up(coefs[:, :HALO])
    parts = 2 if share % 32 == 0 else 1
    rows_each = share // parts
    noise = lax.dynamic_slice(noise_prec, (0, twin * kept), (steps, kept)).reshape(parts, -1)
    noise = lax.dynamic_slice(noise, (0, lax.axis_index(others) * rows_each), (parts, rows_each)).reshape(share)
    prec = jnp.broadcast_to(noise[:, None], (share, width))
    edges, scaled, data, turned, outward = before(field, diag, couple, kern, prec)

    gone, pairs = leaving(which, top, bottom, diag, couple, *note, edges, scaled, outward, data)
    both = join(parts, groups, staying(which, pairs, outward, data), swap_twins(gone))
    copies = scale(parts, lax.all_to_all(both, others, 0, 0, tiled=True), prec)

    span = steps // parts
    blocks, uppers, lowers, tops, bottoms = [], [], [], [], []
    for part in reversed(range(parts)):
        weighted = lax.all_to_all(copies[part], others, 0, 0, tiled=True).reshape(span, kept, width)
        lower, tail, made = adjoint_tail(which, weighted, swap_twins(weighted), turned, blocks)
        tops.insert(0, send_down(tail))
        blocks.insert(0, made)
        upper, head = adjoint_head(blocks, turned, tail)
        bottoms.insert(0, send_up(head))
        uppers.insert(0, upper)
        lowers.insert(0, lower)

    edges, scaled, out, mix = inner(blocks, turned, uppers, lowers, diag, couple, *note)
    for part in reversed(range(parts)):
        for side, message in enumerate((tops[part], bottoms[part])):
            out = finish(side, part * span, message, mix, edges, scaled, out)
    return out.reshape(sketch.shape)


def solution(mesh):
    bands, tiles = mesh.shape["band"], mesh.shape["tile"]
    fine = Mesh(mesh.devices.reshape(bands // 2, 2, tiles), ("pair", "twin", "tile"))
    band = ("pair", "twin")
    placed = (
        P(None, band, "tile", None, None),
        P(band, "tile", None),
        P(band, "tile", None),
        P(None, None, band, "tile", None),
        P(),
    )
    return jax.shard_map(
        body,
        mesh=fine,
        in_specs=placed,
        out_specs=P(None, band, "tile", None, None),
        check_vma=False,
    )
```

```python
import functools

import jax
import jax.numpy as jnp
from jax import lax
from jax.experimental import pallas as pl
from jax.experimental.pallas import tpu as pltpu
from jax.sharding import Mesh
from jax.sharding import PartitionSpec as P

MIB = 1 << 20
HALO = 2
VMEM = pl.BlockSpec(memory_space=pltpu.VMEM)
SMEM = pl.BlockSpec(memory_space=pltpu.SMEM)
HBM = pl.BlockSpec(memory_space=pltpu.HBM)


def call(kernel, name, out_shape, in_specs, out_specs, scratch, moved, grid=(), aliases={}, limit=16):
    return pl.pallas_call(
        kernel,
        grid=grid,
        out_shape=out_shape,
        in_specs=in_specs,
        out_specs=out_specs,
        scratch_shapes=scratch,
        input_output_aliases=aliases,
        compiler_params=pltpu.CompilerParams(vmem_limit_bytes=limit * MIB),
        cost_estimate=pl.CostEstimate(flops=0, bytes_accessed=int(moved * MIB), transcendentals=0),
        name=name,
    )


def f32(*shape):
    return jax.ShapeDtypeStruct(shape, jnp.float32)


def bf16(*shape):
    return jax.ShapeDtypeStruct(shape, jnp.bfloat16)


def edge_rows(rows):
    return [*range(HALO), *range(rows - HALO, rows)]


def beside(w):
    cols = w.shape[0]
    at = lax.broadcasted_iota(jnp.int32, w.shape, 0)
    before = jnp.where(at == 0, 0.0, pltpu.roll(w, 1, 0))
    after = jnp.where(at == cols - 1, 0.0, pltpu.roll(w, cols - 1, 0))
    return before + after


def spread(own, halos, line, wide):
    rows, cols = own[0].shape
    for which in range(2):
        line[...] = jnp.zeros(line.shape, line.dtype)
        for side, halo in enumerate(halos):
            at = side * (HALO + rows)
            line[at : at + HALO, :] = halo[which]
        line[HALO : HALO + rows, :] = own[which][...]
        turned = line[...].T
        for row in range(rows + 2 * HALO):
            wide[which, row] = jnp.broadcast_to(turned[:, row : row + 1], wide.shape[2:])


def mix_coefs(wide, mix):
    total = wide.shape[1]
    for side in range(2):
        far, near, edge, inner = (row if side == 0 else total - 1 - row for row in range(4))
        square = wide[1, edge] * wide[1, edge]
        mix[side, 0] = wide[1, near]
        mix[side, 1] = wide[1, far]
        mix[side, 2] = wide[1, near] * wide[0, near]
        mix[side, 3] = wide[1, near] * wide[1, near]
        mix[side, 4] = -square
        mix[side, 5] = -wide[0, edge] * wide[1, edge]
        mix[side, 6] = wide[1, edge]
        mix[side, 7] = wide[1, inner] * square


def coef_scratch(rows, cols, width):
    return [pltpu.VMEM((cols, cols), jnp.float32), pltpu.VMEM((2, rows, cols, width), jnp.float32)]


def one_sweep(values, scaled, wide, row):
    around = beside(scaled[row])
    if row > 0:
        around = around + scaled[row - 1]
    if row + 1 < len(scaled):
        around = around + scaled[row + 1]
    return wide[0, row + HALO] * values[row] - wide[1, row + HALO] * around


def own_sweeps(load, wide, rows, store):
    values, scaled, first, second = ([None] * rows for _ in range(4))
    for row in range(rows + 2):
        if row < rows:
            values[row] = load(row)
            scaled[row] = wide[1, row + HALO] * values[row]
        if 0 < row <= rows:
            first[row - 1] = one_sweep(values, scaled, wide, row - 1)
            second[row - 1] = wide[1, row - 1 + HALO] * first[row - 1]
        if row > 1:
            store(row - 2, one_sweep(first, second, wide, row - 2), scaled)


def halo_part(message, at, edge_scaled, mix, side):
    cols = edge_scaled.shape[0]
    far_row, near_row = (0, 1) if side == 0 else (1, 0)

    def take(row):
        start = pl.multiple_of(at + row * cols, cols)
        return message[pl.ds(start, cols), :].astype(jnp.float32)

    near = take(near_row)
    scaled = mix[side, 0] * near
    around = mix[side, 1] * take(far_row) + edge_scaled + beside(scaled)
    near_second = mix[side, 2] * near - mix[side, 3] * around
    second = mix[side, 4] * scaled
    on_edge = mix[side, 5] * scaled - mix[side, 6] * (near_second + beside(second))
    return on_edge, mix[side, 7] * scaled


def spots_of(side):
    return (0, 1) if side == 0 else (2 * HALO - 1, 2 * HALO - 2)


def pack_kernel(first, field, _, out, edges, packed, arrived, left):
    steps, rows, cols, width = field.shape
    strip = HALO * cols
    coming, going = [], []
    for step in range(steps):
        source = field.at[step, pl.ds(first, HALO)]
        coming.append(pltpu.make_async_copy(source, edges.at[step], arrived.at[step]))
        coming[step].start()
        going.append(pltpu.make_async_copy(packed.at[step], out.at[pl.ds(step * strip, strip)], left.at[step]))
    for step in range(steps):
        coming[step].wait()
        packed[step] = edges[step].reshape(strip, width).astype(packed.dtype)
        going[step].start()
    for copy in going:
        copy.wait()


def pack(first, field, after):
    steps, rows, cols, width = field.shape
    strip = HALO * cols
    return call(
        functools.partial(pack_kernel, first),
        "pack",
        bf16(steps * strip, width),
        [HBM] * 2,
        HBM,
        [
            pltpu.VMEM((steps, HALO, cols, width), jnp.float32),
            pltpu.VMEM((steps, strip, width), jnp.bfloat16),
            pltpu.SemaphoreType.DMA((steps,)),
            pltpu.SemaphoreType.DMA((steps,)),
        ],
        3,
        limit=62,
    )(field, after)


def before_kernel(field, diag, couple, kern, _, edges, scaled, data, upper, core, lower, outward, line, wide, pairs):
    steps, rows, cols, width = field.shape
    inner = rows - 2 * HALO
    listed = edge_rows(rows)
    spread((diag, couple), (), line, wide)
    pairs[0, :, 0:width] = jnp.zeros((inner * cols, width), pairs.dtype)

    @pl.loop(0, steps)
    def _(step):
        def store(row, value, weighted):
            if row in listed:
                edges[step, listed.index(row)] = value
            else:
                at = (row - HALO) * cols
                rounded = value.astype(pairs.dtype)
                pairs[step, at : at + cols, width : 2 * width] = rounded
                pairs[step + 1, at : at + cols, 0:width] = rounded
            if row == 0:
                scaled[step, 0] = weighted[0]
            if row == rows - 1:
                scaled[step, 1] = weighted[rows - 1]

        own_sweeps(lambda row: field[step, row], wide, rows, store)

    @pl.loop(0, steps)
    def _(lag):
        for target, first in ((upper, 0), (core, HALO), (lower, rows - HALO)):
            for row in range(target.shape[1]):
                target[lag, row] = kern[lag, first + row].T
        for spot, row in enumerate(listed):
            outward[lag, :, spot * cols : (spot + 1) * cols] = kern[lag, row]

    for step in range(0, steps, 2):
        acc = None
        for lag in range(step + 2):
            left = jnp.concatenate([kern[lag, row] for row in range(HALO, rows - HALO)], axis=1)
            term = jnp.dot(left, pairs[step + 1 - lag], preferred_element_type=jnp.float32)
            acc = term if acc is None else acc + term
        data[step] = acc[:, 0:width]
        data[step + 1] = acc[:, width : 2 * width]


def before(field, diag, couple, kern, after):
    steps, rows, cols, width = field.shape
    sensors = kern.shape[2]
    inner = (rows - 2 * HALO) * cols
    return call(
        before_kernel,
        "before",
        (
            f32(steps, 2 * HALO, cols, width),
            f32(steps, 2, cols, width),
            f32(steps, sensors, width),
            bf16(steps, HALO, cols, sensors),
            bf16(steps, rows - 2 * HALO, cols, sensors),
            bf16(steps, HALO, cols, sensors),
            bf16(steps, sensors, 2 * HALO * cols),
        ),
        [VMEM] * 4 + [HBM],
        [VMEM] * 7,
        coef_scratch(rows + 2 * HALO, cols, width) + [pltpu.VMEM((steps + 1, inner, 2 * width), jnp.bfloat16)],
        12,
    )(field, diag, couple, kern, after)


def edge_product(half, pairs, outward, start, out):
    steps, sensors, _ = outward.shape
    width = out.shape[2]
    kept = sensors // 2
    span = pl.ds(pl.multiple_of(half * kept, kept), kept)
    for step in range(0, steps, 2):
        acc = jnp.concatenate([start[step, span, :], start[step + 1, span, :]], axis=1)
        for lag in range(step + 2):
            left = outward[lag, span, :]
            acc = acc + jnp.dot(left, pairs[step + 1 - lag], preferred_element_type=jnp.float32)
        out[step] = acc[:, 0:width].astype(out.dtype)
        out[step + 1] = acc[:, width : 2 * width].astype(out.dtype)


def leaving_kernel(
    twin, top, bottom, diag, couple, ctop, cbottom, edges, scaled, outward, start, out, pairs, line, wide, mix
):
    steps = outward.shape[0]
    cols, width = edges.shape[2], edges.shape[3]
    spread((diag, couple), (ctop, cbottom), line, wide)
    mix_coefs(wide, mix)
    pairs[0, :, 0:width] = jnp.zeros((2 * HALO * cols, width), pairs.dtype)

    @pl.loop(0, steps)
    def _(step):
        for side, message in enumerate((top, bottom)):
            added = halo_part(message, step * (HALO * cols), scaled[step, side], mix, side)
            for spot, extra in zip(spots_of(side), added):
                rounded = (edges[step, spot] + extra).astype(pairs.dtype)
                at = spot * cols
                pairs[step, at : at + cols, width : 2 * width] = rounded
                pairs[step + 1, at : at + cols, 0:width] = rounded

    edge_product(1 - twin[0], pairs, outward, start, out)


def leaving(twin, top, bottom, diag, couple, ctop, cbottom, edges, scaled, outward, start):
    steps, sensors, _ = outward.shape
    rows, cols = diag.shape
    width = edges.shape[3]
    return call(
        leaving_kernel,
        "leaving",
        [bf16(steps, sensors // 2, width), bf16(steps + 1, 2 * HALO * cols, 2 * width)],
        [SMEM] + [VMEM] * 10,
        [VMEM] * 2,
        coef_scratch(rows + 2 * HALO, cols, width) + [pltpu.VMEM((2, 8, cols, width), jnp.float32)],
        1,
    )(twin, top, bottom, diag, couple, ctop, cbottom, edges, scaled, outward, start)


def staying_kernel(twin, pairs, outward, start, out):
    edge_product(twin[0], pairs, outward, start, out)


def staying(twin, pairs, outward, start):
    steps, sensors, width = start.shape
    out = f32(steps, sensors // 2, width)
    return call(staying_kernel, "staying", out, [SMEM] + [VMEM] * 3, VMEM, [], 1)(twin, pairs, outward, start)


def join_kernel(parts, mine, got, both):
    steps, kept, width = mine.shape
    groups, share, _ = both.shape
    rows = share // parts
    span = steps // parts
    for step in range(steps):
        total = (mine[step] + got[step].astype(jnp.float32)).astype(both.dtype)
        part, at = divmod(step, span)
        owners = kept // rows
        place = slice(at * owners, (at + 1) * owners), slice(part * rows, (part + 1) * rows)
        both[place] = total.reshape(owners, rows, width)


def join(parts, groups, mine, got):
    steps, kept, width = mine.shape
    out = bf16(groups, steps * kept // groups, width)
    kernel = functools.partial(join_kernel, parts)
    return call(kernel, "join", out, [VMEM] * 2, VMEM, [], 1)(mine, got)


def scale_kernel(pieces, prec, own, *copies):
    total = pieces[0].astype(jnp.float32)
    for piece in range(1, pieces.shape[0]):
        total = total + pieces[piece].astype(jnp.float32)
    weighted = (total * prec[...]).astype(pieces.dtype)
    rows = own.shape[0]
    own[...] = weighted[0:rows]
    for part, out in enumerate(copies):
        for piece in range(pieces.shape[0]):
            out[piece] = weighted[(part + 1) * rows : (part + 2) * rows]


def scale(parts, pieces, prec):
    groups, share, width = pieces.shape
    rows = share // parts
    shapes = [bf16(rows, width)] + [bf16(groups, rows, width)] * (parts - 1)
    own, *copies = call(scale_kernel, "scale", shapes, [VMEM] * 2, [VMEM] * parts, [], 0)(pieces, prec)
    return own, copies


def merge_kernel(twin, own, got, out):
    rows = own.shape[0]
    for value, half in ((own, twin[0]), (got, 1 - twin[0])):
        for piece in range(out.shape[0]):
            out[piece, pl.ds(pl.multiple_of(half * rows, rows), rows), :] = value[...]


def merge(twin, own, got, groups):
    rows, width = own.shape
    out = bf16(groups, 2 * rows, width)
    return call(merge_kernel, "merge", out, [SMEM, VMEM, VMEM], VMEM, [], 0)(twin, own, got)


def fill_pairs(span, pieces, pairs, later):
    sensors, width = pairs.shape[1], pairs.shape[2] // 2
    follows = later[0][0, :, 0:width] if later else jnp.zeros((sensors, width), pairs.dtype)
    pairs[span - 1, :, width : 2 * width] = follows
    for step, at, value in pieces:
        pairs[step, at, 0:width] = value
        if step:
            pairs[step - 1, at, width : 2 * width] = value


def halves(twin, mine, other):
    span, kept, _ = mine.shape
    for source, half in ((mine, twin[0]), (other, 1 - twin[0])):
        at = pl.ds(pl.multiple_of(half * kept, kept), kept)
        for step in range(span):
            yield step, at, source[step]


def owners(span, sensors, gathered):
    groups, both, _ = gathered.shape
    rows, each = both // 2, groups // span
    for group in range(groups):
        step, at = divmod(group, each)
        for half in range(2):
            first = half * (sensors // 2) + at * rows
            yield step, slice(first, first + rows), gathered[group, half * rows : (half + 1) * rows, :]


def strip_product(turned, blocks, store):
    steps, rows, cols, sensors = turned.shape
    blocks = [block.at[at] for block in blocks for at in range(block.shape[0])]
    first = steps - len(blocks)
    for step in range(first, steps, 2):
        acc = None
        for lag in range(steps - step):
            left = turned[lag].reshape(rows * cols, sensors)
            right = blocks[step + lag - first][...]
            term = jnp.dot(left, right, preferred_element_type=jnp.float32)
            acc = term if acc is None else acc + term
        width = acc.shape[1] // 2
        if not store(step - first, acc[:, 0:width]):
            break
        store(step - first + 1, acc[:, width:])


def strip_store(field, message):
    span, _, cols, width = field.shape
    strip = HALO * cols

    def store(at, part):
        if at >= span:
            return False
        field[at] = part.reshape(HALO, cols, width)
        message[at * strip : (at + 1) * strip, :] = part.astype(message.dtype)
        return True

    return store


def tail_kernel(count, twin, *refs):
    *given, turned, _ = refs[:count]
    *later, field, message, pairs = refs[count:]
    span, sensors = pairs.shape[0], pairs.shape[1]
    pieces = halves(twin, *given) if len(given) == 2 else owners(span, sensors, given[0])
    fill_pairs(span, pieces, pairs, later)
    strip_product(turned, [pairs, *later], strip_store(field, message))


def head_kernel(count, turned, _, *refs):
    field, message = refs[count:]
    strip_product(turned, refs[:count], strip_store(field, message))


def strip_shapes(span, cols, width):
    return [f32(span, HALO, cols, width), bf16(span * HALO * cols, width)]


def adjoint_tail(span, twin, given, turned, later, after):
    _, _, cols, sensors = turned.shape
    width = given[0].shape[2]
    return call(
        functools.partial(tail_kernel, len(given) + 2),
        "adjoint_tail",
        strip_shapes(span, cols, width) + [bf16(span, sensors, 2 * width)],
        [SMEM] + [VMEM] * (len(given) + 1) + [HBM] + [VMEM] * len(later),
        [VMEM] * 3,
        [],
        0,
    )(twin, *given, turned, after, *later)


def adjoint_head(blocks, turned, after):
    cols = turned.shape[2]
    span, _, width = blocks[0].shape
    return call(
        functools.partial(head_kernel, len(blocks)),
        "adjoint_head",
        strip_shapes(span, cols, width // 2),
        [VMEM, HBM] + [VMEM] * len(blocks),
        [VMEM] * 2,
        [],
        1,
    )(turned, after, *blocks)


def inner_kernel(first, count, turned, diag, couple, ctop, cbottom, upper, lower, *refs):
    blocks = refs[:count]
    edges, scaled, mix, out, core, line, wide, sent = refs[-8:]
    _, inner, cols, _ = turned.shape
    span, _, _, width = core.shape
    rows = inner + 2 * HALO
    listed = edge_rows(rows)
    spread((diag, couple), (ctop, cbottom), line, wide)
    mix_coefs(wide, mix)

    def keep(at, part):
        if at >= span:
            return False
        core[at] = part.reshape(inner, cols, width)
        return True

    strip_product(turned, blocks, keep)

    @pl.loop(0, span)
    def _(step):
        def load(row):
            if row < HALO:
                return upper[step, row]
            return core[step, row - HALO] if row < rows - HALO else lower[step, row - rows + HALO]

        def store(row, value, weighted):
            if row in listed:
                edges[step, listed.index(row)] = value
            else:
                core[step, row - HALO] = value
            if row == 0:
                scaled[step, 0] = weighted[0]
            if row == rows - 1:
                scaled[step, 1] = weighted[rows - 1]

        own_sweeps(load, wide, rows, store)

    copy = pltpu.make_async_copy(core, out.at[pl.ds(first, span), pl.ds(HALO, inner)], sent)
    copy.start()
    copy.wait()


def inner(first, blocks, turned, upper, lower, diag, couple, ctop, cbottom, out):
    steps, core, cols, _ = turned.shape
    span, _, _, width = upper.shape
    rows = core + 2 * HALO
    given = [] if out is None else [out]
    count = 7 + len(blocks)
    return call(
        functools.partial(inner_kernel, first, len(blocks)),
        "inner",
        (
            f32(span, 2 * HALO, cols, width),
            f32(span, 2, cols, width),
            f32(2, 8, cols, width),
            f32(steps, rows, cols, width),
        ),
        [VMEM] * count + [HBM] * len(given),
        [VMEM, VMEM, VMEM, HBM],
        [pltpu.VMEM((span, core, cols, width), jnp.float32)]
        + coef_scratch(rows + 2 * HALO, cols, width)
        + [pltpu.SemaphoreType.DMA],
        8,
        aliases={count: 3} if given else {},
    )(turned, diag, couple, ctop, cbottom, upper, lower, *blocks, *given)


def finish_kernel(side, message, mix, edges, scaled, _, out):
    span, _, cols, _ = out.shape
    begin = pl.program_id(0) * span

    @pl.loop(0, span)
    def _(at):
        step = begin + at
        added = halo_part(message, step * (HALO * cols), scaled[step, side], mix, side)
        for spot, extra in zip(spots_of(side), added):
            out[at, spot % HALO] = edges[step, spot] + extra


def finish(side, first, message, mix, edges, scaled, out):
    steps, rows, cols, width = out.shape
    count = message.shape[0] // (HALO * cols)
    span = count // 2
    place = side * (rows // HALO - 1)
    return call(
        functools.partial(finish_kernel, side),
        "finish",
        f32(*out.shape),
        [VMEM] * 4 + [HBM],
        pl.BlockSpec((span, HALO, cols, width), lambda step: (first // span + step, place, 0, 0)),
        [],
        1,
        (count // span,),
        {4: 0},
    )(message, mix, edges, scaled, out)


def send_down(tail):
    return lax.ppermute(tail, "tile", [(i, i + 1) for i in range(lax.axis_size("tile") - 1)])


def send_up(head):
    return lax.ppermute(head, "tile", [(i + 1, i) for i in range(lax.axis_size("tile") - 1)])


def swap_twins(value):
    return lax.ppermute(value, "twin", [(0, 1), (1, 0)])


def body(sketch, diag_coef, couple, kernel, noise_prec):
    steps, _, rows, cols, width = sketch.shape
    sensors = kernel.shape[1]
    others = ("pair", "tile")
    groups = lax.axis_size(others)
    twin = lax.axis_index("twin")
    which = twin.reshape(1)
    field = sketch.reshape(steps, rows, cols, width)
    diag, couple = diag_coef.reshape(rows, cols), couple.reshape(rows, cols)
    kern = jnp.transpose(kernel.reshape(steps, sensors, rows, cols), (0, 2, 1, 3))
    kept = sensors // 2
    share = steps * kept // groups

    tail = pack(rows - HALO, field, sketch)
    top = send_down(tail)
    bottom = send_up(pack(0, field, tail))
    coefs = jnp.stack([diag, couple])
    note = send_down(coefs[:, rows - HALO :]), send_up(coefs[:, :HALO])
    parts = 2 if share % 32 == 0 else 1
    rows_each = share // parts
    noise = lax.dynamic_slice(noise_prec, (0, twin * kept), (steps, kept)).reshape(parts, -1)
    noise = lax.dynamic_slice(noise, (0, lax.axis_index(others) * rows_each), (parts, rows_each)).reshape(share)
    prec = jnp.broadcast_to(noise[:, None], (share, width))
    edges, scaled, data, turned_upper, turned_core, turned_lower, outward = before(field, diag, couple, kern, prec)

    gone, pairs = leaving(which, top, bottom, diag, couple, *note, edges, scaled, outward, data)
    both = join(parts, groups, staying(which, pairs, outward, data), swap_twins(gone))
    own, copies = scale(parts, lax.all_to_all(both, others, 0, 0, tiled=True), prec)

    def gather(sent):
        return lax.all_to_all(sent, others, 0, 0, tiled=True)

    def both_halves(sent):
        mine = gather(sent).reshape(span, kept, width)
        return mine, swap_twins(mine)

    span = steps // parts
    blocks, uppers, lowers, tops, bottoms = [], [], [], [], []
    for part in reversed(range(parts)):
        if part:
            given = both_halves(copies[part - 1])
        elif parts == 1:
            given = both_halves(jnp.broadcast_to(own[None], (groups, share, width)))
        else:
            given = (gather(merge(which, own, swap_twins(own), groups)),)
        lower, tail, made = adjoint_tail(span, which, given, turned_lower, blocks, uppers[0] if uppers else prec)
        tops.insert(0, send_down(tail))
        blocks.insert(0, made)
        upper, head = adjoint_head(blocks, turned_upper, tail)
        bottoms.insert(0, send_up(head))
        uppers.insert(0, upper)
        lowers.insert(0, lower)

    out = None
    for part in reversed(range(parts)):
        first = part * span
        strips = uppers[part], lowers[part]
        edges, scaled, mix, out = inner(first, blocks[part:], turned_core, *strips, diag, couple, *note, out)
        for side, message in enumerate((tops[part], bottoms[part])):
            out = finish(side, first, message, mix, edges, scaled, out)
    return out.reshape(sketch.shape)


def solution(mesh):
    bands, tiles = mesh.shape["band"], mesh.shape["tile"]
    fine = Mesh(mesh.devices.reshape(bands // 2, 2, tiles), ("pair", "twin", "tile"))
    band = ("pair", "twin")
    placed = (
        P(None, band, "tile", None, None),
        P(band, "tile", None),
        P(band, "tile", None),
        P(None, None, band, "tile", None),
        P(),
    )
    return jax.shard_map(
        body,
        mesh=fine,
        in_specs=placed,
        out_specs=P(None, band, "tile", None, None),
        check_vma=False,
    )
```

```python
import functools

import jax
import jax.numpy as jnp
from jax import lax
from jax.experimental import pallas as pl
from jax.experimental.pallas import tpu as pltpu
from jax.sharding import Mesh
from jax.sharding import PartitionSpec as P

MIB = 1 << 20
HALO = 2
TILE = ("slow", "fast")
VMEM = pl.BlockSpec(memory_space=pltpu.VMEM)
SMEM = pl.BlockSpec(memory_space=pltpu.SMEM)
HBM = pl.BlockSpec(memory_space=pltpu.HBM)


def call(kernel, name, out_shape, in_specs, out_specs, scratch, moved, grid=(), aliases={}, limit=16):
    return pl.pallas_call(
        kernel,
        grid=grid,
        out_shape=out_shape,
        in_specs=in_specs,
        out_specs=out_specs,
        scratch_shapes=scratch,
        input_output_aliases=aliases,
        compiler_params=pltpu.CompilerParams(vmem_limit_bytes=limit * MIB),
        cost_estimate=pl.CostEstimate(flops=0, bytes_accessed=moved * MIB, transcendentals=0),
        name=name,
    )


def f32(*shape):
    return jax.ShapeDtypeStruct(shape, jnp.float32)


def bf16(*shape):
    return jax.ShapeDtypeStruct(shape, jnp.bfloat16)


def edge_rows(rows):
    return [*range(HALO), *range(rows - HALO, rows)]


def beside(w):
    cols = w.shape[0]
    at = lax.broadcasted_iota(jnp.int32, w.shape, 0)
    before = jnp.where(at == 0, 0.0, pltpu.roll(w, 1, 0))
    after = jnp.where(at == cols - 1, 0.0, pltpu.roll(w, cols - 1, 0))
    return before + after


def spread(own, halos, line, wide):
    rows, cols = own[0].shape
    for which in range(2):
        line[...] = jnp.zeros(line.shape, line.dtype)
        for side, halo in enumerate(halos):
            at = side * (HALO + rows)
            line[at : at + HALO, :] = halo[which]
        line[HALO : HALO + rows, :] = own[which][...]
        turned = line[...].T
        for row in range(rows + 2 * HALO):
            wide[which, row] = jnp.broadcast_to(turned[:, row : row + 1], wide.shape[2:])


def mix_coefs(wide, mix):
    total = wide.shape[1]
    for side in range(2):
        far, near, edge, inner = (row if side == 0 else total - 1 - row for row in range(4))
        square = wide[1, edge] * wide[1, edge]
        mix[side, 0] = wide[1, near]
        mix[side, 1] = wide[1, far]
        mix[side, 2] = wide[1, near] * wide[0, near]
        mix[side, 3] = wide[1, near] * wide[1, near]
        mix[side, 4] = -square
        mix[side, 5] = -wide[0, edge] * wide[1, edge]
        mix[side, 6] = wide[1, edge]
        mix[side, 7] = wide[1, inner] * square


def coef_scratch(rows, cols, width):
    return [pltpu.VMEM((cols, cols), jnp.float32), pltpu.VMEM((2, rows, cols, width), jnp.float32)]


def one_sweep(values, scaled, wide, row):
    around = beside(scaled[row])
    if row > 0:
        around = around + scaled[row - 1]
    if row + 1 < len(scaled):
        around = around + scaled[row + 1]
    return wide[0, row + HALO] * values[row] - wide[1, row + HALO] * around


def own_sweeps(load, wide, rows, store):
    values, scaled, first, second = ([None] * rows for _ in range(4))
    for row in range(rows + 2):
        if row < rows:
            values[row] = load(row)
            scaled[row] = wide[1, row + HALO] * values[row]
        if 0 < row <= rows:
            first[row - 1] = one_sweep(values, scaled, wide, row - 1)
            second[row - 1] = wide[1, row - 1 + HALO] * first[row - 1]
        if row > 1:
            store(row - 2, one_sweep(first, second, wide, row - 2), scaled)


def halo_part(message, at, edge_scaled, mix, side):
    cols = edge_scaled.shape[0]
    far_row, near_row = (0, 1) if side == 0 else (1, 0)

    def take(row):
        start = pl.multiple_of(at + row * cols, cols)
        return message[pl.ds(start, cols), :].astype(jnp.float32)

    near = take(near_row)
    scaled = mix[side, 0] * near
    around = mix[side, 1] * take(far_row) + edge_scaled + beside(scaled)
    near_second = mix[side, 2] * near - mix[side, 3] * around
    second = mix[side, 4] * scaled
    on_edge = mix[side, 5] * scaled - mix[side, 6] * (near_second + beside(second))
    return on_edge, mix[side, 7] * scaled


def spots_of(side):
    return (0, 1) if side == 0 else (2 * HALO - 1, 2 * HALO - 2)


def pack_kernel(first, field, _, out, edges, packed, arrived, left):
    steps, rows, cols, width = field.shape
    strip = HALO * cols
    coming, going = [], []
    for step in range(steps):
        source = field.at[step, pl.ds(first, HALO)]
        coming.append(pltpu.make_async_copy(source, edges.at[step], arrived.at[step]))
        coming[step].start()
        going.append(pltpu.make_async_copy(packed.at[step], out.at[pl.ds(step * strip, strip)], left.at[step]))
    for step in range(steps):
        coming[step].wait()
        packed[step] = edges[step].reshape(strip, width).astype(packed.dtype)
        going[step].start()
    for copy in going:
        copy.wait()


def pack(first, field, after):
    steps, rows, cols, width = field.shape
    strip = HALO * cols
    return call(
        functools.partial(pack_kernel, first),
        "pack",
        bf16(steps * strip, width),
        [HBM] * 2,
        HBM,
        [
            pltpu.VMEM((steps, HALO, cols, width), jnp.float32),
            pltpu.VMEM((steps, strip, width), jnp.bfloat16),
            pltpu.SemaphoreType.DMA((steps,)),
            pltpu.SemaphoreType.DMA((steps,)),
        ],
        3,
        limit=62,
    )(field, after)


def before_kernel(field, diag, couple, kern, _, edges, scaled, data, turned, outward, line, wide, pairs):
    steps, rows, cols, width = field.shape
    inner = rows - 2 * HALO
    listed = edge_rows(rows)
    spread((diag, couple), (), line, wide)
    pairs[0, :, 0:width] = jnp.zeros((inner * cols, width), pairs.dtype)

    @pl.loop(0, steps)
    def _(step):
        def store(row, value, weighted):
            if row in listed:
                edges[step, listed.index(row)] = value
            else:
                at = (row - HALO) * cols
                rounded = value.astype(pairs.dtype)
                pairs[step, at : at + cols, width : 2 * width] = rounded
                pairs[step + 1, at : at + cols, 0:width] = rounded
            if row == 0:
                scaled[step, 0] = weighted[0]
            if row == rows - 1:
                scaled[step, 1] = weighted[rows - 1]

        own_sweeps(lambda row: field[step, row], wide, rows, store)

    @pl.loop(0, steps)
    def _(lag):
        for row in range(rows):
            turned[lag, row] = kern[lag, row].T
        for spot, row in enumerate(listed):
            outward[lag, :, spot * cols : (spot + 1) * cols] = kern[lag, row]

    for step in range(0, steps, 2):
        acc = None
        for lag in range(step + 2):
            left = jnp.concatenate([kern[lag, row] for row in range(HALO, rows - HALO)], axis=1)
            term = jnp.dot(left, pairs[step + 1 - lag], preferred_element_type=jnp.float32)
            acc = term if acc is None else acc + term
        data[step] = acc[:, 0:width]
        data[step + 1] = acc[:, width : 2 * width]


def before(field, diag, couple, kern, after):
    steps, rows, cols, width = field.shape
    sensors = kern.shape[2]
    inner = (rows - 2 * HALO) * cols
    return call(
        before_kernel,
        "before",
        (
            f32(steps, 2 * HALO, cols, width),
            f32(steps, 2, cols, width),
            f32(steps, sensors, width),
            bf16(steps, rows, cols, sensors),
            bf16(steps, sensors, 2 * HALO * cols),
        ),
        [VMEM] * 4 + [HBM],
        [VMEM] * 5,
        coef_scratch(rows + 2 * HALO, cols, width) + [pltpu.VMEM((steps + 1, inner, 2 * width), jnp.bfloat16)],
        12,
    )(field, diag, couple, kern, after)


def edge_product(half, pairs, outward, start, out):
    steps, sensors, _ = outward.shape
    width = out.shape[2]
    kept = sensors // 2
    span = pl.ds(pl.multiple_of(half * kept, kept), kept)
    for step in range(0, steps, 2):
        acc = jnp.concatenate([start[step, span, :], start[step + 1, span, :]], axis=1)
        for lag in range(step + 2):
            left = outward[lag, span, :]
            acc = acc + jnp.dot(left, pairs[step + 1 - lag], preferred_element_type=jnp.float32)
        out[step] = acc[:, 0:width].astype(out.dtype)
        out[step + 1] = acc[:, width : 2 * width].astype(out.dtype)


def leaving_kernel(
    twin, top, bottom, diag, couple, ctop, cbottom, edges, scaled, outward, start, out, pairs, line, wide, mix
):
    steps = outward.shape[0]
    cols, width = edges.shape[2], edges.shape[3]
    spread((diag, couple), (ctop, cbottom), line, wide)
    mix_coefs(wide, mix)
    pairs[0, :, 0:width] = jnp.zeros((2 * HALO * cols, width), pairs.dtype)

    @pl.loop(0, steps)
    def _(step):
        for side, message in enumerate((top, bottom)):
            added = halo_part(message, step * (HALO * cols), scaled[step, side], mix, side)
            for spot, extra in zip(spots_of(side), added):
                rounded = (edges[step, spot] + extra).astype(pairs.dtype)
                at = spot * cols
                pairs[step, at : at + cols, width : 2 * width] = rounded
                pairs[step + 1, at : at + cols, 0:width] = rounded

    edge_product(1 - twin[0], pairs, outward, start, out)


def leaving(twin, top, bottom, diag, couple, ctop, cbottom, edges, scaled, outward, start):
    steps, sensors, _ = outward.shape
    rows, cols = diag.shape
    width = edges.shape[3]
    return call(
        leaving_kernel,
        "leaving",
        [bf16(steps, sensors // 2, width), bf16(steps + 1, 2 * HALO * cols, 2 * width)],
        [SMEM] + [VMEM] * 10,
        [VMEM] * 2,
        coef_scratch(rows + 2 * HALO, cols, width) + [pltpu.VMEM((2, 8, cols, width), jnp.float32)],
        1,
    )(twin, top, bottom, diag, couple, ctop, cbottom, edges, scaled, outward, start)


def staying_kernel(twin, pairs, outward, start, out):
    edge_product(twin[0], pairs, outward, start, out)


def staying(twin, pairs, outward, start):
    steps, sensors, width = start.shape
    out = f32(steps, sensors // 2, width)
    return call(staying_kernel, "staying", out, [SMEM] + [VMEM] * 3, VMEM, [], 1)(twin, pairs, outward, start)


def join_kernel(mine, got, both):
    both[...] = (mine[...] + got[...].astype(jnp.float32)).astype(both.dtype)


def join(mine, got):
    return call(join_kernel, "join", bf16(*got.shape), [VMEM] * 2, VMEM, [], 1)(mine, got)


def scale_kernel(pieces, prec, out):
    total = pieces[0].astype(jnp.float32)
    for piece in range(1, pieces.shape[0]):
        total = total + pieces[piece].astype(jnp.float32)
    weighted = (total * prec[...]).astype(out.dtype)
    for piece in range(pieces.shape[0]):
        out[piece] = weighted


def scale(pieces, prec):
    return call(scale_kernel, "scale", bf16(*pieces.shape), [VMEM] * 2, VMEM, [], 1)(pieces, prec)


def fill_pairs(twin, mine, other, pairs):
    steps, kept, width = mine.shape
    pairs[steps, :, width : 2 * width] = jnp.zeros((2 * kept, width), pairs.dtype)
    for source, half in ((mine, twin[0]), (other, 1 - twin[0])):
        at = pl.ds(pl.multiple_of(half * kept, kept), kept)
        for step in range(steps):
            pairs[step + 1, at, 0:width] = source[step]
            pairs[step, at, width : 2 * width] = source[step]


def strip_product(rows, turned, pairs, field, message):
    steps, _, cols, sensors = turned.shape
    strip = HALO * cols
    width = message.shape[1]
    for step in range(0, steps, 2):
        acc = None
        for lag in range(steps - step):
            left = turned[lag, rows].reshape(strip, sensors)
            term = jnp.dot(left, pairs[step + lag + 1], preferred_element_type=jnp.float32)
            acc = term if acc is None else acc + term
        for side in range(2):
            part = acc[:, side * width : (side + 1) * width]
            field[step + side] = part.reshape(HALO, cols, width)
            at = (step + side) * strip
            message[at : at + strip, :] = part.astype(message.dtype)


def tail_kernel(twin, mine, other, turned, field, message, pairs):
    rows = turned.shape[1]
    fill_pairs(twin, mine, other, pairs)
    strip_product(slice(rows - HALO, rows), turned, pairs, field, message)


def head_kernel(pairs, turned, _, field, message):
    strip_product(slice(0, HALO), turned, pairs, field, message)


def adjoint_tail(twin, mine, other, turned):
    steps, _, cols, sensors = turned.shape
    width = mine.shape[2]
    return call(
        tail_kernel,
        "adjoint_tail",
        (
            f32(steps, HALO, cols, width),
            bf16(steps * HALO * cols, width),
            bf16(steps + 1, sensors, 2 * width),
        ),
        [SMEM] + [VMEM] * 3,
        [VMEM] * 3,
        [],
        4,
    )(twin, mine, other, turned)


def adjoint_head(pairs, turned, after):
    steps, _, cols, _ = turned.shape
    width = pairs.shape[2] // 2
    return call(
        head_kernel,
        "adjoint_head",
        (f32(steps, HALO, cols, width), bf16(steps * HALO * cols, width)),
        [VMEM, VMEM, HBM],
        [VMEM] * 2,
        [],
        4,
    )(pairs, turned, after)


def inner_kernel(
    pairs, turned, upper, lower, diag, couple, ctop, cbottom, edges, scaled, out, mix, core, line, wide
):
    steps, rows, cols, sensors = turned.shape
    width = core.shape[3]
    inner = rows - 2 * HALO
    pack_at = pl.program_id(0)

    @pl.when(pack_at == 0)
    def _():
        spread((diag, couple), (ctop, cbottom), line, wide)
        mix_coefs(wide, mix)
        for step in range(0, steps, 2):
            acc = None
            for lag in range(steps - step):
                left = turned[lag, HALO : rows - HALO].reshape(inner * cols, sensors)
                term = jnp.dot(left, pairs[step + lag + 1], preferred_element_type=jnp.float32)
                acc = term if acc is None else acc + term
            for side in range(2):
                core[step + side] = acc[:, side * width : (side + 1) * width].reshape(inner, cols, width)

    listed = edge_rows(rows)
    span = out.shape[0]

    @pl.loop(0, span)
    def _(at):
        step = pack_at * span + at

        def load(row):
            if row < HALO:
                return upper[step, row]
            return core[step, row - HALO] if row < rows - HALO else lower[step, row - rows + HALO]

        def store(row, value, weighted):
            if row in listed:
                edges[step, listed.index(row)] = value
            else:
                out[at, row - HALO] = value
            if row == 0:
                scaled[step, 0] = weighted[0]
            if row == rows - 1:
                scaled[step, 1] = weighted[rows - 1]

        own_sweeps(load, wide, rows, store)


def inner(pairs, turned, upper, lower, diag, couple, ctop, cbottom):
    steps, rows, cols, _ = turned.shape
    width = upper.shape[3]
    core = rows - 2 * HALO
    assert core == HALO
    span = steps // 2
    return call(
        inner_kernel,
        "inner",
        (
            f32(steps, 2 * HALO, cols, width),
            f32(steps, 2, cols, width),
            f32(steps, rows, cols, width),
            f32(2, 8, cols, width),
        ),
        [VMEM] * 8,
        [VMEM, VMEM, pl.BlockSpec((span, core, cols, width), lambda step: (step, 1, 0, 0)), VMEM],
        [pltpu.VMEM((steps, core, cols, width), jnp.float32)] + coef_scratch(rows + 2 * HALO, cols, width),
        10,
        (steps // span,),
    )(pairs, turned, upper, lower, diag, couple, ctop, cbottom)


def finish_kernel(side, message, mix, edges, scaled, _, out):
    span, _, cols, _ = out.shape
    first = pl.program_id(0) * span

    @pl.loop(0, span)
    def _(at):
        step = first + at
        added = halo_part(message, step * (HALO * cols), scaled[step, side], mix, side)
        for spot, extra in zip(spots_of(side), added):
            out[at, spot % HALO] = edges[step, spot] + extra


def finish(side, message, mix, edges, scaled, out):
    steps, rows, cols, width = out.shape
    span = steps // 4
    place = side * (rows // HALO - 1)
    return call(
        functools.partial(finish_kernel, side),
        "finish",
        f32(*out.shape),
        [VMEM] * 4 + [HBM],
        pl.BlockSpec((span, HALO, cols, width), lambda step: (step, place, 0, 0)),
        [],
        2,
        (steps // span,),
        {4: 0},
    )(message, mix, edges, scaled, out)


def send_down(tail):
    return lax.ppermute(tail, TILE, [(i, i + 1) for i in range(lax.axis_size(TILE) - 1)])


def send_up(head):
    return lax.ppermute(head, TILE, [(i + 1, i) for i in range(lax.axis_size(TILE) - 1)])


def swap_twins(value):
    return lax.ppermute(value, "twin", [(0, 1), (1, 0)])


def body(sketch, diag_coef, couple, kernel, noise_prec):
    steps, _, rows, cols, width = sketch.shape
    sensors = kernel.shape[1]
    others = ("fast", "pair", "slow")
    groups = lax.axis_size(others)
    twin = lax.axis_index("twin")
    which = twin.reshape(1)
    field = sketch.reshape(steps, rows, cols, width)
    diag, couple = diag_coef.reshape(rows, cols), couple.reshape(rows, cols)
    kern = jnp.transpose(kernel.reshape(steps, sensors, rows, cols), (0, 2, 1, 3))
    kept = sensors // 2
    share = steps * kept // groups

    tail = pack(rows - HALO, field, sketch)
    top = send_down(tail)
    bottom = send_up(pack(0, field, tail))
    coefs = jnp.stack([diag, couple])
    note = send_down(coefs[:, rows - HALO :]), send_up(coefs[:, :HALO])
    noise = lax.dynamic_slice(noise_prec, (0, twin * kept), (steps, kept)).reshape(steps * kept)
    noise = lax.dynamic_slice(noise, (lax.axis_index(others) * share,), (share,))
    prec = jnp.broadcast_to(noise[:, None], (share, width))
    edges, scaled, data, turned, outward = before(field, diag, couple, kern, prec)

    gone, pairs = leaving(which, top, bottom, diag, couple, *note, edges, scaled, outward, data)
    both = join(staying(which, pairs, outward, data), swap_twins(gone)).reshape(groups, share, width)
    pieces = lax.all_to_all(both, others, 0, 0, tiled=True)
    weighted = lax.all_to_all(scale(pieces, prec), others, 0, 0, tiled=True).reshape(steps, kept, width)
    lower, tail, pairs = adjoint_tail(which, weighted, swap_twins(weighted), turned)
    top = send_down(tail)
    upper, head = adjoint_head(pairs, turned, tail)
    bottom = send_up(head)
    edges, scaled, out, mix = inner(pairs, turned, upper, lower, diag, couple, *note)
    out = finish(0, top, mix, edges, scaled, out)
    out = finish(1, bottom, mix, edges, scaled, out)
    return out.reshape(sketch.shape)


def solution(mesh):
    bands, tiles = mesh.shape["band"], mesh.shape["tile"]
    fast = 2 if tiles % 2 == 0 else 1
    fine = Mesh(mesh.devices.reshape(bands // 2, 2, tiles // fast, fast), ("pair", "twin") + TILE)
    band = ("pair", "twin")
    placed = (
        P(None, band, TILE, None, None),
        P(band, TILE, None),
        P(band, TILE, None),
        P(None, None, band, TILE, None),
        P(),
    )
    return jax.shard_map(
        body,
        mesh=fine,
        in_specs=placed,
        out_specs=P(None, band, TILE, None, None),
        check_vma=False,
    )
```

```python
import functools

import jax
import jax.numpy as jnp
from jax import lax
from jax.experimental import pallas as pl
from jax.experimental.pallas import tpu as pltpu
from jax.sharding import Mesh
from jax.sharding import PartitionSpec as P

MIB = 1 << 20
HALO = 2
VMEM = pl.BlockSpec(memory_space=pltpu.VMEM)
SMEM = pl.BlockSpec(memory_space=pltpu.SMEM)
HBM = pl.BlockSpec(memory_space=pltpu.HBM)


def call(kernel, name, out_shape, in_specs, out_specs, scratch, moved, grid=(), aliases={}, limit=16):
    return pl.pallas_call(
        kernel,
        grid=grid,
        out_shape=out_shape,
        in_specs=in_specs,
        out_specs=out_specs,
        scratch_shapes=scratch,
        input_output_aliases=aliases,
        compiler_params=pltpu.CompilerParams(vmem_limit_bytes=limit * MIB),
        cost_estimate=pl.CostEstimate(flops=0, bytes_accessed=moved * MIB, transcendentals=0),
        name=name,
    )


def f32(*shape):
    return jax.ShapeDtypeStruct(shape, jnp.float32)


def bf16(*shape):
    return jax.ShapeDtypeStruct(shape, jnp.bfloat16)


def edge_rows(rows):
    return [*range(HALO), *range(rows - HALO, rows)]


def beside(w):
    cols = w.shape[0]
    at = lax.broadcasted_iota(jnp.int32, w.shape, 0)
    before = jnp.where(at == 0, 0.0, pltpu.roll(w, 1, 0))
    after = jnp.where(at == cols - 1, 0.0, pltpu.roll(w, cols - 1, 0))
    return before + after


def spread(own, halos, line, wide):
    rows, cols = own[0].shape
    for which in range(2):
        line[...] = jnp.zeros(line.shape, line.dtype)
        for side, halo in enumerate(halos):
            at = side * (HALO + rows)
            line[at : at + HALO, :] = halo[which]
        line[HALO : HALO + rows, :] = own[which][...]
        turned = line[...].T
        for row in range(rows + 2 * HALO):
            wide[which, row] = jnp.broadcast_to(turned[:, row : row + 1], wide.shape[2:])


def mix_coefs(wide, mix):
    total = wide.shape[1]
    for side in range(2):
        far, near, edge, inner = (row if side == 0 else total - 1 - row for row in range(4))
        square = wide[1, edge] * wide[1, edge]
        mix[side, 0] = wide[1, near]
        mix[side, 1] = wide[1, far]
        mix[side, 2] = wide[1, near] * wide[0, near]
        mix[side, 3] = wide[1, near] * wide[1, near]
        mix[side, 4] = -square
        mix[side, 5] = -wide[0, edge] * wide[1, edge]
        mix[side, 6] = wide[1, edge]
        mix[side, 7] = wide[1, inner] * square


def coef_scratch(rows, cols, width):
    return [pltpu.VMEM((cols, cols), jnp.float32), pltpu.VMEM((2, rows, cols, width), jnp.float32)]


def one_sweep(values, scaled, wide, row):
    around = beside(scaled[row])
    if row > 0:
        around = around + scaled[row - 1]
    if row + 1 < len(scaled):
        around = around + scaled[row + 1]
    return wide[0, row + HALO] * values[row] - wide[1, row + HALO] * around


def own_sweeps(load, wide, rows, store):
    values, scaled, first, second = ([None] * rows for _ in range(4))
    for row in range(rows + 2):
        if row < rows:
            values[row] = load(row)
            scaled[row] = wide[1, row + HALO] * values[row]
        if 0 < row <= rows:
            first[row - 1] = one_sweep(values, scaled, wide, row - 1)
            second[row - 1] = wide[1, row - 1 + HALO] * first[row - 1]
        if row > 1:
            store(row - 2, one_sweep(first, second, wide, row - 2), scaled)


def halo_part(message, at, edge_scaled, mix, side):
    cols = edge_scaled.shape[0]
    far_row, near_row = (0, 1) if side == 0 else (1, 0)

    def take(row):
        start = pl.multiple_of(at + row * cols, cols)
        return message[pl.ds(start, cols), :].astype(jnp.float32)

    near = take(near_row)
    scaled = mix[side, 0] * near
    around = mix[side, 1] * take(far_row) + edge_scaled + beside(scaled)
    near_second = mix[side, 2] * near - mix[side, 3] * around
    second = mix[side, 4] * scaled
    on_edge = mix[side, 5] * scaled - mix[side, 6] * (near_second + beside(second))
    return on_edge, mix[side, 7] * scaled


def spots_of(side):
    return (0, 1) if side == 0 else (2 * HALO - 1, 2 * HALO - 2)


def pack_kernel(first, field, _, out, edges, packed, arrived, left):
    steps, rows, cols, width = field.shape
    strip = HALO * cols
    coming, going = [], []
    for step in range(steps):
        source = field.at[step, pl.ds(first, HALO)]
        coming.append(pltpu.make_async_copy(source, edges.at[step], arrived.at[step]))
        coming[step].start()
        going.append(pltpu.make_async_copy(packed.at[step], out.at[pl.ds(step * strip, strip)], left.at[step]))
    for step in range(steps):
        coming[step].wait()
        packed[step] = edges[step].reshape(strip, width).astype(packed.dtype)
        going[step].start()
    for copy in going:
        copy.wait()


def pack(first, field, after):
    steps, rows, cols, width = field.shape
    strip = HALO * cols
    return call(
        functools.partial(pack_kernel, first),
        "pack",
        bf16(steps * strip, width),
        [HBM] * 2,
        HBM,
        [
            pltpu.VMEM((steps, HALO, cols, width), jnp.float32),
            pltpu.VMEM((steps, strip, width), jnp.bfloat16),
            pltpu.SemaphoreType.DMA((steps,)),
            pltpu.SemaphoreType.DMA((steps,)),
        ],
        3,
        limit=62,
    )(field, after)


def before_kernel(field, diag, couple, kern, _, edges, scaled, data, turned, outward, line, wide, pairs):
    steps, rows, cols, width = field.shape
    inner = rows - 2 * HALO
    listed = edge_rows(rows)
    spread((diag, couple), (), line, wide)
    pairs[0, :, 0:width] = jnp.zeros((inner * cols, width), pairs.dtype)

    @pl.loop(0, steps)
    def _(step):
        def store(row, value, weighted):
            if row in listed:
                edges[step, listed.index(row)] = value
            else:
                at = (row - HALO) * cols
                rounded = value.astype(pairs.dtype)
                pairs[step, at : at + cols, width : 2 * width] = rounded
                pairs[step + 1, at : at + cols, 0:width] = rounded
            if row == 0:
                scaled[step, 0] = weighted[0]
            if row == rows - 1:
                scaled[step, 1] = weighted[rows - 1]

        own_sweeps(lambda row: field[step, row], wide, rows, store)

    @pl.loop(0, steps)
    def _(lag):
        for row in range(rows):
            turned[lag, row] = kern[lag, row].T
        for spot, row in enumerate(listed):
            outward[lag, :, spot * cols : (spot + 1) * cols] = kern[lag, row]

    for step in range(0, steps, 2):
        acc = None
        for lag in range(step + 2):
            left = jnp.concatenate([kern[lag, row] for row in range(HALO, rows - HALO)], axis=1)
            term = jnp.dot(left, pairs[step + 1 - lag], preferred_element_type=jnp.float32)
            acc = term if acc is None else acc + term
        data[step] = acc[:, 0:width]
        data[step + 1] = acc[:, width : 2 * width]


def before(field, diag, couple, kern, after):
    steps, rows, cols, width = field.shape
    sensors = kern.shape[2]
    inner = (rows - 2 * HALO) * cols
    return call(
        before_kernel,
        "before",
        (
            f32(steps, 2 * HALO, cols, width),
            f32(steps, 2, cols, width),
            f32(steps, sensors, width),
            bf16(steps, rows, cols, sensors),
            bf16(steps, sensors, 2 * HALO * cols),
        ),
        [VMEM] * 4 + [HBM],
        [VMEM] * 5,
        coef_scratch(rows + 2 * HALO, cols, width) + [pltpu.VMEM((steps + 1, inner, 2 * width), jnp.bfloat16)],
        12,
    )(field, diag, couple, kern, after)


def edge_product(half, pairs, outward, start, out):
    steps, sensors, _ = outward.shape
    width = out.shape[2]
    kept = sensors // 2
    span = pl.ds(pl.multiple_of(half * kept, kept), kept)
    for step in range(0, steps, 2):
        acc = jnp.concatenate([start[step, span, :], start[step + 1, span, :]], axis=1)
        for lag in range(step + 2):
            left = outward[lag, span, :]
            acc = acc + jnp.dot(left, pairs[step + 1 - lag], preferred_element_type=jnp.float32)
        out[step] = acc[:, 0:width].astype(out.dtype)
        out[step + 1] = acc[:, width : 2 * width].astype(out.dtype)


def leaving_kernel(
    twin, top, bottom, diag, couple, ctop, cbottom, edges, scaled, outward, start, out, pairs, line, wide, mix
):
    steps = outward.shape[0]
    cols, width = edges.shape[2], edges.shape[3]
    spread((diag, couple), (ctop, cbottom), line, wide)
    mix_coefs(wide, mix)
    pairs[0, :, 0:width] = jnp.zeros((2 * HALO * cols, width), pairs.dtype)

    @pl.loop(0, steps)
    def _(step):
        for side, message in enumerate((top, bottom)):
            added = halo_part(message, step * (HALO * cols), scaled[step, side], mix, side)
            for spot, extra in zip(spots_of(side), added):
                rounded = (edges[step, spot] + extra).astype(pairs.dtype)
                at = spot * cols
                pairs[step, at : at + cols, width : 2 * width] = rounded
                pairs[step + 1, at : at + cols, 0:width] = rounded

    edge_product(1 - twin[0], pairs, outward, start, out)


def leaving(twin, top, bottom, diag, couple, ctop, cbottom, edges, scaled, outward, start):
    steps, sensors, _ = outward.shape
    rows, cols = diag.shape
    width = edges.shape[3]
    return call(
        leaving_kernel,
        "leaving",
        [bf16(steps, sensors // 2, width), bf16(steps + 1, 2 * HALO * cols, 2 * width)],
        [SMEM] + [VMEM] * 10,
        [VMEM] * 2,
        coef_scratch(rows + 2 * HALO, cols, width) + [pltpu.VMEM((2, 8, cols, width), jnp.float32)],
        1,
    )(twin, top, bottom, diag, couple, ctop, cbottom, edges, scaled, outward, start)


def staying_kernel(twin, pairs, outward, start, out):
    edge_product(twin[0], pairs, outward, start, out)


def staying(twin, pairs, outward, start):
    steps, sensors, width = start.shape
    out = f32(steps, sensors // 2, width)
    return call(staying_kernel, "staying", out, [SMEM] + [VMEM] * 3, VMEM, [], 1)(twin, pairs, outward, start)


def join_kernel(mine, got, both):
    both[...] = (mine[...] + got[...].astype(jnp.float32)).astype(both.dtype)


def join(mine, got):
    return call(join_kernel, "join", bf16(*got.shape), [VMEM] * 2, VMEM, [], 1)(mine, got)


def scale_kernel(pieces, prec, out):
    total = pieces[0].astype(jnp.float32)
    for piece in range(1, pieces.shape[0]):
        total = total + pieces[piece].astype(jnp.float32)
    weighted = (total * prec[...]).astype(out.dtype)
    for piece in range(pieces.shape[0]):
        out[piece] = weighted


def scale(pieces, prec):
    return call(scale_kernel, "scale", bf16(*pieces.shape), [VMEM] * 2, VMEM, [], 1)(pieces, prec)


def fill_pairs(twin, mine, other, pairs):
    steps, kept, width = mine.shape
    pairs[steps, :, width : 2 * width] = jnp.zeros((2 * kept, width), pairs.dtype)
    for source, half in ((mine, twin[0]), (other, 1 - twin[0])):
        at = pl.ds(pl.multiple_of(half * kept, kept), kept)
        for step in range(steps):
            pairs[step + 1, at, 0:width] = source[step]
            pairs[step, at, width : 2 * width] = source[step]


def strip_product(rows, turned, pairs, field, message):
    steps, _, cols, sensors = turned.shape
    strip = HALO * cols
    width = message.shape[1]
    for step in range(0, steps, 2):
        acc = None
        for lag in range(steps - step):
            left = turned[lag, rows].reshape(strip, sensors)
            term = jnp.dot(left, pairs[step + lag + 1], preferred_element_type=jnp.float32)
            acc = term if acc is None else acc + term
        for side in range(2):
            part = acc[:, side * width : (side + 1) * width]
            field[step + side] = part.reshape(HALO, cols, width)
            at = (step + side) * strip
            message[at : at + strip, :] = part.astype(message.dtype)


def tail_kernel(twin, mine, other, turned, field, message, pairs):
    rows = turned.shape[1]
    fill_pairs(twin, mine, other, pairs)
    strip_product(slice(rows - HALO, rows), turned, pairs, field, message)


def head_kernel(pairs, turned, _, field, message):
    strip_product(slice(0, HALO), turned, pairs, field, message)


def adjoint_tail(twin, mine, other, turned):
    steps, _, cols, sensors = turned.shape
    width = mine.shape[2]
    return call(
        tail_kernel,
        "adjoint_tail",
        (
            f32(steps, HALO, cols, width),
            bf16(steps * HALO * cols, width),
            bf16(steps + 1, sensors, 2 * width),
        ),
        [SMEM] + [VMEM] * 3,
        [VMEM] * 3,
        [],
        4,
    )(twin, mine, other, turned)


def adjoint_head(pairs, turned, after):
    steps, _, cols, _ = turned.shape
    width = pairs.shape[2] // 2
    return call(
        head_kernel,
        "adjoint_head",
        (f32(steps, HALO, cols, width), bf16(steps * HALO * cols, width)),
        [VMEM, VMEM, HBM],
        [VMEM] * 2,
        [],
        4,
    )(pairs, turned, after)


def inner_kernel(
    pairs, turned, upper, lower, diag, couple, ctop, cbottom, edges, scaled, out, mix, core, line, wide
):
    steps, rows, cols, sensors = turned.shape
    width = core.shape[3]
    inner = rows - 2 * HALO
    pack_at = pl.program_id(0)

    @pl.when(pack_at == 0)
    def _():
        spread((diag, couple), (ctop, cbottom), line, wide)
        mix_coefs(wide, mix)
        for step in range(0, steps, 2):
            acc = None
            for lag in range(steps - step):
                left = turned[lag, HALO : rows - HALO].reshape(inner * cols, sensors)
                term = jnp.dot(left, pairs[step + lag + 1], preferred_element_type=jnp.float32)
                acc = term if acc is None else acc + term
            for side in range(2):
                core[step + side] = acc[:, side * width : (side + 1) * width].reshape(inner, cols, width)

    listed = edge_rows(rows)
    span = out.shape[0]

    @pl.loop(0, span)
    def _(at):
        step = pack_at * span + at

        def load(row):
            if row < HALO:
                return upper[step, row]
            return core[step, row - HALO] if row < rows - HALO else lower[step, row - rows + HALO]

        def store(row, value, weighted):
            if row in listed:
                edges[step, listed.index(row)] = value
            else:
                out[at, row - HALO] = value
            if row == 0:
                scaled[step, 0] = weighted[0]
            if row == rows - 1:
                scaled[step, 1] = weighted[rows - 1]

        own_sweeps(load, wide, rows, store)


def inner(pairs, turned, upper, lower, diag, couple, ctop, cbottom):
    steps, rows, cols, _ = turned.shape
    width = upper.shape[3]
    core = rows - 2 * HALO
    assert core == HALO
    span = steps // 2
    return call(
        inner_kernel,
        "inner",
        (
            f32(steps, 2 * HALO, cols, width),
            f32(steps, 2, cols, width),
            f32(steps, rows, cols, width),
            f32(2, 8, cols, width),
        ),
        [VMEM] * 8,
        [VMEM, VMEM, pl.BlockSpec((span, core, cols, width), lambda step: (step, 1, 0, 0)), VMEM],
        [pltpu.VMEM((steps, core, cols, width), jnp.float32)] + coef_scratch(rows + 2 * HALO, cols, width),
        10,
        (steps // span,),
    )(pairs, turned, upper, lower, diag, couple, ctop, cbottom)


def finish_kernel(side, message, mix, edges, scaled, _, out):
    span, _, cols, _ = out.shape
    first = pl.program_id(0) * span

    @pl.loop(0, span)
    def _(at):
        step = first + at
        added = halo_part(message, step * (HALO * cols), scaled[step, side], mix, side)
        for spot, extra in zip(spots_of(side), added):
            out[at, spot % HALO] = edges[step, spot] + extra


def finish(side, message, mix, edges, scaled, out):
    steps, rows, cols, width = out.shape
    span = steps // 2
    place = side * (rows // HALO - 1)
    return call(
        functools.partial(finish_kernel, side),
        "finish",
        f32(*out.shape),
        [VMEM] * 4 + [HBM],
        pl.BlockSpec((span, HALO, cols, width), lambda step: (step, place, 0, 0)),
        [],
        2,
        (steps // span,),
        {4: 0},
    )(message, mix, edges, scaled, out)


def send_down(tail):
    return lax.ppermute(tail, "tile", [(i, i + 1) for i in range(lax.axis_size("tile") - 1)])


def send_up(head):
    return lax.ppermute(head, "tile", [(i + 1, i) for i in range(lax.axis_size("tile") - 1)])


def swap_twins(value):
    return lax.ppermute(value, "twin", [(0, 1), (1, 0)])


def body(sketch, diag_coef, couple, kernel, noise_prec):
    steps, _, rows, cols, width = sketch.shape
    sensors = kernel.shape[1]
    others = ("tile", "pair")
    groups = lax.axis_size(others)
    twin = lax.axis_index("twin")
    which = twin.reshape(1)
    field = sketch.reshape(steps, rows, cols, width)
    diag, couple = diag_coef.reshape(rows, cols), couple.reshape(rows, cols)
    kern = jnp.transpose(kernel.reshape(steps, sensors, rows, cols), (0, 2, 1, 3))
    kept = sensors // 2
    share = steps * kept // groups

    tail = pack(rows - HALO, field, sketch)
    top = send_down(tail)
    bottom = send_up(pack(0, field, tail))
    coefs = jnp.stack([diag, couple])
    note = send_down(coefs[:, rows - HALO :]), send_up(coefs[:, :HALO])
    noise = lax.dynamic_slice(noise_prec, (0, twin * kept), (steps, kept)).reshape(steps * kept)
    noise = lax.dynamic_slice(noise, (lax.axis_index(others) * share,), (share,))
    prec = jnp.broadcast_to(noise[:, None], (share, width))
    edges, scaled, data, turned, outward = before(field, diag, couple, kern, prec)

    gone, pairs = leaving(which, top, bottom, diag, couple, *note, edges, scaled, outward, data)
    both = join(staying(which, pairs, outward, data), swap_twins(gone)).reshape(groups, share, width)
    pieces = lax.all_to_all(both, others, 0, 0, tiled=True)
    weighted = lax.all_to_all(scale(pieces, prec), others, 0, 0, tiled=True).reshape(steps, kept, width)
    lower, tail, pairs = adjoint_tail(which, weighted, swap_twins(weighted), turned)
    top = send_down(tail)
    upper, head = adjoint_head(pairs, turned, tail)
    bottom = send_up(head)
    edges, scaled, out, mix = inner(pairs, turned, upper, lower, diag, couple, *note)
    out = finish(0, top, mix, edges, scaled, out)
    out = finish(1, bottom, mix, edges, scaled, out)
    return out.reshape(sketch.shape)


def solution(mesh):
    bands, tiles = mesh.shape["band"], mesh.shape["tile"]
    fine = Mesh(mesh.devices.reshape(bands // 2, 2, tiles), ("pair", "twin", "tile"))
    band = ("pair", "twin")
    placed = (
        P(None, band, "tile", None, None),
        P(band, "tile", None),
        P(band, "tile", None),
        P(None, None, band, "tile", None),
        P(),
    )
    return jax.shard_map(
        body,
        mesh=fine,
        in_specs=placed,
        out_specs=P(None, band, "tile", None, None),
        check_vma=False,
    )
```

```python
import functools

import jax
import jax.numpy as jnp
from jax import lax
from jax.experimental import pallas as pl
from jax.experimental.pallas import tpu as pltpu
from jax.sharding import Mesh
from jax.sharding import PartitionSpec as P

MIB = 1 << 20
HALO = 2
VMEM = pl.BlockSpec(memory_space=pltpu.VMEM)
SMEM = pl.BlockSpec(memory_space=pltpu.SMEM)
HBM = pl.BlockSpec(memory_space=pltpu.HBM)


def call(kernel, name, out_shape, in_specs, out_specs, scratch, moved, grid=(), aliases={}, limit=16):
    return pl.pallas_call(
        kernel,
        grid=grid,
        out_shape=out_shape,
        in_specs=in_specs,
        out_specs=out_specs,
        scratch_shapes=scratch,
        input_output_aliases=aliases,
        compiler_params=pltpu.CompilerParams(vmem_limit_bytes=limit * MIB),
        cost_estimate=pl.CostEstimate(flops=0, bytes_accessed=moved * MIB, transcendentals=0),
        name=name,
    )


def f32(*shape):
    return jax.ShapeDtypeStruct(shape, jnp.float32)


def bf16(*shape):
    return jax.ShapeDtypeStruct(shape, jnp.bfloat16)


def edge_rows(rows):
    return [*range(HALO), *range(rows - HALO, rows)]


def beside(w):
    cols = w.shape[0]
    at = lax.broadcasted_iota(jnp.int32, w.shape, 0)
    before = jnp.where(at == 0, 0.0, pltpu.roll(w, 1, 0))
    after = jnp.where(at == cols - 1, 0.0, pltpu.roll(w, cols - 1, 0))
    return before + after


def spread(own, halos, line, wide):
    rows, cols = own[0].shape
    for which in range(2):
        line[...] = jnp.zeros(line.shape, line.dtype)
        for side, halo in enumerate(halos):
            at = side * (HALO + rows)
            line[at : at + HALO, :] = halo[which]
        line[HALO : HALO + rows, :] = own[which][...]
        turned = line[...].T
        for row in range(rows + 2 * HALO):
            wide[which, row] = jnp.broadcast_to(turned[:, row : row + 1], wide.shape[2:])


def mix_coefs(wide, mix):
    total = wide.shape[1]
    for side in range(2):
        far, near, edge, inner = (row if side == 0 else total - 1 - row for row in range(4))
        square = wide[1, edge] * wide[1, edge]
        mix[side, 0] = wide[1, near]
        mix[side, 1] = wide[1, far]
        mix[side, 2] = wide[1, near] * wide[0, near]
        mix[side, 3] = wide[1, near] * wide[1, near]
        mix[side, 4] = -square
        mix[side, 5] = -wide[0, edge] * wide[1, edge]
        mix[side, 6] = wide[1, edge]
        mix[side, 7] = wide[1, inner] * square


def coef_scratch(rows, cols, width):
    return [pltpu.VMEM((cols, cols), jnp.float32), pltpu.VMEM((2, rows, cols, width), jnp.float32)]


def one_sweep(values, scaled, wide, row):
    around = beside(scaled[row])
    if row > 0:
        around = around + scaled[row - 1]
    if row + 1 < len(scaled):
        around = around + scaled[row + 1]
    return wide[0, row + HALO] * values[row] - wide[1, row + HALO] * around


def own_sweeps(load, wide, rows, store):
    values, scaled, first, second = ([None] * rows for _ in range(4))
    for row in range(rows + 2):
        if row < rows:
            values[row] = load(row)
            scaled[row] = wide[1, row + HALO] * values[row]
        if 0 < row <= rows:
            first[row - 1] = one_sweep(values, scaled, wide, row - 1)
            second[row - 1] = wide[1, row - 1 + HALO] * first[row - 1]
        if row > 1:
            store(row - 2, one_sweep(first, second, wide, row - 2), scaled)


def halo_part(message, at, edge_scaled, mix, side):
    cols = edge_scaled.shape[0]
    far_row, near_row = (0, 1) if side == 0 else (1, 0)

    def take(row):
        start = pl.multiple_of(at + row * cols, cols)
        return message[pl.ds(start, cols), :].astype(jnp.float32)

    near = take(near_row)
    scaled = mix[side, 0] * near
    around = mix[side, 1] * take(far_row) + edge_scaled + beside(scaled)
    near_second = mix[side, 2] * near - mix[side, 3] * around
    second = mix[side, 4] * scaled
    on_edge = mix[side, 5] * scaled - mix[side, 6] * (near_second + beside(second))
    return on_edge, mix[side, 7] * scaled


def spots_of(side):
    return (0, 1) if side == 0 else (2 * HALO - 1, 2 * HALO - 2)


def pack_kernel(first, field, _, out, edges, packed, arrived, left):
    steps, rows, cols, width = field.shape
    strip = HALO * cols
    coming, going = [], []
    for step in range(steps):
        source = field.at[step, pl.ds(first, HALO)]
        coming.append(pltpu.make_async_copy(source, edges.at[step], arrived.at[step]))
        coming[step].start()
        going.append(pltpu.make_async_copy(packed.at[step], out.at[pl.ds(step * strip, strip)], left.at[step]))
    for step in range(steps):
        coming[step].wait()
        packed[step] = edges[step].reshape(strip, width).astype(packed.dtype)
        going[step].start()
    for copy in going:
        copy.wait()


def pack(first, field, after):
    steps, rows, cols, width = field.shape
    strip = HALO * cols
    return call(
        functools.partial(pack_kernel, first),
        "pack",
        bf16(steps * strip, width),
        [HBM] * 2,
        HBM,
        [
            pltpu.VMEM((steps, HALO, cols, width), jnp.float32),
            pltpu.VMEM((steps, strip, width), jnp.bfloat16),
            pltpu.SemaphoreType.DMA((steps,)),
            pltpu.SemaphoreType.DMA((steps,)),
        ],
        3,
        limit=62,
    )(field, after)


def before_kernel(field, diag, couple, kern, _, edges, scaled, data, turned, outward, line, wide, pairs):
    steps, rows, cols, width = field.shape
    inner = rows - 2 * HALO
    listed = edge_rows(rows)
    spread((diag, couple), (), line, wide)
    pairs[0, :, 0:width] = jnp.zeros((inner * cols, width), pairs.dtype)

    @pl.loop(0, steps)
    def _(step):
        def store(row, value, weighted):
            if row in listed:
                edges[step, listed.index(row)] = value
            else:
                at = (row - HALO) * cols
                rounded = value.astype(pairs.dtype)
                pairs[step, at : at + cols, width : 2 * width] = rounded
                pairs[step + 1, at : at + cols, 0:width] = rounded
            if row == 0:
                scaled[step, 0] = weighted[0]
            if row == rows - 1:
                scaled[step, 1] = weighted[rows - 1]

        own_sweeps(lambda row: field[step, row], wide, rows, store)

    @pl.loop(0, steps)
    def _(lag):
        for row in range(rows):
            turned[lag, row] = kern[lag, row].T
        for spot, row in enumerate(listed):
            outward[lag, :, spot * cols : (spot + 1) * cols] = kern[lag, row]

    for step in range(0, steps, 2):
        acc = None
        for lag in range(step + 2):
            left = jnp.concatenate([kern[lag, row] for row in range(HALO, rows - HALO)], axis=1)
            term = jnp.dot(left, pairs[step + 1 - lag], preferred_element_type=jnp.float32)
            acc = term if acc is None else acc + term
        data[step] = acc[:, 0:width]
        data[step + 1] = acc[:, width : 2 * width]


def before(field, diag, couple, kern, after):
    steps, rows, cols, width = field.shape
    sensors = kern.shape[2]
    inner = (rows - 2 * HALO) * cols
    return call(
        before_kernel,
        "before",
        (
            f32(steps, 2 * HALO, cols, width),
            f32(steps, 2, cols, width),
            f32(steps, sensors, width),
            bf16(steps, rows, cols, sensors),
            bf16(steps, sensors, 2 * HALO * cols),
        ),
        [VMEM] * 4 + [HBM],
        [VMEM] * 5,
        coef_scratch(rows + 2 * HALO, cols, width) + [pltpu.VMEM((steps + 1, inner, 2 * width), jnp.bfloat16)],
        12,
    )(field, diag, couple, kern, after)


def edge_product(half, pairs, outward, start, out):
    steps, sensors, _ = outward.shape
    width = out.shape[2]
    kept = sensors // 2
    span = pl.ds(pl.multiple_of(half * kept, kept), kept)
    for step in range(0, steps, 2):
        acc = jnp.concatenate([start[step, span, :], start[step + 1, span, :]], axis=1)
        for lag in range(step + 2):
            left = outward[lag, span, :]
            acc = acc + jnp.dot(left, pairs[step + 1 - lag], preferred_element_type=jnp.float32)
        out[step] = acc[:, 0:width].astype(out.dtype)
        out[step + 1] = acc[:, width : 2 * width].astype(out.dtype)


def leaving_kernel(
    twin, top, bottom, diag, couple, ctop, cbottom, edges, scaled, outward, start, out, pairs, line, wide, mix
):
    steps = outward.shape[0]
    cols, width = edges.shape[2], edges.shape[3]
    spread((diag, couple), (ctop, cbottom), line, wide)
    mix_coefs(wide, mix)
    pairs[0, :, 0:width] = jnp.zeros((2 * HALO * cols, width), pairs.dtype)

    @pl.loop(0, steps)
    def _(step):
        for side, message in enumerate((top, bottom)):
            added = halo_part(message, step * (HALO * cols), scaled[step, side], mix, side)
            for spot, extra in zip(spots_of(side), added):
                rounded = (edges[step, spot] + extra).astype(pairs.dtype)
                at = spot * cols
                pairs[step, at : at + cols, width : 2 * width] = rounded
                pairs[step + 1, at : at + cols, 0:width] = rounded

    edge_product(1 - twin[0], pairs, outward, start, out)


def leaving(twin, top, bottom, diag, couple, ctop, cbottom, edges, scaled, outward, start):
    steps, sensors, _ = outward.shape
    rows, cols = diag.shape
    width = edges.shape[3]
    return call(
        leaving_kernel,
        "leaving",
        [bf16(steps, sensors // 2, width), bf16(steps + 1, 2 * HALO * cols, 2 * width)],
        [SMEM] + [VMEM] * 10,
        [VMEM] * 2,
        coef_scratch(rows + 2 * HALO, cols, width) + [pltpu.VMEM((2, 8, cols, width), jnp.float32)],
        1,
    )(twin, top, bottom, diag, couple, ctop, cbottom, edges, scaled, outward, start)


def staying_kernel(twin, pairs, outward, start, out):
    edge_product(twin[0], pairs, outward, start, out)


def staying(twin, pairs, outward, start):
    steps, sensors, width = start.shape
    out = f32(steps, sensors // 2, width)
    return call(staying_kernel, "staying", out, [SMEM] + [VMEM] * 3, VMEM, [], 1)(twin, pairs, outward, start)


def join_kernel(mine, got, both):
    both[...] = (mine[...] + got[...].astype(jnp.float32)).astype(both.dtype)


def join(mine, got):
    return call(join_kernel, "join", bf16(*got.shape), [VMEM] * 2, VMEM, [], 1)(mine, got)


def scale_kernel(pieces, prec, out):
    total = pieces[0].astype(jnp.float32)
    for piece in range(1, pieces.shape[0]):
        total = total + pieces[piece].astype(jnp.float32)
    weighted = (total * prec[...]).astype(out.dtype)
    for piece in range(pieces.shape[0]):
        out[piece] = weighted


def scale(pieces, prec):
    return call(scale_kernel, "scale", bf16(*pieces.shape), [VMEM] * 2, VMEM, [], 1)(pieces, prec)


def fill_pairs(twin, mine, other, pairs):
    groups, share, width = mine.shape
    sensors = pairs.shape[1]
    kept = sensors // 2
    steps = groups * share // kept
    pairs[steps, :, width : 2 * width] = jnp.zeros((sensors, width), pairs.dtype)
    for source, half in ((mine, twin[0]), (other, 1 - twin[0])):
        for piece in range(groups):
            step, first = divmod(piece * share, kept)
            at = pl.ds(pl.multiple_of(half * kept + first, share), share)
            value = source[groups - 1 - piece]
            pairs[step + 1, at, 0:width] = value
            pairs[step, at, width : 2 * width] = value


def strip_product(rows, turned, pairs, field, message):
    steps, _, cols, sensors = turned.shape
    strip = HALO * cols
    width = message.shape[1]
    for step in range(0, steps, 2):
        acc = None
        for lag in range(steps - step):
            left = turned[lag, rows].reshape(strip, sensors)
            term = jnp.dot(left, pairs[step + lag + 1], preferred_element_type=jnp.float32)
            acc = term if acc is None else acc + term
        for side in range(2):
            part = acc[:, side * width : (side + 1) * width]
            field[step + side] = part.reshape(HALO, cols, width)
            at = (step + side) * strip
            message[at : at + strip, :] = part.astype(message.dtype)


def tail_kernel(twin, mine, other, turned, field, message, pairs):
    rows = turned.shape[1]
    fill_pairs(twin, mine, other, pairs)
    strip_product(slice(rows - HALO, rows), turned, pairs, field, message)


def head_kernel(pairs, turned, _, field, message):
    strip_product(slice(0, HALO), turned, pairs, field, message)


def adjoint_tail(twin, mine, other, turned):
    steps, _, cols, sensors = turned.shape
    width = mine.shape[2]
    return call(
        tail_kernel,
        "adjoint_tail",
        (
            f32(steps, HALO, cols, width),
            bf16(steps * HALO * cols, width),
            bf16(steps + 1, sensors, 2 * width),
        ),
        [SMEM] + [VMEM] * 3,
        [VMEM] * 3,
        [],
        4,
    )(twin, mine, other, turned)


def adjoint_head(pairs, turned, after):
    steps, _, cols, _ = turned.shape
    width = pairs.shape[2] // 2
    return call(
        head_kernel,
        "adjoint_head",
        (f32(steps, HALO, cols, width), bf16(steps * HALO * cols, width)),
        [VMEM, VMEM, HBM],
        [VMEM] * 2,
        [],
        4,
    )(pairs, turned, after)


def inner_kernel(
    pairs, turned, upper, lower, diag, couple, ctop, cbottom, edges, scaled, out, mix, core, line, wide
):
    steps, rows, cols, sensors = turned.shape
    width = core.shape[3]
    inner = rows - 2 * HALO
    pack_at = pl.program_id(0)

    @pl.when(pack_at == 0)
    def _():
        spread((diag, couple), (ctop, cbottom), line, wide)
        mix_coefs(wide, mix)
        for step in range(0, steps, 2):
            acc = None
            for lag in range(steps - step):
                left = turned[lag, HALO : rows - HALO].reshape(inner * cols, sensors)
                term = jnp.dot(left, pairs[step + lag + 1], preferred_element_type=jnp.float32)
                acc = term if acc is None else acc + term
            for side in range(2):
                core[step + side] = acc[:, side * width : (side + 1) * width].reshape(inner, cols, width)

    listed = edge_rows(rows)
    span = out.shape[0]

    @pl.loop(0, span)
    def _(at):
        step = pack_at * span + at

        def load(row):
            if row < HALO:
                return upper[step, row]
            return core[step, row - HALO] if row < rows - HALO else lower[step, row - rows + HALO]

        def store(row, value, weighted):
            if row in listed:
                edges[step, listed.index(row)] = value
            else:
                out[at, row - HALO] = value
            if row == 0:
                scaled[step, 0] = weighted[0]
            if row == rows - 1:
                scaled[step, 1] = weighted[rows - 1]

        own_sweeps(load, wide, rows, store)


def inner(pairs, turned, upper, lower, diag, couple, ctop, cbottom):
    steps, rows, cols, _ = turned.shape
    width = upper.shape[3]
    core = rows - 2 * HALO
    assert core == HALO
    span = steps // 2
    return call(
        inner_kernel,
        "inner",
        (
            f32(steps, 2 * HALO, cols, width),
            f32(steps, 2, cols, width),
            f32(steps, rows, cols, width),
            f32(2, 8, cols, width),
        ),
        [VMEM] * 8,
        [VMEM, VMEM, pl.BlockSpec((span, core, cols, width), lambda step: (step, 1, 0, 0)), VMEM],
        [pltpu.VMEM((steps, core, cols, width), jnp.float32)] + coef_scratch(rows + 2 * HALO, cols, width),
        10,
        (steps // span,),
    )(pairs, turned, upper, lower, diag, couple, ctop, cbottom)


def finish_kernel(side, message, mix, edges, scaled, _, out):
    span, _, cols, _ = out.shape
    first = pl.program_id(0) * span

    @pl.loop(0, span)
    def _(at):
        step = first + at
        added = halo_part(message, step * (HALO * cols), scaled[step, side], mix, side)
        for spot, extra in zip(spots_of(side), added):
            out[at, spot % HALO] = edges[step, spot] + extra


def finish(side, message, mix, edges, scaled, out):
    steps, rows, cols, width = out.shape
    span = steps // 2
    place = side * (rows // HALO - 1)
    return call(
        functools.partial(finish_kernel, side),
        "finish",
        f32(*out.shape),
        [VMEM] * 4 + [HBM],
        pl.BlockSpec((span, HALO, cols, width), lambda step: (step, place, 0, 0)),
        [],
        2,
        (steps // span,),
        {4: 0},
    )(message, mix, edges, scaled, out)


def send_down(tail):
    return lax.ppermute(tail, "tile", [(i, i + 1) for i in range(lax.axis_size("tile") - 1)])


def send_up(head):
    return lax.ppermute(head, "tile", [(i + 1, i) for i in range(lax.axis_size("tile") - 1)])


def swap_twins(value):
    return lax.ppermute(value, "twin", [(0, 1), (1, 0)])


def body(sketch, diag_coef, couple, kernel, noise_prec):
    steps, _, rows, cols, width = sketch.shape
    sensors = kernel.shape[1]
    others = ("pair", "tile")
    groups = lax.axis_size(others)
    twin = lax.axis_index("twin")
    which = twin.reshape(1)
    field = sketch.reshape(steps, rows, cols, width)
    diag, couple = diag_coef.reshape(rows, cols), couple.reshape(rows, cols)
    kern = jnp.transpose(kernel.reshape(steps, sensors, rows, cols), (0, 2, 1, 3))
    kept = sensors // 2
    share = steps * kept // groups

    tail = pack(rows - HALO, field, sketch)
    top = send_down(tail)
    bottom = send_up(pack(0, field, tail))
    coefs = jnp.stack([diag, couple])
    note = send_down(coefs[:, rows - HALO :]), send_up(coefs[:, :HALO])
    noise = lax.dynamic_slice(noise_prec, (0, twin * kept), (steps, kept)).reshape(steps * kept)
    noise = lax.dynamic_slice(noise, (lax.axis_index(others) * share,), (share,))
    prec = jnp.broadcast_to(noise[:, None], (share, width))
    edges, scaled, data, turned, outward = before(field, diag, couple, kern, prec)

    gone, pairs = leaving(which, top, bottom, diag, couple, *note, edges, scaled, outward, data)
    both = join(staying(which, pairs, outward, data), swap_twins(gone)).reshape(groups, share, width)
    pieces = lax.all_to_all(both, others, 0, 0, tiled=True)
    backwards = [list(reversed(range(groups)))]
    weighted = lax.all_to_all(scale(pieces, prec), others, 0, 0, axis_index_groups=backwards, tiled=True)
    lower, tail, pairs = adjoint_tail(which, weighted, swap_twins(weighted), turned)
    top = send_down(tail)
    upper, head = adjoint_head(pairs, turned, tail)
    bottom = send_up(head)
    edges, scaled, out, mix = inner(pairs, turned, upper, lower, diag, couple, *note)
    out = finish(0, top, mix, edges, scaled, out)
    out = finish(1, bottom, mix, edges, scaled, out)
    return out.reshape(sketch.shape)


def solution(mesh):
    bands, tiles = mesh.shape["band"], mesh.shape["tile"]
    fine = Mesh(mesh.devices.reshape(bands // 2, 2, tiles), ("pair", "twin", "tile"))
    band = ("pair", "twin")
    placed = (
        P(None, band, "tile", None, None),
        P(band, "tile", None),
        P(band, "tile", None),
        P(None, None, band, "tile", None),
        P(),
    )
    return jax.shard_map(
        body,
        mesh=fine,
        in_specs=placed,
        out_specs=P(None, band, "tile", None, None),
        check_vma=False,
    )
```

```python
import functools

import jax
import jax.numpy as jnp
from jax import lax
from jax.experimental import pallas as pl
from jax.experimental.pallas import tpu as pltpu
from jax.sharding import Mesh
from jax.sharding import PartitionSpec as P

MIB = 1 << 20
HALO = 2
VMEM = pl.BlockSpec(memory_space=pltpu.VMEM)
SMEM = pl.BlockSpec(memory_space=pltpu.SMEM)
HBM = pl.BlockSpec(memory_space=pltpu.HBM)


def call(kernel, name, out_shape, in_specs, out_specs, scratch, moved, grid=(), aliases={}, limit=16):
    return pl.pallas_call(
        kernel,
        grid=grid,
        out_shape=out_shape,
        in_specs=in_specs,
        out_specs=out_specs,
        scratch_shapes=scratch,
        input_output_aliases=aliases,
        compiler_params=pltpu.CompilerParams(vmem_limit_bytes=limit * MIB),
        cost_estimate=pl.CostEstimate(flops=0, bytes_accessed=moved * MIB, transcendentals=0),
        name=name,
    )


def f32(*shape):
    return jax.ShapeDtypeStruct(shape, jnp.float32)


def bf16(*shape):
    return jax.ShapeDtypeStruct(shape, jnp.bfloat16)


def edge_rows(rows):
    return [*range(HALO), *range(rows - HALO, rows)]


def beside(w):
    cols = w.shape[0]
    at = lax.broadcasted_iota(jnp.int32, w.shape, 0)
    before = jnp.where(at == 0, 0.0, pltpu.roll(w, 1, 0))
    after = jnp.where(at == cols - 1, 0.0, pltpu.roll(w, cols - 1, 0))
    return before + after


def spread(own, halos, line, wide):
    rows, cols = own[0].shape
    for which in range(2):
        line[...] = jnp.zeros(line.shape, line.dtype)
        for side, halo in enumerate(halos):
            at = side * (HALO + rows)
            line[at : at + HALO, :] = halo[which]
        line[HALO : HALO + rows, :] = own[which][...]
        turned = line[...].T
        for row in range(rows + 2 * HALO):
            wide[which, row] = jnp.broadcast_to(turned[:, row : row + 1], wide.shape[2:])


def mix_coefs(wide, mix):
    total = wide.shape[1]
    for side in range(2):
        far, near, edge, inner = (row if side == 0 else total - 1 - row for row in range(4))
        square = wide[1, edge] * wide[1, edge]
        mix[side, 0] = wide[1, near]
        mix[side, 1] = wide[1, far]
        mix[side, 2] = wide[1, near] * wide[0, near]
        mix[side, 3] = wide[1, near] * wide[1, near]
        mix[side, 4] = -square
        mix[side, 5] = -wide[0, edge] * wide[1, edge]
        mix[side, 6] = wide[1, edge]
        mix[side, 7] = wide[1, inner] * square


def coef_scratch(rows, cols, width):
    return [pltpu.VMEM((cols, cols), jnp.float32), pltpu.VMEM((2, rows, cols, width), jnp.float32)]


def one_sweep(values, scaled, wide, row):
    around = beside(scaled[row])
    if row > 0:
        around = around + scaled[row - 1]
    if row + 1 < len(scaled):
        around = around + scaled[row + 1]
    return wide[0, row + HALO] * values[row] - wide[1, row + HALO] * around


def own_sweeps(load, wide, rows, store):
    values, scaled, first, second = ([None] * rows for _ in range(4))
    for row in range(rows + 2):
        if row < rows:
            values[row] = load(row)
            scaled[row] = wide[1, row + HALO] * values[row]
        if 0 < row <= rows:
            first[row - 1] = one_sweep(values, scaled, wide, row - 1)
            second[row - 1] = wide[1, row - 1 + HALO] * first[row - 1]
        if row > 1:
            store(row - 2, one_sweep(first, second, wide, row - 2), scaled)


def halo_part(message, at, edge_scaled, mix, side):
    cols = edge_scaled.shape[0]
    far_row, near_row = (0, 1) if side == 0 else (1, 0)

    def take(row):
        start = pl.multiple_of(at + row * cols, cols)
        return message[pl.ds(start, cols), :].astype(jnp.float32)

    near = take(near_row)
    scaled = mix[side, 0] * near
    around = mix[side, 1] * take(far_row) + edge_scaled + beside(scaled)
    near_second = mix[side, 2] * near - mix[side, 3] * around
    second = mix[side, 4] * scaled
    on_edge = mix[side, 5] * scaled - mix[side, 6] * (near_second + beside(second))
    return on_edge, mix[side, 7] * scaled


def spots_of(side):
    return (0, 1) if side == 0 else (2 * HALO - 1, 2 * HALO - 2)


def pack_kernel(first, field, _, out, edges, packed, arrived, left):
    steps, rows, cols, width = field.shape
    strip = HALO * cols
    coming, going = [], []
    for step in range(steps):
        source = field.at[step, pl.ds(first, HALO)]
        coming.append(pltpu.make_async_copy(source, edges.at[step], arrived.at[step]))
        coming[step].start()
        going.append(pltpu.make_async_copy(packed.at[step], out.at[pl.ds(step * strip, strip)], left.at[step]))
    for step in range(steps):
        coming[step].wait()
        packed[step] = edges[step].reshape(strip, width).astype(packed.dtype)
        going[step].start()
    for copy in going:
        copy.wait()


def pack(first, field, after):
    steps, rows, cols, width = field.shape
    strip = HALO * cols
    return call(
        functools.partial(pack_kernel, first),
        "pack",
        bf16(steps * strip, width),
        [HBM] * 2,
        HBM,
        [
            pltpu.VMEM((steps, HALO, cols, width), jnp.float32),
            pltpu.VMEM((steps, strip, width), jnp.bfloat16),
            pltpu.SemaphoreType.DMA((steps,)),
            pltpu.SemaphoreType.DMA((steps,)),
        ],
        3,
        limit=62,
    )(field, after)


def before_kernel(field, diag, couple, kern, _, edges, scaled, data, turned, outward, line, wide, pairs):
    steps, rows, cols, width = field.shape
    inner = rows - 2 * HALO
    listed = edge_rows(rows)
    spread((diag, couple), (), line, wide)
    pairs[0, :, 0:width] = jnp.zeros((inner * cols, width), pairs.dtype)

    @pl.loop(0, steps)
    def _(step):
        def store(row, value, weighted):
            if row in listed:
                edges[step, listed.index(row)] = value
            else:
                at = (row - HALO) * cols
                rounded = value.astype(pairs.dtype)
                pairs[step, at : at + cols, width : 2 * width] = rounded
                pairs[step + 1, at : at + cols, 0:width] = rounded
            if row == 0:
                scaled[step, 0] = weighted[0]
            if row == rows - 1:
                scaled[step, 1] = weighted[rows - 1]

        own_sweeps(lambda row: field[step, row], wide, rows, store)

    @pl.loop(0, steps)
    def _(lag):
        for row in range(rows):
            turned[lag, row] = kern[lag, row].T
        for spot, row in enumerate(listed):
            outward[lag, :, spot * cols : (spot + 1) * cols] = kern[lag, row]

    for step in range(0, steps, 2):
        acc = None
        for lag in range(step + 2):
            left = jnp.concatenate([kern[lag, row] for row in range(HALO, rows - HALO)], axis=1)
            term = jnp.dot(left, pairs[step + 1 - lag], preferred_element_type=jnp.float32)
            acc = term if acc is None else acc + term
        data[step] = acc[:, 0:width]
        data[step + 1] = acc[:, width : 2 * width]


def before(field, diag, couple, kern, after):
    steps, rows, cols, width = field.shape
    sensors = kern.shape[2]
    inner = (rows - 2 * HALO) * cols
    return call(
        before_kernel,
        "before",
        (
            f32(steps, 2 * HALO, cols, width),
            f32(steps, 2, cols, width),
            f32(steps, sensors, width),
            bf16(steps, rows, cols, sensors),
            bf16(steps, sensors, 2 * HALO * cols),
        ),
        [VMEM] * 4 + [HBM],
        [VMEM] * 5,
        coef_scratch(rows + 2 * HALO, cols, width) + [pltpu.VMEM((steps + 1, inner, 2 * width), jnp.bfloat16)],
        12,
    )(field, diag, couple, kern, after)


def edge_product(half, pairs, outward, start, out):
    steps, sensors, _ = outward.shape
    width = out.shape[2]
    kept = sensors // 2
    span = pl.ds(pl.multiple_of(half * kept, kept), kept)
    for step in range(0, steps, 2):
        acc = jnp.concatenate([start[step, span, :], start[step + 1, span, :]], axis=1)
        for lag in range(step + 2):
            left = outward[lag, span, :]
            acc = acc + jnp.dot(left, pairs[step + 1 - lag], preferred_element_type=jnp.float32)
        out[step] = acc[:, 0:width].astype(out.dtype)
        out[step + 1] = acc[:, width : 2 * width].astype(out.dtype)


def leaving_kernel(
    twin, top, bottom, diag, couple, ctop, cbottom, edges, scaled, outward, start, out, pairs, line, wide, mix
):
    steps = outward.shape[0]
    cols, width = edges.shape[2], edges.shape[3]
    spread((diag, couple), (ctop, cbottom), line, wide)
    mix_coefs(wide, mix)
    pairs[0, :, 0:width] = jnp.zeros((2 * HALO * cols, width), pairs.dtype)

    @pl.loop(0, steps)
    def _(step):
        for side, message in enumerate((top, bottom)):
            added = halo_part(message, step * (HALO * cols), scaled[step, side], mix, side)
            for spot, extra in zip(spots_of(side), added):
                rounded = (edges[step, spot] + extra).astype(pairs.dtype)
                at = spot * cols
                pairs[step, at : at + cols, width : 2 * width] = rounded
                pairs[step + 1, at : at + cols, 0:width] = rounded

    edge_product(1 - twin[0], pairs, outward, start, out)


def leaving(twin, top, bottom, diag, couple, ctop, cbottom, edges, scaled, outward, start):
    steps, sensors, _ = outward.shape
    rows, cols = diag.shape
    width = edges.shape[3]
    return call(
        leaving_kernel,
        "leaving",
        [bf16(steps, sensors // 2, width), bf16(steps + 1, 2 * HALO * cols, 2 * width)],
        [SMEM] + [VMEM] * 10,
        [VMEM] * 2,
        coef_scratch(rows + 2 * HALO, cols, width) + [pltpu.VMEM((2, 8, cols, width), jnp.float32)],
        1,
    )(twin, top, bottom, diag, couple, ctop, cbottom, edges, scaled, outward, start)


def staying_kernel(twin, pairs, outward, start, out):
    edge_product(twin[0], pairs, outward, start, out)


def staying(twin, pairs, outward, start):
    steps, sensors, width = start.shape
    out = f32(steps, sensors // 2, width)
    return call(staying_kernel, "staying", out, [SMEM] + [VMEM] * 3, VMEM, [], 1)(twin, pairs, outward, start)


def join_kernel(mine, got, both):
    both[...] = (mine[...] + got[...].astype(jnp.float32)).astype(both.dtype)


def join(mine, got):
    return call(join_kernel, "join", bf16(*got.shape), [VMEM] * 2, VMEM, [], 1)(mine, got)


def scale_kernel(pieces, prec, out):
    total = pieces[0].astype(jnp.float32)
    for piece in range(1, pieces.shape[0]):
        total = total + pieces[piece].astype(jnp.float32)
    weighted = (total * prec[...]).astype(out.dtype)
    for piece in range(pieces.shape[0]):
        out[piece] = weighted


def scale(pieces, prec):
    return call(scale_kernel, "scale", bf16(*pieces.shape), [VMEM] * 2, VMEM, [], 1)(pieces, prec)


def fill_half(source, pairs):
    groups, share, width = source.shape
    kept = pairs.shape[1]
    steps = groups * share // kept
    pairs[steps, :, width : 2 * width] = jnp.zeros((kept, width), pairs.dtype)
    for piece in range(groups):
        step, first = divmod(piece * share, kept)
        value = source[groups - 1 - piece]
        pairs[step + 1, first : first + share, 0:width] = value
        pairs[step, first : first + share, width : 2 * width] = value


def half_product(rows, turned, half, pairs, step, acc):
    steps, _, cols, sensors = turned.shape
    kept = sensors // 2
    span = pl.ds(pl.multiple_of(half * kept, kept), kept)
    for lag in range(steps - step):
        left = turned[lag, rows, :, span].reshape((rows.stop - rows.start) * cols, kept)
        term = jnp.dot(left, pairs[step + lag + 1], preferred_element_type=jnp.float32)
        acc = term if acc is None else acc + term
    return acc


def strip_product(rows, turned, half, pairs, begun, field, message):
    steps, _, cols, _ = turned.shape
    strip = HALO * cols
    width = message.shape[1]
    for step in range(0, steps, 2):
        acc = half_product(rows, turned, half, pairs, step, begun[step // 2])
        for side in range(2):
            part = acc[:, side * width : (side + 1) * width]
            field[step + side] = part.reshape(HALO, cols, width)
            at = (step + side) * strip
            message[at : at + strip, :] = part.astype(message.dtype)


def own_kernel(twin, mine, turned, tail, head, pairs):
    steps, rows = turned.shape[0], turned.shape[1]
    fill_half(mine, pairs)
    for strip, out in ((slice(rows - HALO, rows), tail), (slice(0, HALO), head)):
        for step in range(0, steps, 2):
            out[step // 2] = half_product(strip, turned, twin[0], pairs, step, None)


def adjoint_own(twin, mine, turned):
    steps, _, cols, sensors = turned.shape
    width = mine.shape[2]
    strip = f32(steps // 2, HALO * cols, 2 * width)
    return call(
        own_kernel,
        "adjoint_own",
        (strip, strip, bf16(steps + 1, sensors // 2, 2 * width)),
        [SMEM] + [VMEM] * 2,
        [VMEM] * 3,
        [],
        4,
    )(twin, mine, turned)


def tail_kernel(twin, other, turned, begun, field, message, pairs):
    rows = turned.shape[1]
    fill_half(other, pairs)
    strip_product(slice(rows - HALO, rows), turned, 1 - twin[0], pairs, begun, field, message)


def head_kernel(twin, pairs, turned, begun, _, field, message):
    strip_product(slice(0, HALO), turned, 1 - twin[0], pairs, begun, field, message)


def adjoint_tail(twin, other, turned, begun):
    steps, _, cols, sensors = turned.shape
    width = other.shape[2]
    return call(
        tail_kernel,
        "adjoint_tail",
        (
            f32(steps, HALO, cols, width),
            bf16(steps * HALO * cols, width),
            bf16(steps + 1, sensors // 2, 2 * width),
        ),
        [SMEM] + [VMEM] * 3,
        [VMEM] * 3,
        [],
        4,
    )(twin, other, turned, begun)


def adjoint_head(twin, pairs, turned, begun, after):
    steps, _, cols, _ = turned.shape
    width = pairs.shape[2] // 2
    return call(
        head_kernel,
        "adjoint_head",
        (f32(steps, HALO, cols, width), bf16(steps * HALO * cols, width)),
        [SMEM, VMEM, VMEM, VMEM, HBM],
        [VMEM] * 2,
        [],
        4,
    )(twin, pairs, turned, begun, after)


def inner_kernel(
    twin, own, got, turned, upper, lower, diag, couple, ctop, cbottom, edges, scaled, out, mix, core, line, wide
):
    steps, rows, cols, sensors = turned.shape
    width = core.shape[3]
    inner = rows - 2 * HALO
    pack_at = pl.program_id(0)

    @pl.when(pack_at == 0)
    def _():
        spread((diag, couple), (ctop, cbottom), line, wide)
        mix_coefs(wide, mix)
        for step in range(0, steps, 2):
            acc = None
            for pairs, half in ((own, twin[0]), (got, 1 - twin[0])):
                acc = half_product(slice(HALO, rows - HALO), turned, half, pairs, step, acc)
            for side in range(2):
                core[step + side] = acc[:, side * width : (side + 1) * width].reshape(inner, cols, width)

    listed = edge_rows(rows)
    span = out.shape[0]

    @pl.loop(0, span)
    def _(at):
        step = pack_at * span + at

        def load(row):
            if row < HALO:
                return upper[step, row]
            return core[step, row - HALO] if row < rows - HALO else lower[step, row - rows + HALO]

        def store(row, value, weighted):
            if row in listed:
                edges[step, listed.index(row)] = value
            else:
                out[at, row - HALO] = value
            if row == 0:
                scaled[step, 0] = weighted[0]
            if row == rows - 1:
                scaled[step, 1] = weighted[rows - 1]

        own_sweeps(load, wide, rows, store)


def inner(twin, own, got, turned, upper, lower, diag, couple, ctop, cbottom):
    steps, rows, cols, _ = turned.shape
    width = upper.shape[3]
    core = rows - 2 * HALO
    assert core == HALO
    span = steps // 2
    return call(
        inner_kernel,
        "inner",
        (
            f32(steps, 2 * HALO, cols, width),
            f32(steps, 2, cols, width),
            f32(steps, rows, cols, width),
            f32(2, 8, cols, width),
        ),
        [SMEM] + [VMEM] * 9,
        [VMEM, VMEM, pl.BlockSpec((span, core, cols, width), lambda step: (step, 1, 0, 0)), VMEM],
        [pltpu.VMEM((steps, core, cols, width), jnp.float32)] + coef_scratch(rows + 2 * HALO, cols, width),
        10,
        (steps // span,),
    )(twin, own, got, turned, upper, lower, diag, couple, ctop, cbottom)


def finish_kernel(side, message, mix, edges, scaled, _, out):
    span, _, cols, _ = out.shape
    first = pl.program_id(0) * span

    @pl.loop(0, span)
    def _(at):
        step = first + at
        added = halo_part(message, step * (HALO * cols), scaled[step, side], mix, side)
        for spot, extra in zip(spots_of(side), added):
            out[at, spot % HALO] = edges[step, spot] + extra


def finish(side, message, mix, edges, scaled, out):
    steps, rows, cols, width = out.shape
    span = steps // 2
    place = side * (rows // HALO - 1)
    return call(
        functools.partial(finish_kernel, side),
        "finish",
        f32(*out.shape),
        [VMEM] * 4 + [HBM],
        pl.BlockSpec((span, HALO, cols, width), lambda step: (step, place, 0, 0)),
        [],
        2,
        (steps // span,),
        {4: 0},
    )(message, mix, edges, scaled, out)


def send_down(tail):
    return lax.ppermute(tail, "tile", [(i, i + 1) for i in range(lax.axis_size("tile") - 1)])


def send_up(head):
    return lax.ppermute(head, "tile", [(i + 1, i) for i in range(lax.axis_size("tile") - 1)])


def swap_twins(value):
    return lax.ppermute(value, "twin", [(0, 1), (1, 0)])


def body(sketch, diag_coef, couple, kernel, noise_prec):
    steps, _, rows, cols, width = sketch.shape
    sensors = kernel.shape[1]
    others = ("pair", "tile")
    groups = lax.axis_size(others)
    twin = lax.axis_index("twin")
    which = twin.reshape(1)
    field = sketch.reshape(steps, rows, cols, width)
    diag, couple = diag_coef.reshape(rows, cols), couple.reshape(rows, cols)
    kern = jnp.transpose(kernel.reshape(steps, sensors, rows, cols), (0, 2, 1, 3))
    kept = sensors // 2
    share = steps * kept // groups

    tail = pack(rows - HALO, field, sketch)
    top = send_down(tail)
    bottom = send_up(pack(0, field, tail))
    coefs = jnp.stack([diag, couple])
    note = send_down(coefs[:, rows - HALO :]), send_up(coefs[:, :HALO])
    noise = lax.dynamic_slice(noise_prec, (0, twin * kept), (steps, kept)).reshape(steps * kept)
    noise = lax.dynamic_slice(noise, (lax.axis_index(others) * share,), (share,))
    prec = jnp.broadcast_to(noise[:, None], (share, width))
    edges, scaled, data, turned, outward = before(field, diag, couple, kern, prec)

    gone, pairs = leaving(which, top, bottom, diag, couple, *note, edges, scaled, outward, data)
    both = join(staying(which, pairs, outward, data), swap_twins(gone)).reshape(groups, share, width)
    pieces = lax.all_to_all(both, others, 0, 0, tiled=True)
    backwards = [list(reversed(range(groups)))]
    weighted = lax.all_to_all(scale(pieces, prec), others, 0, 0, axis_index_groups=backwards, tiled=True)
    other = swap_twins(weighted)
    tail, head, own = adjoint_own(which, weighted, turned)
    lower, tail, got = adjoint_tail(which, other, turned, tail)
    top = send_down(tail)
    upper, head = adjoint_head(which, got, turned, head, tail)
    bottom = send_up(head)
    edges, scaled, out, mix = inner(which, own, got, turned, upper, lower, diag, couple, *note)
    out = finish(0, top, mix, edges, scaled, out)
    out = finish(1, bottom, mix, edges, scaled, out)
    return out.reshape(sketch.shape)


def solution(mesh):
    bands, tiles = mesh.shape["band"], mesh.shape["tile"]
    fine = Mesh(mesh.devices.reshape(bands // 2, 2, tiles), ("pair", "twin", "tile"))
    band = ("pair", "twin")
    placed = (
        P(None, band, "tile", None, None),
        P(band, "tile", None),
        P(band, "tile", None),
        P(None, None, band, "tile", None),
        P(),
    )
    return jax.shard_map(
        body,
        mesh=fine,
        in_specs=placed,
        out_specs=P(None, band, "tile", None, None),
        check_vma=False,
    )
```

```python
import functools

import jax
import jax.numpy as jnp
from jax import lax
from jax.experimental import pallas as pl
from jax.experimental.pallas import tpu as pltpu
from jax.sharding import Mesh
from jax.sharding import PartitionSpec as P

MIB = 1 << 20
HALO = 2
VMEM = pl.BlockSpec(memory_space=pltpu.VMEM)
SMEM = pl.BlockSpec(memory_space=pltpu.SMEM)
HBM = pl.BlockSpec(memory_space=pltpu.HBM)


def call(kernel, name, out_shape, in_specs, out_specs, scratch, moved, grid=(), aliases={}, limit=16):
    return pl.pallas_call(
        kernel,
        grid=grid,
        out_shape=out_shape,
        in_specs=in_specs,
        out_specs=out_specs,
        scratch_shapes=scratch,
        input_output_aliases=aliases,
        compiler_params=pltpu.CompilerParams(vmem_limit_bytes=limit * MIB),
        cost_estimate=pl.CostEstimate(flops=0, bytes_accessed=moved * MIB, transcendentals=0),
        name=name,
    )


def f32(*shape):
    return jax.ShapeDtypeStruct(shape, jnp.float32)


def bf16(*shape):
    return jax.ShapeDtypeStruct(shape, jnp.bfloat16)


def edge_rows(rows):
    return [*range(HALO), *range(rows - HALO, rows)]


def beside(w):
    cols = w.shape[0]
    at = lax.broadcasted_iota(jnp.int32, w.shape, 0)
    before = jnp.where(at == 0, 0.0, pltpu.roll(w, 1, 0))
    after = jnp.where(at == cols - 1, 0.0, pltpu.roll(w, cols - 1, 0))
    return before + after


def spread(own, halos, line, wide):
    rows, cols = own[0].shape
    for which in range(2):
        line[...] = jnp.zeros(line.shape, line.dtype)
        for side, halo in enumerate(halos):
            at = side * (HALO + rows)
            line[at : at + HALO, :] = halo[which]
        line[HALO : HALO + rows, :] = own[which][...]
        turned = line[...].T
        for row in range(rows + 2 * HALO):
            wide[which, row] = jnp.broadcast_to(turned[:, row : row + 1], wide.shape[2:])


def mix_coefs(wide, mix):
    total = wide.shape[1]
    for side in range(2):
        far, near, edge, inner = (row if side == 0 else total - 1 - row for row in range(4))
        square = wide[1, edge] * wide[1, edge]
        mix[side, 0] = wide[1, near]
        mix[side, 1] = wide[1, far]
        mix[side, 2] = wide[1, near] * wide[0, near]
        mix[side, 3] = wide[1, near] * wide[1, near]
        mix[side, 4] = -square
        mix[side, 5] = -wide[0, edge] * wide[1, edge]
        mix[side, 6] = wide[1, edge]
        mix[side, 7] = wide[1, inner] * square


def coef_scratch(rows, cols, width):
    return [pltpu.VMEM((cols, cols), jnp.float32), pltpu.VMEM((2, rows, cols, width), jnp.float32)]


def one_sweep(values, scaled, wide, row):
    around = beside(scaled[row])
    if row > 0:
        around = around + scaled[row - 1]
    if row + 1 < len(scaled):
        around = around + scaled[row + 1]
    return wide[0, row + HALO] * values[row] - wide[1, row + HALO] * around


def own_sweeps(load, wide, rows, store):
    values, scaled, first, second = ([None] * rows for _ in range(4))
    for row in range(rows + 2):
        if row < rows:
            values[row] = load(row)
            scaled[row] = wide[1, row + HALO] * values[row]
        if 0 < row <= rows:
            first[row - 1] = one_sweep(values, scaled, wide, row - 1)
            second[row - 1] = wide[1, row - 1 + HALO] * first[row - 1]
        if row > 1:
            store(row - 2, one_sweep(first, second, wide, row - 2), scaled)


def halo_part(message, at, edge_scaled, mix, side):
    cols = edge_scaled.shape[0]
    far_row, near_row = (0, 1) if side == 0 else (1, 0)

    def take(row):
        start = pl.multiple_of(at + row * cols, cols)
        return message[pl.ds(start, cols), :].astype(jnp.float32)

    near = take(near_row)
    scaled = mix[side, 0] * near
    around = mix[side, 1] * take(far_row) + edge_scaled + beside(scaled)
    near_second = mix[side, 2] * near - mix[side, 3] * around
    second = mix[side, 4] * scaled
    on_edge = mix[side, 5] * scaled - mix[side, 6] * (near_second + beside(second))
    return on_edge, mix[side, 7] * scaled


def spots_of(side):
    return (0, 1) if side == 0 else (2 * HALO - 1, 2 * HALO - 2)


def pack_kernel(first, field, _, out, edges, packed, arrived, left):
    steps, rows, cols, width = field.shape
    strip = HALO * cols
    coming, going = [], []
    for step in range(steps):
        source = field.at[step, pl.ds(first, HALO)]
        coming.append(pltpu.make_async_copy(source, edges.at[step], arrived.at[step]))
        coming[step].start()
        going.append(pltpu.make_async_copy(packed.at[step], out.at[pl.ds(step * strip, strip)], left.at[step]))
    for step in range(steps):
        coming[step].wait()
        packed[step] = edges[step].reshape(strip, width).astype(packed.dtype)
        going[step].start()
    for copy in going:
        copy.wait()


def pack(first, field, after):
    steps, rows, cols, width = field.shape
    strip = HALO * cols
    return call(
        functools.partial(pack_kernel, first),
        "pack",
        bf16(steps * strip, width),
        [HBM] * 2,
        HBM,
        [
            pltpu.VMEM((steps, HALO, cols, width), jnp.float32),
            pltpu.VMEM((steps, strip, width), jnp.bfloat16),
            pltpu.SemaphoreType.DMA((steps,)),
            pltpu.SemaphoreType.DMA((steps,)),
        ],
        3,
        limit=62,
    )(field, after)


def before_kernel(field, diag, couple, kern, _, edges, scaled, data, turned, outward, line, wide, pairs):
    steps, rows, cols, width = field.shape
    inner = rows - 2 * HALO
    listed = edge_rows(rows)
    spread((diag, couple), (), line, wide)
    pairs[0, :, 0:width] = jnp.zeros((inner * cols, width), pairs.dtype)

    @pl.loop(0, steps)
    def _(step):
        def store(row, value, weighted):
            if row in listed:
                edges[step, listed.index(row)] = value
            else:
                at = (row - HALO) * cols
                rounded = value.astype(pairs.dtype)
                pairs[step, at : at + cols, width : 2 * width] = rounded
                pairs[step + 1, at : at + cols, 0:width] = rounded
            if row == 0:
                scaled[step, 0] = weighted[0]
            if row == rows - 1:
                scaled[step, 1] = weighted[rows - 1]

        own_sweeps(lambda row: field[step, row], wide, rows, store)

    @pl.loop(0, steps)
    def _(lag):
        for row in range(rows):
            turned[lag, row] = kern[lag, row].T
        for spot, row in enumerate(listed):
            outward[lag, :, spot * cols : (spot + 1) * cols] = kern[lag, row]

    for step in range(0, steps, 2):
        acc = None
        for lag in range(step + 2):
            left = jnp.concatenate([kern[lag, row] for row in range(HALO, rows - HALO)], axis=1)
            term = jnp.dot(left, pairs[step + 1 - lag], preferred_element_type=jnp.float32)
            acc = term if acc is None else acc + term
        data[step] = acc[:, 0:width]
        data[step + 1] = acc[:, width : 2 * width]


def before(field, diag, couple, kern, after):
    steps, rows, cols, width = field.shape
    sensors = kern.shape[2]
    inner = (rows - 2 * HALO) * cols
    return call(
        before_kernel,
        "before",
        (
            f32(steps, 2 * HALO, cols, width),
            f32(steps, 2, cols, width),
            f32(steps, sensors, width),
            bf16(steps, rows, cols, sensors),
            bf16(steps, sensors, 2 * HALO * cols),
        ),
        [VMEM] * 4 + [HBM],
        [VMEM] * 5,
        coef_scratch(rows + 2 * HALO, cols, width) + [pltpu.VMEM((steps + 1, inner, 2 * width), jnp.bfloat16)],
        12,
    )(field, diag, couple, kern, after)


def edge_product(half, pairs, outward, start, out):
    steps, sensors, _ = outward.shape
    width = out.shape[2]
    kept = sensors // 2
    span = pl.ds(pl.multiple_of(half * kept, kept), kept)
    for step in range(0, steps, 2):
        acc = jnp.concatenate([start[step, span, :], start[step + 1, span, :]], axis=1)
        for lag in range(step + 2):
            left = outward[lag, span, :]
            acc = acc + jnp.dot(left, pairs[step + 1 - lag], preferred_element_type=jnp.float32)
        out[step] = acc[:, 0:width].astype(out.dtype)
        out[step + 1] = acc[:, width : 2 * width].astype(out.dtype)


def leaving_kernel(
    twin, top, bottom, diag, couple, ctop, cbottom, edges, scaled, outward, start, out, pairs, line, wide, mix
):
    steps = outward.shape[0]
    cols, width = edges.shape[2], edges.shape[3]
    spread((diag, couple), (ctop, cbottom), line, wide)
    mix_coefs(wide, mix)
    pairs[0, :, 0:width] = jnp.zeros((2 * HALO * cols, width), pairs.dtype)

    @pl.loop(0, steps)
    def _(step):
        for side, message in enumerate((top, bottom)):
            added = halo_part(message, step * (HALO * cols), scaled[step, side], mix, side)
            for spot, extra in zip(spots_of(side), added):
                rounded = (edges[step, spot] + extra).astype(pairs.dtype)
                at = spot * cols
                pairs[step, at : at + cols, width : 2 * width] = rounded
                pairs[step + 1, at : at + cols, 0:width] = rounded

    edge_product(1 - twin[0], pairs, outward, start, out)


def leaving(twin, top, bottom, diag, couple, ctop, cbottom, edges, scaled, outward, start):
    steps, sensors, _ = outward.shape
    rows, cols = diag.shape
    width = edges.shape[3]
    return call(
        leaving_kernel,
        "leaving",
        [bf16(steps, sensors // 2, width), bf16(steps + 1, 2 * HALO * cols, 2 * width)],
        [SMEM] + [VMEM] * 10,
        [VMEM] * 2,
        coef_scratch(rows + 2 * HALO, cols, width) + [pltpu.VMEM((2, 8, cols, width), jnp.float32)],
        1,
    )(twin, top, bottom, diag, couple, ctop, cbottom, edges, scaled, outward, start)


def staying_kernel(twin, pairs, outward, start, out):
    edge_product(twin[0], pairs, outward, start, out)


def staying(twin, pairs, outward, start):
    steps, sensors, width = start.shape
    out = f32(steps, sensors // 2, width)
    return call(staying_kernel, "staying", out, [SMEM] + [VMEM] * 3, VMEM, [], 1)(twin, pairs, outward, start)


def join_kernel(mine, got, both):
    both[...] = (mine[...] + got[...].astype(jnp.float32)).astype(both.dtype)


def join(mine, got):
    return call(join_kernel, "join", bf16(*got.shape), [VMEM] * 2, VMEM, [], 1)(mine, got)


def scale_kernel(pieces, prec, out):
    total = pieces[0].astype(jnp.float32)
    for piece in range(1, pieces.shape[0]):
        total = total + pieces[piece].astype(jnp.float32)
    weighted = (total * prec[...]).astype(out.dtype)
    for piece in range(pieces.shape[0]):
        out[piece] = weighted


def scale(pieces, prec):
    return call(scale_kernel, "scale", bf16(*pieces.shape), [VMEM] * 2, VMEM, [], 1)(pieces, prec)


def fill_half(source, pairs):
    groups, share, width = source.shape
    kept = pairs.shape[1]
    steps = groups * share // kept
    pairs[steps, :, width : 2 * width] = jnp.zeros((kept, width), pairs.dtype)
    for piece in range(groups):
        step, first = divmod(piece * share, kept)
        value = source[groups - 1 - piece]
        pairs[step + 1, first : first + share, 0:width] = value
        pairs[step, first : first + share, width : 2 * width] = value


def half_product(rows, turned, half, pairs, step, acc):
    steps, _, cols, sensors = turned.shape
    kept = sensors // 2
    span = pl.ds(pl.multiple_of(half * kept, kept), kept)
    for lag in range(steps - step):
        left = turned[lag, rows, :, span].reshape((rows.stop - rows.start) * cols, kept)
        term = jnp.dot(left, pairs[step + lag + 1], preferred_element_type=jnp.float32)
        acc = term if acc is None else acc + term
    return acc


def strip_product(rows, turned, half, pairs, begun, field, message):
    steps, _, cols, _ = turned.shape
    strip = HALO * cols
    width = message.shape[1]
    for step in range(0, steps, 2):
        acc = half_product(rows, turned, half, pairs, step, begun[step // 2])
        for side in range(2):
            part = acc[:, side * width : (side + 1) * width]
            field[step + side] = part.reshape(HALO, cols, width)
            at = (step + side) * strip
            message[at : at + strip, :] = part.astype(message.dtype)


def own_kernel(twin, mine, turned, tail, head, pairs):
    steps, rows = turned.shape[0], turned.shape[1]
    fill_half(mine, pairs)
    for strip, out in ((slice(rows - HALO, rows), tail), (slice(0, HALO), head)):
        for step in range(0, steps, 2):
            out[step // 2] = half_product(strip, turned, twin[0], pairs, step, None)


def adjoint_own(twin, mine, turned):
    steps, _, cols, sensors = turned.shape
    width = mine.shape[2]
    strip = f32(steps // 2, HALO * cols, 2 * width)
    return call(
        own_kernel,
        "adjoint_own",
        (strip, strip, bf16(steps + 1, sensors // 2, 2 * width)),
        [SMEM] + [VMEM] * 2,
        [VMEM] * 3,
        [],
        4,
    )(twin, mine, turned)


def tail_kernel(twin, other, turned, begun, field, message, pairs):
    rows = turned.shape[1]
    fill_half(other, pairs)
    strip_product(slice(rows - HALO, rows), turned, 1 - twin[0], pairs, begun, field, message)


def head_kernel(twin, pairs, turned, begun, _, field, message):
    strip_product(slice(0, HALO), turned, 1 - twin[0], pairs, begun, field, message)


def adjoint_tail(twin, other, turned, begun):
    steps, _, cols, sensors = turned.shape
    width = other.shape[2]
    return call(
        tail_kernel,
        "adjoint_tail",
        (
            f32(steps, HALO, cols, width),
            bf16(steps * HALO * cols, width),
            bf16(steps + 1, sensors // 2, 2 * width),
        ),
        [SMEM] + [VMEM] * 3,
        [VMEM] * 3,
        [],
        4,
    )(twin, other, turned, begun)


def adjoint_head(twin, pairs, turned, begun, after):
    steps, _, cols, _ = turned.shape
    width = pairs.shape[2] // 2
    return call(
        head_kernel,
        "adjoint_head",
        (f32(steps, HALO, cols, width), bf16(steps * HALO * cols, width)),
        [SMEM, VMEM, VMEM, VMEM, HBM],
        [VMEM] * 2,
        [],
        4,
    )(twin, pairs, turned, begun, after)


def inner_kernel(
    twin, own, got, turned, upper, lower, diag, couple, ctop, cbottom, edges, scaled, out, mix, core, line, wide
):
    steps, rows, cols, sensors = turned.shape
    width = core.shape[3]
    inner = rows - 2 * HALO
    pack_at = pl.program_id(0)

    @pl.when(pack_at == 0)
    def _():
        spread((diag, couple), (ctop, cbottom), line, wide)
        mix_coefs(wide, mix)
        for step in range(0, steps, 2):
            acc = None
            for pairs, half in ((own, twin[0]), (got, 1 - twin[0])):
                acc = half_product(slice(HALO, rows - HALO), turned, half, pairs, step, acc)
            for side in range(2):
                core[step + side] = acc[:, side * width : (side + 1) * width].reshape(inner, cols, width)

    listed = edge_rows(rows)
    span = out.shape[0]

    @pl.loop(0, span)
    def _(at):
        step = pack_at * span + at

        def load(row):
            if row < HALO:
                return upper[step, row]
            return core[step, row - HALO] if row < rows - HALO else lower[step, row - rows + HALO]

        def store(row, value, weighted):
            if row in listed:
                edges[step, listed.index(row)] = value
            else:
                out[at, row - HALO] = value
            if row == 0:
                scaled[step, 0] = weighted[0]
            if row == rows - 1:
                scaled[step, 1] = weighted[rows - 1]

        own_sweeps(load, wide, rows, store)


def inner(twin, own, got, turned, upper, lower, diag, couple, ctop, cbottom):
    steps, rows, cols, _ = turned.shape
    width = upper.shape[3]
    core = rows - 2 * HALO
    assert core == HALO
    span = steps // 2
    return call(
        inner_kernel,
        "inner",
        (
            f32(steps, 2 * HALO, cols, width),
            f32(steps, 2, cols, width),
            f32(steps, rows, cols, width),
            f32(2, 8, cols, width),
        ),
        [SMEM] + [VMEM] * 9,
        [VMEM, VMEM, pl.BlockSpec((span, core, cols, width), lambda step: (step, 1, 0, 0)), VMEM],
        [pltpu.VMEM((steps, core, cols, width), jnp.float32)] + coef_scratch(rows + 2 * HALO, cols, width),
        10,
        (steps // span,),
    )(twin, own, got, turned, upper, lower, diag, couple, ctop, cbottom)


def finish_kernel(side, message, mix, edges, scaled, _, out):
    span, _, cols, _ = out.shape
    first = pl.program_id(0) * span

    @pl.loop(0, span)
    def _(at):
        step = first + at
        added = halo_part(message, step * (HALO * cols), scaled[step, side], mix, side)
        for spot, extra in zip(spots_of(side), added):
            out[at, spot % HALO] = edges[step, spot] + extra


def finish(side, message, mix, edges, scaled, out):
    steps, rows, cols, width = out.shape
    span = steps // 2
    place = side * (rows // HALO - 1)
    return call(
        functools.partial(finish_kernel, side),
        "finish",
        f32(*out.shape),
        [VMEM] * 4 + [HBM],
        pl.BlockSpec((span, HALO, cols, width), lambda step: (step, place, 0, 0)),
        [],
        2,
        (steps // span,),
        {4: 0},
    )(message, mix, edges, scaled, out)


def send_down(tail):
    return lax.ppermute(tail, "tile", [(i, i + 1) for i in range(lax.axis_size("tile") - 1)])


def send_up(head):
    return lax.ppermute(head, "tile", [(i + 1, i) for i in range(lax.axis_size("tile") - 1)])


def swap_twins(value):
    return lax.ppermute(value, "twin", [(0, 1), (1, 0)])


def body(sketch, diag_coef, couple, kernel, noise_prec):
    steps, _, rows, cols, width = sketch.shape
    sensors = kernel.shape[1]
    others = ("pair", "tile")
    groups = lax.axis_size(others)
    twin = lax.axis_index("twin")
    which = twin.reshape(1)
    field = sketch.reshape(steps, rows, cols, width)
    diag, couple = diag_coef.reshape(rows, cols), couple.reshape(rows, cols)
    kern = jnp.transpose(kernel.reshape(steps, sensors, rows, cols), (0, 2, 1, 3))
    kept = sensors // 2
    share = steps * kept // groups

    tail = pack(rows - HALO, field, sketch)
    top = send_down(tail)
    bottom = send_up(pack(0, field, tail))
    coefs = jnp.stack([diag, couple])
    note = send_down(coefs[:, rows - HALO :]), send_up(coefs[:, :HALO])
    noise = lax.dynamic_slice(noise_prec, (0, twin * kept), (steps, kept)).reshape(steps * kept)
    noise = lax.dynamic_slice(noise, ((groups - 1 - lax.axis_index(others)) * share,), (share,))
    prec = jnp.broadcast_to(noise[:, None], (share, width))
    edges, scaled, data, turned, outward = before(field, diag, couple, kern, prec)

    gone, pairs = leaving(which, top, bottom, diag, couple, *note, edges, scaled, outward, data)
    both = join(staying(which, pairs, outward, data), swap_twins(gone)).reshape(groups, share, width)
    backwards = [list(reversed(range(groups)))]
    pieces = lax.all_to_all(both, others, 0, 0, axis_index_groups=backwards, tiled=True)
    weighted = lax.all_to_all(scale(pieces, prec), others, 0, 0, tiled=True)
    other = swap_twins(weighted)
    tail, head, own = adjoint_own(which, weighted, turned)
    lower, tail, got = adjoint_tail(which, other, turned, tail)
    top = send_down(tail)
    upper, head = adjoint_head(which, got, turned, head, tail)
    bottom = send_up(head)
    edges, scaled, out, mix = inner(which, own, got, turned, upper, lower, diag, couple, *note)
    out = finish(0, top, mix, edges, scaled, out)
    out = finish(1, bottom, mix, edges, scaled, out)
    return out.reshape(sketch.shape)


def solution(mesh):
    bands, tiles = mesh.shape["band"], mesh.shape["tile"]
    fine = Mesh(mesh.devices.reshape(bands // 2, 2, tiles), ("pair", "twin", "tile"))
    band = ("pair", "twin")
    placed = (
        P(None, band, "tile", None, None),
        P(band, "tile", None),
        P(band, "tile", None),
        P(None, None, band, "tile", None),
        P(),
    )
    return jax.shard_map(
        body,
        mesh=fine,
        in_specs=placed,
        out_specs=P(None, band, "tile", None, None),
        check_vma=False,
    )
```

```python
import functools

import jax
import jax.numpy as jnp
from jax import lax
from jax.experimental import pallas as pl
from jax.experimental.pallas import tpu as pltpu
from jax.sharding import Mesh
from jax.sharding import PartitionSpec as P

MIB = 1 << 20
HALO = 2
VMEM = pl.BlockSpec(memory_space=pltpu.VMEM)
SMEM = pl.BlockSpec(memory_space=pltpu.SMEM)
HBM = pl.BlockSpec(memory_space=pltpu.HBM)


def call(kernel, name, out_shape, in_specs, out_specs, scratch, moved, grid=(), aliases={}, limit=16):
    return pl.pallas_call(
        kernel,
        grid=grid,
        out_shape=out_shape,
        in_specs=in_specs,
        out_specs=out_specs,
        scratch_shapes=scratch,
        input_output_aliases=aliases,
        compiler_params=pltpu.CompilerParams(vmem_limit_bytes=limit * MIB),
        cost_estimate=pl.CostEstimate(flops=0, bytes_accessed=moved * MIB, transcendentals=0),
        name=name,
    )


def f32(*shape):
    return jax.ShapeDtypeStruct(shape, jnp.float32)


def bf16(*shape):
    return jax.ShapeDtypeStruct(shape, jnp.bfloat16)


def edge_rows(rows):
    return [*range(HALO), *range(rows - HALO, rows)]


def beside(w):
    cols = w.shape[0]
    at = lax.broadcasted_iota(jnp.int32, w.shape, 0)
    before = jnp.where(at == 0, 0.0, pltpu.roll(w, 1, 0))
    after = jnp.where(at == cols - 1, 0.0, pltpu.roll(w, cols - 1, 0))
    return before + after


def spread(own, halos, line, wide):
    rows, cols = own[0].shape
    for which in range(2):
        line[...] = jnp.zeros(line.shape, line.dtype)
        for side, halo in enumerate(halos):
            at = side * (HALO + rows)
            line[at : at + HALO, :] = halo[which]
        line[HALO : HALO + rows, :] = own[which][...]
        turned = line[...].T
        for row in range(rows + 2 * HALO):
            wide[which, row] = jnp.broadcast_to(turned[:, row : row + 1], wide.shape[2:])


def mix_coefs(wide, mix):
    total = wide.shape[1]
    for side in range(2):
        far, near, edge, inner = (row if side == 0 else total - 1 - row for row in range(4))
        square = wide[1, edge] * wide[1, edge]
        mix[side, 0] = wide[1, near]
        mix[side, 1] = wide[1, far]
        mix[side, 2] = wide[1, near] * wide[0, near]
        mix[side, 3] = wide[1, near] * wide[1, near]
        mix[side, 4] = -square
        mix[side, 5] = -wide[0, edge] * wide[1, edge]
        mix[side, 6] = wide[1, edge]
        mix[side, 7] = wide[1, inner] * square


def coef_scratch(rows, cols, width):
    return [pltpu.VMEM((cols, cols), jnp.float32), pltpu.VMEM((2, rows, cols, width), jnp.float32)]


def one_sweep(values, scaled, wide, row):
    around = beside(scaled[row])
    if row > 0:
        around = around + scaled[row - 1]
    if row + 1 < len(scaled):
        around = around + scaled[row + 1]
    return wide[0, row + HALO] * values[row] - wide[1, row + HALO] * around


def own_sweeps(load, wide, rows, store):
    values, scaled, first, second = ([None] * rows for _ in range(4))
    for row in range(rows + 2):
        if row < rows:
            values[row] = load(row)
            scaled[row] = wide[1, row + HALO] * values[row]
        if 0 < row <= rows:
            first[row - 1] = one_sweep(values, scaled, wide, row - 1)
            second[row - 1] = wide[1, row - 1 + HALO] * first[row - 1]
        if row > 1:
            store(row - 2, one_sweep(first, second, wide, row - 2), scaled)


def halo_part(message, at, edge_scaled, mix, side):
    cols = edge_scaled.shape[0]
    far_row, near_row = (0, 1) if side == 0 else (1, 0)

    def take(row):
        start = pl.multiple_of(at + row * cols, cols)
        return message[pl.ds(start, cols), :].astype(jnp.float32)

    near = take(near_row)
    scaled = mix[side, 0] * near
    around = mix[side, 1] * take(far_row) + edge_scaled + beside(scaled)
    near_second = mix[side, 2] * near - mix[side, 3] * around
    second = mix[side, 4] * scaled
    on_edge = mix[side, 5] * scaled - mix[side, 6] * (near_second + beside(second))
    return on_edge, mix[side, 7] * scaled


def spots_of(side):
    return (0, 1) if side == 0 else (2 * HALO - 1, 2 * HALO - 2)


def pack_kernel(first, field, _, out, edges, packed, arrived, left):
    steps, rows, cols, width = field.shape
    strip = HALO * cols
    coming, going = [], []
    for step in range(steps):
        source = field.at[step, pl.ds(first, HALO)]
        coming.append(pltpu.make_async_copy(source, edges.at[step], arrived.at[step]))
        coming[step].start()
        going.append(pltpu.make_async_copy(packed.at[step], out.at[pl.ds(step * strip, strip)], left.at[step]))
    for step in range(steps):
        coming[step].wait()
        packed[step] = edges[step].reshape(strip, width).astype(packed.dtype)
        going[step].start()
    for copy in going:
        copy.wait()


def pack(first, field, after):
    steps, rows, cols, width = field.shape
    strip = HALO * cols
    return call(
        functools.partial(pack_kernel, first),
        "pack",
        bf16(steps * strip, width),
        [HBM] * 2,
        HBM,
        [
            pltpu.VMEM((steps, HALO, cols, width), jnp.float32),
            pltpu.VMEM((steps, strip, width), jnp.bfloat16),
            pltpu.SemaphoreType.DMA((steps,)),
            pltpu.SemaphoreType.DMA((steps,)),
        ],
        3,
        limit=62,
    )(field, after)


def before_kernel(field, diag, couple, kern, _, edges, scaled, data, turned, outward, line, wide, pairs):
    steps, rows, cols, width = field.shape
    inner = rows - 2 * HALO
    listed = edge_rows(rows)
    spread((diag, couple), (), line, wide)
    pairs[0, :, 0:width] = jnp.zeros((inner * cols, width), pairs.dtype)

    @pl.loop(0, steps)
    def _(step):
        def store(row, value, weighted):
            if row in listed:
                edges[step, listed.index(row)] = value
            else:
                at = (row - HALO) * cols
                rounded = value.astype(pairs.dtype)
                pairs[step, at : at + cols, width : 2 * width] = rounded
                pairs[step + 1, at : at + cols, 0:width] = rounded
            if row == 0:
                scaled[step, 0] = weighted[0]
            if row == rows - 1:
                scaled[step, 1] = weighted[rows - 1]

        own_sweeps(lambda row: field[step, row], wide, rows, store)

    @pl.loop(0, steps)
    def _(lag):
        for row in range(rows):
            turned[lag, row] = kern[lag, row].T
        for spot, row in enumerate(listed):
            outward[lag, :, spot * cols : (spot + 1) * cols] = kern[lag, row]

    for step in range(0, steps, 2):
        acc = None
        for lag in range(step + 2):
            left = jnp.concatenate([kern[lag, row] for row in range(HALO, rows - HALO)], axis=1)
            term = jnp.dot(left, pairs[step + 1 - lag], preferred_element_type=jnp.float32)
            acc = term if acc is None else acc + term
        data[step] = acc[:, 0:width]
        data[step + 1] = acc[:, width : 2 * width]


def before(field, diag, couple, kern, after):
    steps, rows, cols, width = field.shape
    sensors = kern.shape[2]
    inner = (rows - 2 * HALO) * cols
    return call(
        before_kernel,
        "before",
        (
            f32(steps, 2 * HALO, cols, width),
            f32(steps, 2, cols, width),
            f32(steps, sensors, width),
            bf16(steps, rows, cols, sensors),
            bf16(steps, sensors, 2 * HALO * cols),
        ),
        [VMEM] * 4 + [HBM],
        [VMEM] * 5,
        coef_scratch(rows + 2 * HALO, cols, width) + [pltpu.VMEM((steps + 1, inner, 2 * width), jnp.bfloat16)],
        12,
    )(field, diag, couple, kern, after)


def edge_product(half, pairs, outward, start, out):
    steps, sensors, _ = outward.shape
    width = out.shape[2]
    kept = sensors // 2
    span = pl.ds(pl.multiple_of(half * kept, kept), kept)
    for step in range(0, steps, 2):
        acc = jnp.concatenate([start[step, span, :], start[step + 1, span, :]], axis=1)
        for lag in range(step + 2):
            left = outward[lag, span, :]
            acc = acc + jnp.dot(left, pairs[step + 1 - lag], preferred_element_type=jnp.float32)
        out[step] = acc[:, 0:width].astype(out.dtype)
        out[step + 1] = acc[:, width : 2 * width].astype(out.dtype)


def leaving_kernel(
    twin, top, bottom, diag, couple, ctop, cbottom, edges, scaled, outward, start, out, pairs, line, wide, mix
):
    steps = outward.shape[0]
    cols, width = edges.shape[2], edges.shape[3]
    spread((diag, couple), (ctop, cbottom), line, wide)
    mix_coefs(wide, mix)
    pairs[0, :, 0:width] = jnp.zeros((2 * HALO * cols, width), pairs.dtype)

    @pl.loop(0, steps)
    def _(step):
        for side, message in enumerate((top, bottom)):
            added = halo_part(message, step * (HALO * cols), scaled[step, side], mix, side)
            for spot, extra in zip(spots_of(side), added):
                rounded = (edges[step, spot] + extra).astype(pairs.dtype)
                at = spot * cols
                pairs[step, at : at + cols, width : 2 * width] = rounded
                pairs[step + 1, at : at + cols, 0:width] = rounded

    edge_product(1 - twin[0], pairs, outward, start, out)


def leaving(twin, top, bottom, diag, couple, ctop, cbottom, edges, scaled, outward, start):
    steps, sensors, _ = outward.shape
    rows, cols = diag.shape
    width = edges.shape[3]
    return call(
        leaving_kernel,
        "leaving",
        [bf16(steps, sensors // 2, width), bf16(steps + 1, 2 * HALO * cols, 2 * width)],
        [SMEM] + [VMEM] * 10,
        [VMEM] * 2,
        coef_scratch(rows + 2 * HALO, cols, width) + [pltpu.VMEM((2, 8, cols, width), jnp.float32)],
        1,
    )(twin, top, bottom, diag, couple, ctop, cbottom, edges, scaled, outward, start)


def staying_kernel(twin, pairs, outward, start, out):
    edge_product(twin[0], pairs, outward, start, out)


def staying(twin, pairs, outward, start):
    steps, sensors, width = start.shape
    out = f32(steps, sensors // 2, width)
    return call(staying_kernel, "staying", out, [SMEM] + [VMEM] * 3, VMEM, [], 1)(twin, pairs, outward, start)


def join_kernel(mine, got, both):
    both[...] = (mine[...] + got[...].astype(jnp.float32)).astype(both.dtype)


def join(mine, got):
    return call(join_kernel, "join", bf16(*got.shape), [VMEM] * 2, VMEM, [], 1)(mine, got)


def scale_kernel(pieces, prec, out):
    total = pieces[0].astype(jnp.float32)
    for piece in range(1, pieces.shape[0]):
        total = total + pieces[piece].astype(jnp.float32)
    weighted = (total * prec[...]).astype(out.dtype)
    for piece in range(pieces.shape[0]):
        out[piece] = weighted


def scale(pieces, prec):
    return call(scale_kernel, "scale", bf16(*pieces.shape), [VMEM] * 2, VMEM, [], 1)(pieces, prec)


def fill_half(source, pairs):
    groups, share, width = source.shape
    kept = pairs.shape[1]
    steps = groups * share // kept
    pairs[steps, :, width : 2 * width] = jnp.zeros((kept, width), pairs.dtype)
    for piece in range(groups):
        step, first = divmod(piece * share, kept)
        value = source[piece]
        pairs[step + 1, first : first + share, 0:width] = value
        pairs[step, first : first + share, width : 2 * width] = value


def half_product(rows, turned, half, pairs, step, acc):
    steps, _, cols, sensors = turned.shape
    kept = sensors // 2
    span = pl.ds(pl.multiple_of(half * kept, kept), kept)
    for lag in range(steps - step):
        left = turned[lag, rows, :, span].reshape((rows.stop - rows.start) * cols, kept)
        term = jnp.dot(left, pairs[step + lag + 1], preferred_element_type=jnp.float32)
        acc = term if acc is None else acc + term
    return acc


def strip_product(rows, turned, half, pairs, begun, field, message):
    steps, _, cols, _ = turned.shape
    strip = HALO * cols
    width = message.shape[1]
    for step in range(0, steps, 2):
        acc = half_product(rows, turned, half, pairs, step, begun[step // 2])
        for side in range(2):
            part = acc[:, side * width : (side + 1) * width]
            field[step + side] = part.reshape(HALO, cols, width)
            at = (step + side) * strip
            message[at : at + strip, :] = part.astype(message.dtype)


def own_kernel(twin, mine, turned, tail, head, pairs):
    steps, rows = turned.shape[0], turned.shape[1]
    fill_half(mine, pairs)
    for strip, out in ((slice(rows - HALO, rows), tail), (slice(0, HALO), head)):
        for step in range(0, steps, 2):
            out[step // 2] = half_product(strip, turned, twin[0], pairs, step, None)


def adjoint_own(twin, mine, turned):
    steps, _, cols, sensors = turned.shape
    width = mine.shape[2]
    strip = f32(steps // 2, HALO * cols, 2 * width)
    return call(
        own_kernel,
        "adjoint_own",
        (strip, strip, bf16(steps + 1, sensors // 2, 2 * width)),
        [SMEM] + [VMEM] * 2,
        [VMEM] * 3,
        [],
        4,
    )(twin, mine, turned)


def tail_kernel(twin, other, turned, begun, field, message, pairs):
    rows = turned.shape[1]
    fill_half(other, pairs)
    strip_product(slice(rows - HALO, rows), turned, 1 - twin[0], pairs, begun, field, message)


def head_kernel(twin, pairs, turned, begun, _, field, message):
    strip_product(slice(0, HALO), turned, 1 - twin[0], pairs, begun, field, message)


def adjoint_tail(twin, other, turned, begun):
    steps, _, cols, sensors = turned.shape
    width = other.shape[2]
    return call(
        tail_kernel,
        "adjoint_tail",
        (
            f32(steps, HALO, cols, width),
            bf16(steps * HALO * cols, width),
            bf16(steps + 1, sensors // 2, 2 * width),
        ),
        [SMEM] + [VMEM] * 3,
        [VMEM] * 3,
        [],
        4,
    )(twin, other, turned, begun)


def adjoint_head(twin, pairs, turned, begun, after):
    steps, _, cols, _ = turned.shape
    width = pairs.shape[2] // 2
    return call(
        head_kernel,
        "adjoint_head",
        (f32(steps, HALO, cols, width), bf16(steps * HALO * cols, width)),
        [SMEM, VMEM, VMEM, VMEM, HBM],
        [VMEM] * 2,
        [],
        4,
    )(twin, pairs, turned, begun, after)


def inner_kernel(
    twin, own, got, turned, upper, lower, diag, couple, ctop, cbottom, edges, scaled, out, mix, core, line, wide
):
    steps, rows, cols, sensors = turned.shape
    width = core.shape[3]
    inner = rows - 2 * HALO
    pack_at = pl.program_id(0)

    @pl.when(pack_at == 0)
    def _():
        spread((diag, couple), (ctop, cbottom), line, wide)
        mix_coefs(wide, mix)
        for step in range(0, steps, 2):
            acc = None
            for pairs, half in ((own, twin[0]), (got, 1 - twin[0])):
                acc = half_product(slice(HALO, rows - HALO), turned, half, pairs, step, acc)
            for side in range(2):
                core[step + side] = acc[:, side * width : (side + 1) * width].reshape(inner, cols, width)

    listed = edge_rows(rows)
    span = out.shape[0]

    @pl.loop(0, span)
    def _(at):
        step = pack_at * span + at

        def load(row):
            if row < HALO:
                return upper[step, row]
            return core[step, row - HALO] if row < rows - HALO else lower[step, row - rows + HALO]

        def store(row, value, weighted):
            if row in listed:
                edges[step, listed.index(row)] = value
            else:
                out[at, row - HALO] = value
            if row == 0:
                scaled[step, 0] = weighted[0]
            if row == rows - 1:
                scaled[step, 1] = weighted[rows - 1]

        own_sweeps(load, wide, rows, store)


def inner(twin, own, got, turned, upper, lower, diag, couple, ctop, cbottom):
    steps, rows, cols, _ = turned.shape
    width = upper.shape[3]
    core = rows - 2 * HALO
    assert core == HALO
    span = steps // 2
    return call(
        inner_kernel,
        "inner",
        (
            f32(steps, 2 * HALO, cols, width),
            f32(steps, 2, cols, width),
            f32(steps, rows, cols, width),
            f32(2, 8, cols, width),
        ),
        [SMEM] + [VMEM] * 9,
        [VMEM, VMEM, pl.BlockSpec((span, core, cols, width), lambda step: (step, 1, 0, 0)), VMEM],
        [pltpu.VMEM((steps, core, cols, width), jnp.float32)] + coef_scratch(rows + 2 * HALO, cols, width),
        10,
        (steps // span,),
    )(twin, own, got, turned, upper, lower, diag, couple, ctop, cbottom)


def finish_kernel(side, message, mix, edges, scaled, _, out):
    span, _, cols, _ = out.shape
    first = pl.program_id(0) * span

    @pl.loop(0, span)
    def _(at):
        step = first + at
        added = halo_part(message, step * (HALO * cols), scaled[step, side], mix, side)
        for spot, extra in zip(spots_of(side), added):
            out[at, spot % HALO] = edges[step, spot] + extra


def finish(side, message, mix, edges, scaled, out):
    steps, rows, cols, width = out.shape
    span = steps // 2
    place = side * (rows // HALO - 1)
    return call(
        functools.partial(finish_kernel, side),
        "finish",
        f32(*out.shape),
        [VMEM] * 4 + [HBM],
        pl.BlockSpec((span, HALO, cols, width), lambda step: (step, place, 0, 0)),
        [],
        2,
        (steps // span,),
        {4: 0},
    )(message, mix, edges, scaled, out)


def send_down(tail):
    return lax.ppermute(tail, "tile", [(i, i + 1) for i in range(lax.axis_size("tile") - 1)])


def send_up(head):
    return lax.ppermute(head, "tile", [(i + 1, i) for i in range(lax.axis_size("tile") - 1)])


def swap_twins(value):
    return lax.ppermute(value, "twin", [(0, 1), (1, 0)])


def body(sketch, diag_coef, couple, kernel, noise_prec):
    steps, _, rows, cols, width = sketch.shape
    sensors = kernel.shape[1]
    others = ("pair", "tile")
    groups = lax.axis_size(others)
    twin = lax.axis_index("twin")
    which = twin.reshape(1)
    field = sketch.reshape(steps, rows, cols, width)
    diag, couple = diag_coef.reshape(rows, cols), couple.reshape(rows, cols)
    kern = jnp.transpose(kernel.reshape(steps, sensors, rows, cols), (0, 2, 1, 3))
    kept = sensors // 2
    share = steps * kept // groups

    tail = pack(rows - HALO, field, sketch)
    top = send_down(tail)
    bottom = send_up(pack(0, field, tail))
    coefs = jnp.stack([diag, couple])
    note = send_down(coefs[:, rows - HALO :]), send_up(coefs[:, :HALO])
    noise = lax.dynamic_slice(noise_prec, (0, twin * kept), (steps, kept)).reshape(steps * kept)
    noise = lax.dynamic_slice(noise, ((groups - 1 - lax.axis_index(others)) * share,), (share,))
    prec = jnp.broadcast_to(noise[:, None], (share, width))
    edges, scaled, data, turned, outward = before(field, diag, couple, kern, prec)

    gone, pairs = leaving(which, top, bottom, diag, couple, *note, edges, scaled, outward, data)
    both = join(staying(which, pairs, outward, data), swap_twins(gone)).reshape(groups, share, width)
    backwards = [list(reversed(range(groups)))]
    pieces = lax.all_to_all(both, others, 0, 0, axis_index_groups=backwards, tiled=True)
    weighted = lax.all_to_all(scale(pieces, prec), others, 0, 0, axis_index_groups=backwards, tiled=True)
    other = swap_twins(weighted)
    tail, head, own = adjoint_own(which, weighted, turned)
    lower, tail, got = adjoint_tail(which, other, turned, tail)
    top = send_down(tail)
    upper, head = adjoint_head(which, got, turned, head, tail)
    bottom = send_up(head)
    edges, scaled, out, mix = inner(which, own, got, turned, upper, lower, diag, couple, *note)
    out = finish(0, top, mix, edges, scaled, out)
    out = finish(1, bottom, mix, edges, scaled, out)
    return out.reshape(sketch.shape)


def solution(mesh):
    bands, tiles = mesh.shape["band"], mesh.shape["tile"]
    fine = Mesh(mesh.devices.reshape(bands // 2, 2, tiles), ("pair", "twin", "tile"))
    band = ("pair", "twin")
    placed = (
        P(None, band, "tile", None, None),
        P(band, "tile", None),
        P(band, "tile", None),
        P(None, None, band, "tile", None),
        P(),
    )
    return jax.shard_map(
        body,
        mesh=fine,
        in_specs=placed,
        out_specs=P(None, band, "tile", None, None),
        check_vma=False,
    )
```

```python
import functools

import jax
import jax.numpy as jnp
from jax import lax
from jax.experimental import pallas as pl
from jax.experimental.pallas import tpu as pltpu
from jax.sharding import Mesh
from jax.sharding import PartitionSpec as P

MIB = 1 << 20
HALO = 2
VMEM = pl.BlockSpec(memory_space=pltpu.VMEM)
SMEM = pl.BlockSpec(memory_space=pltpu.SMEM)
HBM = pl.BlockSpec(memory_space=pltpu.HBM)


def call(kernel, name, out_shape, in_specs, out_specs, scratch, moved, grid=(), aliases={}, limit=16):
    return pl.pallas_call(
        kernel,
        grid=grid,
        out_shape=out_shape,
        in_specs=in_specs,
        out_specs=out_specs,
        scratch_shapes=scratch,
        input_output_aliases=aliases,
        compiler_params=pltpu.CompilerParams(vmem_limit_bytes=limit * MIB),
        cost_estimate=pl.CostEstimate(flops=0, bytes_accessed=moved * MIB, transcendentals=0),
        name=name,
    )


def f32(*shape):
    return jax.ShapeDtypeStruct(shape, jnp.float32)


def bf16(*shape):
    return jax.ShapeDtypeStruct(shape, jnp.bfloat16)


def edge_rows(rows):
    return [*range(HALO), *range(rows - HALO, rows)]


def beside(w):
    cols = w.shape[0]
    at = lax.broadcasted_iota(jnp.int32, w.shape, 0)
    before = jnp.where(at == 0, 0.0, pltpu.roll(w, 1, 0))
    after = jnp.where(at == cols - 1, 0.0, pltpu.roll(w, cols - 1, 0))
    return before + after


def spread(own, halos, line, wide):
    rows, cols = own[0].shape
    for which in range(2):
        line[...] = jnp.zeros(line.shape, line.dtype)
        for side, halo in enumerate(halos):
            at = side * (HALO + rows)
            line[at : at + HALO, :] = halo[which]
        line[HALO : HALO + rows, :] = own[which][...]
        turned = line[...].T
        for row in range(rows + 2 * HALO):
            wide[which, row] = jnp.broadcast_to(turned[:, row : row + 1], wide.shape[2:])


def mix_coefs(wide, mix):
    total = wide.shape[1]
    for side in range(2):
        far, near, edge, inner = (row if side == 0 else total - 1 - row for row in range(4))
        square = wide[1, edge] * wide[1, edge]
        mix[side, 0] = wide[1, near]
        mix[side, 1] = wide[1, far]
        mix[side, 2] = wide[1, near] * wide[0, near]
        mix[side, 3] = wide[1, near] * wide[1, near]
        mix[side, 4] = -square
        mix[side, 5] = -wide[0, edge] * wide[1, edge]
        mix[side, 6] = wide[1, edge]
        mix[side, 7] = wide[1, inner] * square


def coef_scratch(rows, cols, width):
    return [pltpu.VMEM((cols, cols), jnp.float32), pltpu.VMEM((2, rows, cols, width), jnp.float32)]


def one_sweep(values, scaled, wide, row):
    around = beside(scaled[row])
    if row > 0:
        around = around + scaled[row - 1]
    if row + 1 < len(scaled):
        around = around + scaled[row + 1]
    return wide[0, row + HALO] * values[row] - wide[1, row + HALO] * around


def own_sweeps(load, wide, rows, store):
    values, scaled, first, second = ([None] * rows for _ in range(4))
    for row in range(rows + 2):
        if row < rows:
            values[row] = load(row)
            scaled[row] = wide[1, row + HALO] * values[row]
        if 0 < row <= rows:
            first[row - 1] = one_sweep(values, scaled, wide, row - 1)
            second[row - 1] = wide[1, row - 1 + HALO] * first[row - 1]
        if row > 1:
            store(row - 2, one_sweep(first, second, wide, row - 2), scaled)


def halo_part(message, at, edge_scaled, mix, side):
    cols = edge_scaled.shape[0]
    far_row, near_row = (0, 1) if side == 0 else (1, 0)

    def take(row):
        start = pl.multiple_of(at + row * cols, cols)
        return message[pl.ds(start, cols), :].astype(jnp.float32)

    near = take(near_row)
    scaled = mix[side, 0] * near
    around = mix[side, 1] * take(far_row) + edge_scaled + beside(scaled)
    near_second = mix[side, 2] * near - mix[side, 3] * around
    second = mix[side, 4] * scaled
    on_edge = mix[side, 5] * scaled - mix[side, 6] * (near_second + beside(second))
    return on_edge, mix[side, 7] * scaled


def spots_of(side):
    return (0, 1) if side == 0 else (2 * HALO - 1, 2 * HALO - 2)


def pack_kernel(first, field, _, out, edges, packed, arrived, left):
    steps, rows, cols, width = field.shape
    strip = HALO * cols
    coming, going = [], []
    for step in range(steps):
        source = field.at[step, pl.ds(first, HALO)]
        coming.append(pltpu.make_async_copy(source, edges.at[step], arrived.at[step]))
        coming[step].start()
        going.append(pltpu.make_async_copy(packed.at[step], out.at[pl.ds(step * strip, strip)], left.at[step]))
    for step in range(steps):
        coming[step].wait()
        packed[step] = edges[step].reshape(strip, width).astype(packed.dtype)
        going[step].start()
    for copy in going:
        copy.wait()


def pack(first, field, after):
    steps, rows, cols, width = field.shape
    strip = HALO * cols
    return call(
        functools.partial(pack_kernel, first),
        "pack",
        bf16(steps * strip, width),
        [HBM] * 2,
        HBM,
        [
            pltpu.VMEM((steps, HALO, cols, width), jnp.float32),
            pltpu.VMEM((steps, strip, width), jnp.bfloat16),
            pltpu.SemaphoreType.DMA((steps,)),
            pltpu.SemaphoreType.DMA((steps,)),
        ],
        3,
        limit=62,
    )(field, after)


def before_kernel(field, diag, couple, kern, _, edges, scaled, data, turned, outward, line, wide, pairs):
    steps, rows, cols, width = field.shape
    inner = rows - 2 * HALO
    listed = edge_rows(rows)
    spread((diag, couple), (), line, wide)
    pairs[0, :, 0:width] = jnp.zeros((inner * cols, width), pairs.dtype)

    @pl.loop(0, steps)
    def _(step):
        def store(row, value, weighted):
            if row in listed:
                edges[step, listed.index(row)] = value
            else:
                at = (row - HALO) * cols
                rounded = value.astype(pairs.dtype)
                pairs[step, at : at + cols, width : 2 * width] = rounded
                pairs[step + 1, at : at + cols, 0:width] = rounded
            if row == 0:
                scaled[step, 0] = weighted[0]
            if row == rows - 1:
                scaled[step, 1] = weighted[rows - 1]

        own_sweeps(lambda row: field[step, row], wide, rows, store)

    @pl.loop(0, steps)
    def _(lag):
        for row in range(rows):
            turned[lag, row] = kern[lag, row].T
        for spot, row in enumerate(listed):
            outward[lag, :, spot * cols : (spot + 1) * cols] = kern[lag, row]

    for step in range(0, steps, 2):
        acc = None
        for lag in range(step + 2):
            left = jnp.concatenate([kern[lag, row] for row in range(HALO, rows - HALO)], axis=1)
            term = jnp.dot(left, pairs[step + 1 - lag], preferred_element_type=jnp.float32)
            acc = term if acc is None else acc + term
        data[step] = acc[:, 0:width]
        data[step + 1] = acc[:, width : 2 * width]


def before(field, diag, couple, kern, after):
    steps, rows, cols, width = field.shape
    sensors = kern.shape[2]
    inner = (rows - 2 * HALO) * cols
    return call(
        before_kernel,
        "before",
        (
            f32(steps, 2 * HALO, cols, width),
            f32(steps, 2, cols, width),
            f32(steps, sensors, width),
            bf16(steps, rows, cols, sensors),
            bf16(steps, sensors, 2 * HALO * cols),
        ),
        [VMEM] * 4 + [HBM],
        [VMEM] * 5,
        coef_scratch(rows + 2 * HALO, cols, width) + [pltpu.VMEM((steps + 1, inner, 2 * width), jnp.bfloat16)],
        12,
    )(field, diag, couple, kern, after)


def edge_product(half, pairs, outward, start, out):
    steps, sensors, _ = outward.shape
    width = out.shape[2]
    kept = sensors // 2
    span = pl.ds(pl.multiple_of(half * kept, kept), kept)
    for step in range(0, steps, 2):
        acc = jnp.concatenate([start[step, span, :], start[step + 1, span, :]], axis=1)
        for lag in range(step + 2):
            left = outward[lag, span, :]
            acc = acc + jnp.dot(left, pairs[step + 1 - lag], preferred_element_type=jnp.float32)
        out[step] = acc[:, 0:width].astype(out.dtype)
        out[step + 1] = acc[:, width : 2 * width].astype(out.dtype)


def leaving_kernel(
    twin, top, bottom, diag, couple, ctop, cbottom, edges, scaled, outward, start, out, pairs, line, wide, mix
):
    steps = outward.shape[0]
    cols, width = edges.shape[2], edges.shape[3]
    spread((diag, couple), (ctop, cbottom), line, wide)
    mix_coefs(wide, mix)
    pairs[0, :, 0:width] = jnp.zeros((2 * HALO * cols, width), pairs.dtype)

    @pl.loop(0, steps)
    def _(step):
        for side, message in enumerate((top, bottom)):
            added = halo_part(message, step * (HALO * cols), scaled[step, side], mix, side)
            for spot, extra in zip(spots_of(side), added):
                rounded = (edges[step, spot] + extra).astype(pairs.dtype)
                at = spot * cols
                pairs[step, at : at + cols, width : 2 * width] = rounded
                pairs[step + 1, at : at + cols, 0:width] = rounded

    edge_product(1 - twin[0], pairs, outward, start, out)


def leaving(twin, top, bottom, diag, couple, ctop, cbottom, edges, scaled, outward, start):
    steps, sensors, _ = outward.shape
    rows, cols = diag.shape
    width = edges.shape[3]
    return call(
        leaving_kernel,
        "leaving",
        [bf16(steps, sensors // 2, width), bf16(steps + 1, 2 * HALO * cols, 2 * width)],
        [SMEM] + [VMEM] * 10,
        [VMEM] * 2,
        coef_scratch(rows + 2 * HALO, cols, width) + [pltpu.VMEM((2, 8, cols, width), jnp.float32)],
        1,
    )(twin, top, bottom, diag, couple, ctop, cbottom, edges, scaled, outward, start)


def staying_kernel(twin, pairs, outward, start, out):
    edge_product(twin[0], pairs, outward, start, out)


def staying(twin, pairs, outward, start):
    steps, sensors, width = start.shape
    out = f32(steps, sensors // 2, width)
    return call(staying_kernel, "staying", out, [SMEM] + [VMEM] * 3, VMEM, [], 1)(twin, pairs, outward, start)


def join_kernel(mine, got, both):
    both[...] = (mine[...] + got[...].astype(jnp.float32)).astype(both.dtype)


def join(mine, got):
    return call(join_kernel, "join", bf16(*got.shape), [VMEM] * 2, VMEM, [], 1)(mine, got)


def scale_kernel(pieces, prec, out):
    total = pieces[0].astype(jnp.float32)
    for piece in range(1, pieces.shape[0]):
        total = total + pieces[piece].astype(jnp.float32)
    weighted = (total * prec[...]).astype(out.dtype)
    for piece in range(pieces.shape[0]):
        out[piece] = weighted


def scale(pieces, prec):
    return call(scale_kernel, "scale", bf16(*pieces.shape), [VMEM] * 2, VMEM, [], 1)(pieces, prec)


def fill_half(source, pairs):
    groups, share, width = source.shape
    kept = pairs.shape[1]
    steps = groups * share // kept
    pairs[steps, :, width : 2 * width] = jnp.zeros((kept, width), pairs.dtype)
    for piece in range(groups):
        step, first = divmod(piece * share, kept)
        value = source[groups - 1 - piece]
        pairs[step + 1, first : first + share, 0:width] = value
        pairs[step, first : first + share, width : 2 * width] = value


def half_product(rows, turned, half, pairs, step, acc):
    steps, _, cols, sensors = turned.shape
    kept = sensors // 2
    span = pl.ds(pl.multiple_of(half * kept, kept), kept)
    for lag in range(steps - step):
        left = turned[lag, rows, :, span].reshape((rows.stop - rows.start) * cols, kept)
        term = jnp.dot(left, pairs[step + lag + 1], preferred_element_type=jnp.float32)
        acc = term if acc is None else acc + term
    return acc


def strip_product(rows, turned, half, pairs, begun, field, message):
    steps, _, cols, _ = turned.shape
    strip = HALO * cols
    width = message.shape[1]
    for step in range(0, steps, 2):
        acc = half_product(rows, turned, half, pairs, step, begun[step // 2])
        for side in range(2):
            part = acc[:, side * width : (side + 1) * width]
            field[step + side] = part.reshape(HALO, cols, width)
            at = (step + side) * strip
            message[at : at + strip, :] = part.astype(message.dtype)


def own_kernel(twin, mine, turned, tail, head, pairs):
    steps, rows = turned.shape[0], turned.shape[1]
    fill_half(mine, pairs)
    for strip, out in ((slice(rows - HALO, rows), tail), (slice(0, HALO), head)):
        for step in range(0, steps, 2):
            out[step // 2] = half_product(strip, turned, twin[0], pairs, step, None)


def adjoint_own(twin, mine, turned):
    steps, _, cols, sensors = turned.shape
    width = mine.shape[2]
    strip = f32(steps // 2, HALO * cols, 2 * width)
    return call(
        own_kernel,
        "adjoint_own",
        (strip, strip, bf16(steps + 1, sensors // 2, 2 * width)),
        [SMEM] + [VMEM] * 2,
        [VMEM] * 3,
        [],
        4,
    )(twin, mine, turned)


def first_kernel(twin, other, turned, begun, field, message, pairs):
    fill_half(other, pairs)
    strip_product(slice(0, HALO), turned, 1 - twin[0], pairs, begun, field, message)


def second_kernel(twin, pairs, turned, begun, _, field, message):
    rows = turned.shape[1]
    strip_product(slice(rows - HALO, rows), turned, 1 - twin[0], pairs, begun, field, message)


def adjoint_first(twin, other, turned, begun):
    steps, _, cols, sensors = turned.shape
    width = other.shape[2]
    return call(
        first_kernel,
        "adjoint_first",
        (
            f32(steps, HALO, cols, width),
            bf16(steps * HALO * cols, width),
            bf16(steps + 1, sensors // 2, 2 * width),
        ),
        [SMEM] + [VMEM] * 3,
        [VMEM] * 3,
        [],
        4,
    )(twin, other, turned, begun)


def adjoint_second(twin, pairs, turned, begun, after):
    steps, _, cols, _ = turned.shape
    width = pairs.shape[2] // 2
    return call(
        second_kernel,
        "adjoint_second",
        (f32(steps, HALO, cols, width), bf16(steps * HALO * cols, width)),
        [SMEM, VMEM, VMEM, VMEM, HBM],
        [VMEM] * 2,
        [],
        4,
    )(twin, pairs, turned, begun, after)


def inner_kernel(
    twin, own, got, turned, upper, lower, diag, couple, ctop, cbottom, edges, scaled, out, mix, core, line, wide
):
    steps, rows, cols, sensors = turned.shape
    width = core.shape[3]
    inner = rows - 2 * HALO
    pack_at = pl.program_id(0)

    @pl.when(pack_at == 0)
    def _():
        spread((diag, couple), (ctop, cbottom), line, wide)
        mix_coefs(wide, mix)
        for step in range(0, steps, 2):
            acc = None
            for pairs, half in ((own, twin[0]), (got, 1 - twin[0])):
                acc = half_product(slice(HALO, rows - HALO), turned, half, pairs, step, acc)
            for side in range(2):
                core[step + side] = acc[:, side * width : (side + 1) * width].reshape(inner, cols, width)

    listed = edge_rows(rows)
    span = out.shape[0]

    @pl.loop(0, span)
    def _(at):
        step = pack_at * span + at

        def load(row):
            if row < HALO:
                return upper[step, row]
            return core[step, row - HALO] if row < rows - HALO else lower[step, row - rows + HALO]

        def store(row, value, weighted):
            if row in listed:
                edges[step, listed.index(row)] = value
            else:
                out[at, row - HALO] = value
            if row == 0:
                scaled[step, 0] = weighted[0]
            if row == rows - 1:
                scaled[step, 1] = weighted[rows - 1]

        own_sweeps(load, wide, rows, store)


def inner(twin, own, got, turned, upper, lower, diag, couple, ctop, cbottom):
    steps, rows, cols, _ = turned.shape
    width = upper.shape[3]
    core = rows - 2 * HALO
    assert core == HALO
    span = steps // 2
    return call(
        inner_kernel,
        "inner",
        (
            f32(steps, 2 * HALO, cols, width),
            f32(steps, 2, cols, width),
            f32(steps, rows, cols, width),
            f32(2, 8, cols, width),
        ),
        [SMEM] + [VMEM] * 9,
        [VMEM, VMEM, pl.BlockSpec((span, core, cols, width), lambda step: (step, 1, 0, 0)), VMEM],
        [pltpu.VMEM((steps, core, cols, width), jnp.float32)] + coef_scratch(rows + 2 * HALO, cols, width),
        10,
        (steps // span,),
    )(twin, own, got, turned, upper, lower, diag, couple, ctop, cbottom)


def finish_kernel(side, message, mix, edges, scaled, _, out):
    span, _, cols, _ = out.shape
    first = pl.program_id(0) * span

    @pl.loop(0, span)
    def _(at):
        step = first + at
        added = halo_part(message, step * (HALO * cols), scaled[step, side], mix, side)
        for spot, extra in zip(spots_of(side), added):
            out[at, spot % HALO] = edges[step, spot] + extra


def finish(side, message, mix, edges, scaled, out):
    steps, rows, cols, width = out.shape
    span = steps // 2
    place = side * (rows // HALO - 1)
    return call(
        functools.partial(finish_kernel, side),
        "finish",
        f32(*out.shape),
        [VMEM] * 4 + [HBM],
        pl.BlockSpec((span, HALO, cols, width), lambda step: (step, place, 0, 0)),
        [],
        2,
        (steps // span,),
        {4: 0},
    )(message, mix, edges, scaled, out)


def send_down(tail):
    return lax.ppermute(tail, "tile", [(i, i + 1) for i in range(lax.axis_size("tile") - 1)])


def send_up(head):
    return lax.ppermute(head, "tile", [(i + 1, i) for i in range(lax.axis_size("tile") - 1)])


def swap_twins(value):
    return lax.ppermute(value, "twin", [(0, 1), (1, 0)])


def body(sketch, diag_coef, couple, kernel, noise_prec):
    steps, _, rows, cols, width = sketch.shape
    sensors = kernel.shape[1]
    others = ("pair", "tile")
    groups = lax.axis_size(others)
    twin = lax.axis_index("twin")
    which = twin.reshape(1)
    field = sketch.reshape(steps, rows, cols, width)
    diag, couple = diag_coef.reshape(rows, cols), couple.reshape(rows, cols)
    kern = jnp.transpose(kernel.reshape(steps, sensors, rows, cols), (0, 2, 1, 3))
    kept = sensors // 2
    share = steps * kept // groups

    tail = pack(rows - HALO, field, sketch)
    top = send_down(tail)
    bottom = send_up(pack(0, field, tail))
    coefs = jnp.stack([diag, couple])
    note = send_down(coefs[:, rows - HALO :]), send_up(coefs[:, :HALO])
    noise = lax.dynamic_slice(noise_prec, (0, twin * kept), (steps, kept)).reshape(steps * kept)
    noise = lax.dynamic_slice(noise, ((groups - 1 - lax.axis_index(others)) * share,), (share,))
    prec = jnp.broadcast_to(noise[:, None], (share, width))
    edges, scaled, data, turned, outward = before(field, diag, couple, kern, prec)

    gone, pairs = leaving(which, top, bottom, diag, couple, *note, edges, scaled, outward, data)
    both = join(staying(which, pairs, outward, data), swap_twins(gone)).reshape(groups, share, width)
    backwards = [list(reversed(range(groups)))]
    pieces = lax.all_to_all(both, others, 0, 0, axis_index_groups=backwards, tiled=True)
    weighted = lax.all_to_all(scale(pieces, prec), others, 0, 0, tiled=True)
    other = swap_twins(weighted)
    tail, head, own = adjoint_own(which, weighted, turned)
    upper, head, got = adjoint_first(which, other, turned, head)
    bottom = send_up(head)
    lower, tail = adjoint_second(which, got, turned, tail, head)
    top = send_down(tail)
    edges, scaled, out, mix = inner(which, own, got, turned, upper, lower, diag, couple, *note)
    out = finish(1, bottom, mix, edges, scaled, out)
    out = finish(0, top, mix, edges, scaled, out)
    return out.reshape(sketch.shape)


def solution(mesh):
    bands, tiles = mesh.shape["band"], mesh.shape["tile"]
    fine = Mesh(mesh.devices.reshape(bands // 2, 2, tiles), ("pair", "twin", "tile"))
    band = ("pair", "twin")
    placed = (
        P(None, band, "tile", None, None),
        P(band, "tile", None),
        P(band, "tile", None),
        P(None, None, band, "tile", None),
        P(),
    )
    return jax.shard_map(
        body,
        mesh=fine,
        in_specs=placed,
        out_specs=P(None, band, "tile", None, None),
        check_vma=False,
    )
```

```python
import functools

import jax
import jax.numpy as jnp
from jax import lax
from jax.experimental import pallas as pl
from jax.experimental.pallas import tpu as pltpu
from jax.sharding import Mesh
from jax.sharding import PartitionSpec as P

MIB = 1 << 20
HALO = 2
VMEM = pl.BlockSpec(memory_space=pltpu.VMEM)
SMEM = pl.BlockSpec(memory_space=pltpu.SMEM)
HBM = pl.BlockSpec(memory_space=pltpu.HBM)


def call(kernel, name, out_shape, in_specs, out_specs, scratch, moved, grid=(), aliases={}, limit=16):
    return pl.pallas_call(
        kernel,
        grid=grid,
        out_shape=out_shape,
        in_specs=in_specs,
        out_specs=out_specs,
        scratch_shapes=scratch,
        input_output_aliases=aliases,
        compiler_params=pltpu.CompilerParams(vmem_limit_bytes=limit * MIB),
        cost_estimate=pl.CostEstimate(flops=0, bytes_accessed=moved * MIB, transcendentals=0),
        name=name,
    )


def f32(*shape):
    return jax.ShapeDtypeStruct(shape, jnp.float32)


def bf16(*shape):
    return jax.ShapeDtypeStruct(shape, jnp.bfloat16)


def edge_rows(rows):
    return [*range(HALO), *range(rows - HALO, rows)]


def beside(w):
    cols = w.shape[0]
    at = lax.broadcasted_iota(jnp.int32, w.shape, 0)
    before = jnp.where(at == 0, 0.0, pltpu.roll(w, 1, 0))
    after = jnp.where(at == cols - 1, 0.0, pltpu.roll(w, cols - 1, 0))
    return before + after


def spread(own, halos, line, wide):
    rows, cols = own[0].shape
    for which in range(2):
        line[...] = jnp.zeros(line.shape, line.dtype)
        for side, halo in enumerate(halos):
            at = side * (HALO + rows)
            line[at : at + HALO, :] = halo[which]
        line[HALO : HALO + rows, :] = own[which][...]
        turned = line[...].T
        for row in range(rows + 2 * HALO):
            wide[which, row] = jnp.broadcast_to(turned[:, row : row + 1], wide.shape[2:])


def mix_coefs(wide, mix):
    total = wide.shape[1]
    for side in range(2):
        far, near, edge, inner = (row if side == 0 else total - 1 - row for row in range(4))
        square = wide[1, edge] * wide[1, edge]
        mix[side, 0] = wide[1, near]
        mix[side, 1] = wide[1, far]
        mix[side, 2] = wide[1, near] * wide[0, near]
        mix[side, 3] = wide[1, near] * wide[1, near]
        mix[side, 4] = -square
        mix[side, 5] = -wide[0, edge] * wide[1, edge]
        mix[side, 6] = wide[1, edge]
        mix[side, 7] = wide[1, inner] * square


def coef_scratch(rows, cols, width):
    return [pltpu.VMEM((cols, cols), jnp.float32), pltpu.VMEM((2, rows, cols, width), jnp.float32)]


def one_sweep(values, scaled, wide, row):
    around = beside(scaled[row])
    if row > 0:
        around = around + scaled[row - 1]
    if row + 1 < len(scaled):
        around = around + scaled[row + 1]
    return wide[0, row + HALO] * values[row] - wide[1, row + HALO] * around


def own_sweeps(load, wide, rows, store):
    values, scaled, first, second = ([None] * rows for _ in range(4))
    for row in range(rows + 2):
        if row < rows:
            values[row] = load(row)
            scaled[row] = wide[1, row + HALO] * values[row]
        if 0 < row <= rows:
            first[row - 1] = one_sweep(values, scaled, wide, row - 1)
            second[row - 1] = wide[1, row - 1 + HALO] * first[row - 1]
        if row > 1:
            store(row - 2, one_sweep(first, second, wide, row - 2), scaled)


def halo_part(message, at, edge_scaled, mix, side):
    cols = edge_scaled.shape[0]
    far_row, near_row = (0, 1) if side == 0 else (1, 0)

    def take(row):
        start = pl.multiple_of(at + row * cols, cols)
        return message[pl.ds(start, cols), :].astype(jnp.float32)

    near = take(near_row)
    scaled = mix[side, 0] * near
    around = mix[side, 1] * take(far_row) + edge_scaled + beside(scaled)
    near_second = mix[side, 2] * near - mix[side, 3] * around
    second = mix[side, 4] * scaled
    on_edge = mix[side, 5] * scaled - mix[side, 6] * (near_second + beside(second))
    return on_edge, mix[side, 7] * scaled


def spots_of(side):
    return (0, 1) if side == 0 else (2 * HALO - 1, 2 * HALO - 2)


def pack_kernel(first, field, _, out, edges, packed, arrived, left):
    steps, rows, cols, width = field.shape
    strip = HALO * cols
    coming, going = [], []
    for step in range(steps):
        source = field.at[step, pl.ds(first, HALO)]
        coming.append(pltpu.make_async_copy(source, edges.at[step], arrived.at[step]))
        coming[step].start()
        going.append(pltpu.make_async_copy(packed.at[step], out.at[pl.ds(step * strip, strip)], left.at[step]))
    for step in range(steps):
        coming[step].wait()
        packed[step] = edges[step].reshape(strip, width).astype(packed.dtype)
        going[step].start()
    for copy in going:
        copy.wait()


def pack(first, field, after):
    steps, rows, cols, width = field.shape
    strip = HALO * cols
    return call(
        functools.partial(pack_kernel, first),
        "pack",
        bf16(steps * strip, width),
        [HBM] * 2,
        HBM,
        [
            pltpu.VMEM((steps, HALO, cols, width), jnp.float32),
            pltpu.VMEM((steps, strip, width), jnp.bfloat16),
            pltpu.SemaphoreType.DMA((steps,)),
            pltpu.SemaphoreType.DMA((steps,)),
        ],
        3,
        limit=62,
    )(field, after)


def before_kernel(field, diag, couple, kern, _, edges, scaled, data, turned, outward, line, wide, pairs):
    steps, rows, cols, width = field.shape
    inner = rows - 2 * HALO
    listed = edge_rows(rows)
    spread((diag, couple), (), line, wide)
    pairs[0, :, 0:width] = jnp.zeros((inner * cols, width), pairs.dtype)

    @pl.loop(0, steps)
    def _(step):
        def store(row, value, weighted):
            if row in listed:
                edges[step, listed.index(row)] = value
            else:
                at = (row - HALO) * cols
                rounded = value.astype(pairs.dtype)
                pairs[step, at : at + cols, width : 2 * width] = rounded
                pairs[step + 1, at : at + cols, 0:width] = rounded
            if row == 0:
                scaled[step, 0] = weighted[0]
            if row == rows - 1:
                scaled[step, 1] = weighted[rows - 1]

        own_sweeps(lambda row: field[step, row], wide, rows, store)

    @pl.loop(0, steps)
    def _(lag):
        for row in range(rows):
            turned[lag, row] = kern[lag, row].T
        for spot, row in enumerate(listed):
            outward[lag, :, spot * cols : (spot + 1) * cols] = kern[lag, row]

    for step in range(0, steps, 2):
        acc = None
        for lag in range(step + 2):
            left = jnp.concatenate([kern[lag, row] for row in range(HALO, rows - HALO)], axis=1)
            term = jnp.dot(left, pairs[step + 1 - lag], preferred_element_type=jnp.float32)
            acc = term if acc is None else acc + term
        data[step] = acc[:, 0:width]
        data[step + 1] = acc[:, width : 2 * width]


def before(field, diag, couple, kern, after):
    steps, rows, cols, width = field.shape
    sensors = kern.shape[2]
    inner = (rows - 2 * HALO) * cols
    return call(
        before_kernel,
        "before",
        (
            f32(steps, 2 * HALO, cols, width),
            f32(steps, 2, cols, width),
            f32(steps, sensors, width),
            bf16(steps, rows, cols, sensors),
            bf16(steps, sensors, 2 * HALO * cols),
        ),
        [VMEM] * 4 + [HBM],
        [VMEM] * 5,
        coef_scratch(rows + 2 * HALO, cols, width) + [pltpu.VMEM((steps + 1, inner, 2 * width), jnp.bfloat16)],
        12,
    )(field, diag, couple, kern, after)


def edge_product(half, pairs, outward, start, out):
    steps, sensors, _ = outward.shape
    width = out.shape[2]
    kept = sensors // 2
    span = pl.ds(pl.multiple_of(half * kept, kept), kept)
    for step in range(0, steps, 2):
        acc = jnp.concatenate([start[step, span, :], start[step + 1, span, :]], axis=1)
        for lag in range(step + 2):
            left = outward[lag, span, :]
            acc = acc + jnp.dot(left, pairs[step + 1 - lag], preferred_element_type=jnp.float32)
        out[step] = acc[:, 0:width].astype(out.dtype)
        out[step + 1] = acc[:, width : 2 * width].astype(out.dtype)


def leaving_kernel(
    twin, top, bottom, diag, couple, ctop, cbottom, edges, scaled, outward, start, out, pairs, line, wide, mix
):
    steps = outward.shape[0]
    cols, width = edges.shape[2], edges.shape[3]
    spread((diag, couple), (ctop, cbottom), line, wide)
    mix_coefs(wide, mix)
    pairs[0, :, 0:width] = jnp.zeros((2 * HALO * cols, width), pairs.dtype)

    @pl.loop(0, steps)
    def _(step):
        for side, message in enumerate((top, bottom)):
            added = halo_part(message, step * (HALO * cols), scaled[step, side], mix, side)
            for spot, extra in zip(spots_of(side), added):
                rounded = (edges[step, spot] + extra).astype(pairs.dtype)
                at = spot * cols
                pairs[step, at : at + cols, width : 2 * width] = rounded
                pairs[step + 1, at : at + cols, 0:width] = rounded

    edge_product(1 - twin[0], pairs, outward, start, out)


def leaving(twin, top, bottom, diag, couple, ctop, cbottom, edges, scaled, outward, start):
    steps, sensors, _ = outward.shape
    rows, cols = diag.shape
    width = edges.shape[3]
    return call(
        leaving_kernel,
        "leaving",
        [bf16(steps, sensors // 2, width), bf16(steps + 1, 2 * HALO * cols, 2 * width)],
        [SMEM] + [VMEM] * 10,
        [VMEM] * 2,
        coef_scratch(rows + 2 * HALO, cols, width) + [pltpu.VMEM((2, 8, cols, width), jnp.float32)],
        1,
    )(twin, top, bottom, diag, couple, ctop, cbottom, edges, scaled, outward, start)


def staying_kernel(twin, pairs, outward, start, out):
    edge_product(twin[0], pairs, outward, start, out)


def staying(twin, pairs, outward, start):
    steps, sensors, width = start.shape
    out = f32(steps, sensors // 2, width)
    return call(staying_kernel, "staying", out, [SMEM] + [VMEM] * 3, VMEM, [], 1)(twin, pairs, outward, start)


def join_kernel(mine, got, both):
    both[...] = (mine[...] + got[...].astype(jnp.float32)).astype(both.dtype)


def join(mine, got):
    return call(join_kernel, "join", bf16(*got.shape), [VMEM] * 2, VMEM, [], 1)(mine, got)


def scale_kernel(pieces, prec, out):
    total = pieces[0].astype(jnp.float32)
    for piece in range(1, pieces.shape[0]):
        total = total + pieces[piece].astype(jnp.float32)
    weighted = (total * prec[...]).astype(out.dtype)
    for piece in range(pieces.shape[0]):
        out[piece] = weighted


def scale(pieces, prec):
    return call(scale_kernel, "scale", bf16(*pieces.shape), [VMEM] * 2, VMEM, [], 1)(pieces, prec)


def fill_half(source, pairs):
    groups, share, width = source.shape
    kept = pairs.shape[1]
    steps = groups * share // kept
    pairs[steps, :, width : 2 * width] = jnp.zeros((kept, width), pairs.dtype)
    for piece in range(groups):
        step, first = divmod(piece * share, kept)
        value = source[piece]
        pairs[step + 1, first : first + share, 0:width] = value
        pairs[step, first : first + share, width : 2 * width] = value


def half_product(rows, turned, half, pairs, step, acc):
    steps, _, cols, sensors = turned.shape
    kept = sensors // 2
    span = pl.ds(pl.multiple_of(half * kept, kept), kept)
    for lag in range(steps - step):
        left = turned[lag, rows, :, span].reshape((rows.stop - rows.start) * cols, kept)
        term = jnp.dot(left, pairs[step + lag + 1], preferred_element_type=jnp.float32)
        acc = term if acc is None else acc + term
    return acc


def strip_product(rows, turned, half, pairs, begun, field, message):
    steps, _, cols, _ = turned.shape
    strip = HALO * cols
    width = message.shape[1]
    for step in range(0, steps, 2):
        acc = half_product(rows, turned, half, pairs, step, begun[step // 2])
        for side in range(2):
            part = acc[:, side * width : (side + 1) * width]
            field[step + side] = part.reshape(HALO, cols, width)
            at = (step + side) * strip
            message[at : at + strip, :] = part.astype(message.dtype)


def own_kernel(twin, mine, turned, tail, head, pairs):
    steps, rows = turned.shape[0], turned.shape[1]
    fill_half(mine, pairs)
    for strip, out in ((slice(rows - HALO, rows), tail), (slice(0, HALO), head)):
        for step in range(0, steps, 2):
            out[step // 2] = half_product(strip, turned, twin[0], pairs, step, None)


def adjoint_own(twin, mine, turned):
    steps, _, cols, sensors = turned.shape
    width = mine.shape[2]
    strip = f32(steps // 2, HALO * cols, 2 * width)
    return call(
        own_kernel,
        "adjoint_own",
        (strip, strip, bf16(steps + 1, sensors // 2, 2 * width)),
        [SMEM] + [VMEM] * 2,
        [VMEM] * 3,
        [],
        4,
    )(twin, mine, turned)


def first_kernel(twin, other, turned, begun, field, message, pairs):
    fill_half(other, pairs)
    strip_product(slice(0, HALO), turned, 1 - twin[0], pairs, begun, field, message)


def second_kernel(twin, pairs, turned, begun, _, field, message):
    rows = turned.shape[1]
    strip_product(slice(rows - HALO, rows), turned, 1 - twin[0], pairs, begun, field, message)


def adjoint_first(twin, other, turned, begun):
    steps, _, cols, sensors = turned.shape
    width = other.shape[2]
    return call(
        first_kernel,
        "adjoint_first",
        (
            f32(steps, HALO, cols, width),
            bf16(steps * HALO * cols, width),
            bf16(steps + 1, sensors // 2, 2 * width),
        ),
        [SMEM] + [VMEM] * 3,
        [VMEM] * 3,
        [],
        4,
    )(twin, other, turned, begun)


def adjoint_second(twin, pairs, turned, begun, after):
    steps, _, cols, _ = turned.shape
    width = pairs.shape[2] // 2
    return call(
        second_kernel,
        "adjoint_second",
        (f32(steps, HALO, cols, width), bf16(steps * HALO * cols, width)),
        [SMEM, VMEM, VMEM, VMEM, HBM],
        [VMEM] * 2,
        [],
        4,
    )(twin, pairs, turned, begun, after)


def inner_kernel(
    twin, own, got, turned, upper, lower, diag, couple, ctop, cbottom, edges, scaled, out, mix, core, line, wide
):
    steps, rows, cols, sensors = turned.shape
    width = core.shape[3]
    inner = rows - 2 * HALO
    pack_at = pl.program_id(0)

    @pl.when(pack_at == 0)
    def _():
        spread((diag, couple), (ctop, cbottom), line, wide)
        mix_coefs(wide, mix)
        for step in range(0, steps, 2):
            acc = None
            for pairs, half in ((own, twin[0]), (got, 1 - twin[0])):
                acc = half_product(slice(HALO, rows - HALO), turned, half, pairs, step, acc)
            for side in range(2):
                core[step + side] = acc[:, side * width : (side + 1) * width].reshape(inner, cols, width)

    listed = edge_rows(rows)
    span = out.shape[0]

    @pl.loop(0, span)
    def _(at):
        step = pack_at * span + at

        def load(row):
            if row < HALO:
                return upper[step, row]
            return core[step, row - HALO] if row < rows - HALO else lower[step, row - rows + HALO]

        def store(row, value, weighted):
            if row in listed:
                edges[step, listed.index(row)] = value
            else:
                out[at, row - HALO] = value
            if row == 0:
                scaled[step, 0] = weighted[0]
            if row == rows - 1:
                scaled[step, 1] = weighted[rows - 1]

        own_sweeps(load, wide, rows, store)


def inner(twin, own, got, turned, upper, lower, diag, couple, ctop, cbottom):
    steps, rows, cols, _ = turned.shape
    width = upper.shape[3]
    core = rows - 2 * HALO
    assert core == HALO
    span = steps // 2
    return call(
        inner_kernel,
        "inner",
        (
            f32(steps, 2 * HALO, cols, width),
            f32(steps, 2, cols, width),
            f32(steps, rows, cols, width),
            f32(2, 8, cols, width),
        ),
        [SMEM] + [VMEM] * 9,
        [VMEM, VMEM, pl.BlockSpec((span, core, cols, width), lambda step: (step, 1, 0, 0)), VMEM],
        [pltpu.VMEM((steps, core, cols, width), jnp.float32)] + coef_scratch(rows + 2 * HALO, cols, width),
        10,
        (steps // span,),
    )(twin, own, got, turned, upper, lower, diag, couple, ctop, cbottom)


def finish_kernel(side, message, mix, edges, scaled, _, out):
    span, _, cols, _ = out.shape
    first = pl.program_id(0) * span

    @pl.loop(0, span)
    def _(at):
        step = first + at
        added = halo_part(message, step * (HALO * cols), scaled[step, side], mix, side)
        for spot, extra in zip(spots_of(side), added):
            out[at, spot % HALO] = edges[step, spot] + extra


def finish(side, message, mix, edges, scaled, out):
    steps, rows, cols, width = out.shape
    span = steps // 2
    place = side * (rows // HALO - 1)
    return call(
        functools.partial(finish_kernel, side),
        "finish",
        f32(*out.shape),
        [VMEM] * 4 + [HBM],
        pl.BlockSpec((span, HALO, cols, width), lambda step: (step, place, 0, 0)),
        [],
        2,
        (steps // span,),
        {4: 0},
    )(message, mix, edges, scaled, out)


def send_down(tail):
    return lax.ppermute(tail, "tile", [(i, i + 1) for i in range(lax.axis_size("tile") - 1)])


def send_up(head):
    return lax.ppermute(head, "tile", [(i + 1, i) for i in range(lax.axis_size("tile") - 1)])


def swap_twins(value):
    return lax.ppermute(value, "twin", [(0, 1), (1, 0)])


def body(sketch, diag_coef, couple, kernel, noise_prec):
    steps, _, rows, cols, width = sketch.shape
    sensors = kernel.shape[1]
    others = ("pair", "tile")
    groups = lax.axis_size(others)
    twin = lax.axis_index("twin")
    which = twin.reshape(1)
    field = sketch.reshape(steps, rows, cols, width)
    diag, couple = diag_coef.reshape(rows, cols), couple.reshape(rows, cols)
    kern = jnp.transpose(kernel.reshape(steps, sensors, rows, cols), (0, 2, 1, 3))
    kept = sensors // 2
    share = steps * kept // groups

    tail = pack(rows - HALO, field, sketch)
    top = send_down(tail)
    bottom = send_up(pack(0, field, tail))
    coefs = jnp.stack([diag, couple])
    note = send_down(coefs[:, rows - HALO :]), send_up(coefs[:, :HALO])
    noise = lax.dynamic_slice(noise_prec, (0, twin * kept), (steps, kept)).reshape(steps * kept)
    noise = lax.dynamic_slice(noise, ((groups - 1 - lax.axis_index(others)) * share,), (share,))
    prec = jnp.broadcast_to(noise[:, None], (share, width))
    edges, scaled, data, turned, outward = before(field, diag, couple, kern, prec)

    gone, pairs = leaving(which, top, bottom, diag, couple, *note, edges, scaled, outward, data)
    both = join(staying(which, pairs, outward, data), swap_twins(gone)).reshape(groups, share, width)
    backwards = [list(reversed(range(groups)))]
    pieces = lax.all_to_all(both, others, 0, 0, axis_index_groups=backwards, tiled=True)
    weighted = lax.all_to_all(scale(pieces, prec), others, 0, 0, axis_index_groups=backwards, tiled=True)
    other = swap_twins(weighted)
    tail, head, own = adjoint_own(which, weighted, turned)
    upper, head, got = adjoint_first(which, other, turned, head)
    bottom = send_up(head)
    lower, tail = adjoint_second(which, got, turned, tail, head)
    top = send_down(tail)
    edges, scaled, out, mix = inner(which, own, got, turned, upper, lower, diag, couple, *note)
    out = finish(1, bottom, mix, edges, scaled, out)
    out = finish(0, top, mix, edges, scaled, out)
    return out.reshape(sketch.shape)


def solution(mesh):
    bands, tiles = mesh.shape["band"], mesh.shape["tile"]
    fine = Mesh(mesh.devices.reshape(bands // 2, 2, tiles), ("pair", "twin", "tile"))
    band = ("pair", "twin")
    placed = (
        P(None, band, "tile", None, None),
        P(band, "tile", None),
        P(band, "tile", None),
        P(None, None, band, "tile", None),
        P(),
    )
    return jax.shard_map(
        body,
        mesh=fine,
        in_specs=placed,
        out_specs=P(None, band, "tile", None, None),
        check_vma=False,
    )
```
